256 devices in a mesh: lon: 64 (over x_hi, y, z), dp: 4 (over x_lo, core).
Axes of the slice: x: 4 (x_hi: 2, x_lo: 2; x = x_hi * 2 + x_lo), y: 4, z: 8, core: 2. Of those that a mesh axis runs over, the one named last changes fastest.
Arguments:
- fields: bfloat16 [4, 77, 512, 128], P('dp', None, 'lon'), may hold values from -6 to 6
- targets: bfloat16 [4, 77, 512, 128], P('dp', None, 'lon'), as said below
- land_sea: int32 [512, 128], P('lon'), may hold values 0 or 1
- clip_level: int32 [77], replicated, may hold values from 2 to 63
- stem_weight: bfloat16 [200, 77], P('dp'), may hold values from -0.625 to 0.625
- dw_kernel: bfloat16 [200, 49], P('dp'), may hold values from -0.875 to 0.875
- up_weight: bfloat16 [200, 800], P('dp'), may hold values from -0.4375 to 0.4375
- down_weight: bfloat16 [800, 200], P('dp'), may hold values from -0.21875 to 0.21875
- head_weight: bfloat16 [200, 77], P('dp'), may hold values from -0.4375 to 0.4375
Outputs:
- stem_weight_gradient: float32 [200, 77], P('dp')
- grad_kernel: float32 [200, 49], P('dp')
- grad_up: float32 [200, 800], P('dp')
- grad_down: float32 [800, 200], P('dp')
- grad_head: float32 [200, 77], P('dp')
- loss: float32 [], replicated
- field_sensitivity: float32 [4, 77, 512, 128], P('dp', None, 'lon')
The draws below stay inside these ranges and needn't reach their ends.
Inputs may be any that keep to these rules, and one draw needn't show every extreme that they name: targets are real-valued ocean fields between -8 and 8.
All inputs are finite; a program needn't handle non-finite values. No bound on the sum of `land_sea` on one device may be relied on, other than what follows from the above.
Results may differ from the reference program's by a relative error of at most 0.011.
Values may be sent and summed in bfloat16 or wider, within the bound.
A program may use at most 64 MiB of HBM per device.

```python
import jax
import jax.numpy as jnp
from jax import lax

V = 77
C = 200
FF = 800
KERNEL_SIDE = 7
KERNEL_SPACING = 2
HALO = 6
LAT = 128
LON = 512
SAMPLES = 4


def draw_targets(key, part):
    key = jax.random.fold_in(key, 11)
    base_key, scale_key = jax.random.split(key, 2)
    position = jnp.arange(LON, dtype=jnp.float32) / LON
    scales = jnp.exp(jax.random.uniform(scale_key, (V,), jnp.float32, jnp.log(0.3), jnp.log(3.0)))
    base = jax.random.normal(base_key, (SAMPLES, V, LON, LAT), jnp.float32)
    ramp = jnp.exp(0.5 * jnp.log(3.0) * position)
    values = base * scales[None, :, None, None] * ramp[None, None, :, None]
    return jnp.clip(values, -8.0, 8.0).astype(jnp.bfloat16)


def set_ends(entries, stream_key, smallest, largest):
    place = [jax.random.randint(jax.random.fold_in(stream_key, axis), (), 0, length) for axis, length in enumerate(entries.shape)]
    longest = entries.shape.index(max(entries.shape))
    beside = place[:longest] + [(place[longest] + 1) % entries.shape[longest]] + place[longest + 1:]
    return entries.at[tuple(place)].set(smallest).at[tuple(beside)].set(largest)


def steps_of(own_key, shape, cuts, least, largest):
    gain = 1.0
    for axis_at, shards_of in cuts:
        draws = jax.random.uniform(jax.random.fold_in(jax.random.fold_in(own_key, 6), axis_at), (shards_of,), jnp.float32, least / len(cuts), largest / len(cuts))
        gain = gain * jnp.repeat(jnp.exp(draws), shape[axis_at] // shards_of).reshape((-1,) + (1,) * (len(shape) - 1 - axis_at))
    return gain


def normal_values(own_key, shape, scale, bound, pieces=(), kind=jnp.bfloat16):
    entries = jax.random.normal(own_key, shape, jnp.float32) * scale
    if len(pieces) > 0:
        entries = steps_of(own_key, shape, pieces, -0.22, 0.18) * entries
    return jnp.clip(entries, min=-bound, max=bound).astype(kind)


def setup_inputs(seed: int = 0) -> dict:
    streams_of = jax.random.split(jax.random.key(seed), 10)
    fields = normal_values(streams_of[0], (SAMPLES, V, LON, LAT), 1.0, 6.0, ((0, 4), (2, 64)))
    targets = draw_targets(jax.random.fold_in(streams_of[9], 71), 0)
    land_sea = set_ends((jax.random.randint(streams_of[2], (LON, LAT), 0, 3) < 2).astype(jnp.int32), jax.random.fold_in(streams_of[2], 1), 0, 1)
    clip_level = set_ends(jax.random.randint(streams_of[3], (V,), 2, 64), jax.random.fold_in(streams_of[3], 1), 2, 63).astype(jnp.int32)
    stem_weight = normal_values(streams_of[4], (C, V), V ** -0.5, 0.625, ((0, 4),))
    dw_kernel = normal_values(streams_of[5], (C, KERNEL_SIDE * KERNEL_SIDE), (KERNEL_SIDE * KERNEL_SIDE) ** -0.5, 0.875, ((0, 4),))
    up_weight = normal_values(streams_of[6], (C, FF), C ** -0.5, 0.4375, ((0, 4),))
    down_weight = normal_values(streams_of[7], (FF, C), FF ** -0.5, 0.21875, ((0, 4),))
    head_weight = normal_values(streams_of[8], (C, V), C ** -0.5, 0.4375, ((0, 4),))
    return dict(fields=fields, targets=targets, land_sea=land_sea, clip_level=clip_level, stem_weight=stem_weight, dw_kernel=dw_kernel, up_weight=up_weight, down_weight=down_weight, head_weight=head_weight)


gelu_scale = 0.7978845608

def gelu_pair(values):
    inner = gelu_scale * (values + 0.044715 * values ** 3)
    tanh_val = jnp.tanh(inner)
    act = 0.5 * values * (1.0 + tanh_val)
    slope = 0.5 * (1.0 + tanh_val) + 0.5 * values * (1.0 - tanh_val ** 2) * gelu_scale * (1.0 + 3.0 * 0.044715 * values ** 2)
    return (act, slope)

def tap_list():
    return [((first_operand - KERNEL_SIDE // 2) * KERNEL_SPACING, (second_operand - KERNEL_SIDE // 2) * KERNEL_SPACING) for first_operand in range(KERNEL_SIDE) for second_operand in range(KERNEL_SIDE)]

def shifted(field, lon_off, lat_off):
    rolled = jnp.roll(field, -lon_off, axis=1)
    padded = jnp.pad(rolled, ((0, 0), (0, 0), (HALO, HALO)))
    return padded[:, :, HALO + lat_off:HALO + lat_off + LAT]

def f32(value):
    return value.astype(jnp.float32)

def forward(sample, target, ocean, stem_weight, dw_kernel, up_weight, down_weight, head_weight):
    stem_out = jnp.einsum('cv,vla->cla', f32(stem_weight), f32(sample)).astype(jnp.bfloat16)
    kern32 = f32(dw_kernel)
    mixed = jnp.zeros(stem_out.shape, jnp.float32)
    for index, (lon_off, lat_off) in enumerate(tap_list()):
        mixed = mixed + kern32[:, index, None, None] * f32(shifted(stem_out, lon_off, lat_off))
    centre = lax.optimization_barrier(jnp.mean(mixed, axis=0, keepdims=True))
    centred = mixed - centre
    spread = lax.optimization_barrier(jnp.mean(centred * centred, axis=0, keepdims=True))
    rstd = lax.rsqrt(spread + 1e-06)
    normed = centred * rstd
    normed_half = normed.astype(jnp.bfloat16)
    hidden_pre = jnp.einsum('cf,cla->fla', f32(up_weight), f32(normed_half))
    act, slope = gelu_pair(hidden_pre)
    act_half = act.astype(jnp.bfloat16)
    branch = jnp.einsum('fc,fla->cla', f32(down_weight), f32(act_half))
    block_out = (f32(stem_out) + branch).astype(jnp.bfloat16)
    predicted = jnp.einsum('cv,cla->vla', f32(head_weight), f32(block_out))
    misfit = (predicted - f32(target)) * ocean[None]
    return (stem_out, normed, normed_half, rstd, slope, act_half, block_out, misfit)

def reference(fields, targets, land_sea, clip_level, stem_weight, dw_kernel, up_weight, down_weight, head_weight):
    ocean = land_sea.astype(jnp.float32)
    weights = (stem_weight, dw_kernel, up_weight, down_weight, head_weight)

    def sample_squares(pair):
        misfit = forward(pair[0], pair[1], ocean, *weights)[-1]
        return lax.optimization_barrier(jnp.sum(misfit * misfit, axis=(1, 2)))
    squares = lax.optimization_barrier(jnp.sum(lax.map(sample_squares, (fields, targets)), axis=0))
    ocean_count = SAMPLES * jnp.sum(ocean)
    threshold = clip_level.astype(jnp.float32) / 16.0
    mean_error = squares / ocean_count
    loss = jnp.sum(threshold * jnp.log(1.0 + mean_error / threshold))
    factor = 2.0 / (ocean_count * (1.0 + mean_error / threshold))
    kern32 = f32(dw_kernel)

    def sample_grads(carry, pair):
        sample, target = pair
        stem_out, normed, normed_half, rstd, slope, act_half, block_out, misfit = forward(sample, target, ocean, *weights)
        pred_grad = (misfit * factor[:, None, None]).astype(jnp.bfloat16)
        g_head = jnp.einsum('cla,vla->cv', f32(block_out), f32(pred_grad))
        block_grad = jnp.einsum('cv,vla->cla', f32(head_weight), f32(pred_grad))
        block_half = block_grad.astype(jnp.bfloat16)
        g_down = jnp.einsum('fla,cla->fc', f32(act_half), f32(block_half))
        hidden_gradient = jnp.einsum('fc,cla->fla', f32(down_weight), f32(block_half))
        pre_half = (hidden_gradient * slope).astype(jnp.bfloat16)
        g_up = jnp.einsum('cla,fla->cf', f32(normed_half), f32(pre_half))
        normed_grad = jnp.einsum('cf,fla->cla', f32(up_weight), f32(pre_half))
        mixed_half = (rstd * (normed_grad - lax.optimization_barrier(jnp.mean(normed_grad, axis=0, keepdims=True)) - normed * lax.optimization_barrier(jnp.mean(normed_grad * normed, axis=0, keepdims=True)))).astype(jnp.bfloat16)
        kern_terms = []
        back = jnp.zeros(block_grad.shape, jnp.float32)
        for index, (lon_off, lat_off) in enumerate(tap_list()):
            kern_terms.append(lax.optimization_barrier(jnp.sum(f32(mixed_half) * f32(shifted(stem_out, lon_off, lat_off)), axis=(1, 2))))
            back = back + kern32[:, index, None, None] * f32(shifted(mixed_half, -lon_off, -lat_off))
        g_kern = jnp.stack(kern_terms, axis=1)
        stem_half = (block_grad + back).astype(jnp.bfloat16)
        g_stem = jnp.einsum('cla,vla->cv', f32(stem_half), f32(sample))
        sensitivity = jnp.einsum('cv,cla->vla', f32(stem_weight), f32(stem_half)) * ocean_count
        new = (carry[0] + g_stem, carry[1] + g_kern, carry[2] + g_up, carry[3] + g_down, carry[4] + g_head)
        return (new, sensitivity)
    init = (jnp.zeros((C, V), jnp.float32), jnp.zeros((C, KERNEL_SIDE * KERNEL_SIDE), jnp.float32), jnp.zeros((C, FF), jnp.float32), jnp.zeros((FF, C), jnp.float32), jnp.zeros((C, V), jnp.float32))
    grads, field_sensitivity = lax.scan(sample_grads, init, (fields, targets))
    return (grads[0], grads[1], grads[2], grads[3], grads[4], loss, field_sensitivity)
```

```python
import jax
import jax.numpy as jnp
from jax import lax
from jax.experimental import pallas as pl
from jax.experimental.pallas import tpu as pltpu
from jax.sharding import PartitionSpec as P

MESH = pl.DeviceIdType.MESH
F32 = jnp.float32
BF16 = jnp.bfloat16

V = 77
VP = 80
C = 200
CP = 256
FF = 800
FP = 896
FB = 160
COLS = 8
LAT = 128
SIDE = 7
HALO = 6
SLOTS = COLS + 2 * HALO
CELLS = COLS * LAT
GELU_K = 0.7978845608


def dot(a, b):
    return jnp.dot(a, b, preferred_element_type=F32)


def dot_nt(a, b):
    return lax.dot_general(a, b, (((1,), (1,)), ((), ())), preferred_element_type=F32)


def remote(src, dst, send, recv, device):
    return pltpu.make_async_remote_copy(
        src_ref=src,
        dst_ref=dst,
        send_sem=send,
        recv_sem=recv,
        device_id=device,
        device_id_type=MESH,
    )


def padded_row(channel):
    step = (channel >= 50).astype(jnp.int32)
    step += (channel >= 100).astype(jnp.int32)
    step += (channel >= 150).astype(jnp.int32)
    return channel + 14 * step


def body(
    fields, targets, land, clip, stem, dw, up, down, head,
    o_stem, o_kern, o_up, o_down, o_head, o_loss, o_sens,
    f32a, f32b, fbuf, fm, wp, wd, ga, gb, gd,
    stem_w, stem_t, kern_w, up_w, up_t, head_w, head_t, down_w, down_t, down_f,
    xs, ms, nh, nhp, act, slope, pre, bo, mis, sq, sa, sb,
    bg, bh, gdn, gup, back, sh, small, smp,
    ld, lu, rd0, ru0, ls1, rx1, s2, rx2, fin, lg,
    stx, srx, s2x, sfin, sen, hl, hr,
    send_g, recv_g, send_h, recv_h, send_s, recv_s,
):
    lon = lax.axis_index("lon")
    dp = lax.axis_index("dp")
    x_hi, y, z = lon // 32, (lon // 8) % 4, lon % 8
    x_lo, core = dp // 2, dp % 2
    right = ((lon + 1) % 64, dp)
    left = ((lon + 63) % 64, dp)
    sibling = (lon, x_lo * 2 + (1 - core))
    idx_a = y * 4 + dp
    idx_b = x_hi * 8 + z
    idx_c = x_lo * 4 + y

    def peer_a(k):
        j = (idx_a + k) % 16
        return j, (x_hi * 32 + (j // 4) * 8 + z, j % 4)

    def peer_b(k):
        j = (idx_b + k) % 16
        return j, ((j // 8) * 32 + y * 8 + j % 8, dp)

    def peer_c(k):
        j = (idx_c + k) % 8
        return j, (x_hi * 32 + (j % 4) * 8 + z, (j // 4) * 2 + core)

    def peer_y(k):
        j = (y + k) % 4
        return j, (x_hi * 32 + j * 8 + z, dp)

    barrier = pltpu.get_barrier_semaphore()
    for target in (right, left):
        pl.semaphore_signal(barrier, inc=1, device_id=target, device_id_type=MESH)
    for k in range(1, 16):
        pl.semaphore_signal(barrier, inc=1, device_id=peer_a(k)[1], device_id_type=MESH)
        pl.semaphore_signal(barrier, inc=1, device_id=peer_b(k)[1], device_id_type=MESH)

    f32a[0 : V * COLS, :] = fields[...].astype(F32).reshape(V * COLS, LAT)
    f32a[V * COLS : VP * COLS, :] = jnp.zeros(((VP - V) * COLS, LAT), F32)
    f32b[0 : V * COLS, :] = targets[...].astype(F32).reshape(V * COLS, LAT)
    f32b[V * COLS : VP * COLS, :] = jnp.zeros(((VP - V) * COLS, LAT), F32)
    for i in range(COLS):
        fbuf[HALO + i] = f32a[pl.ds(i, VP, stride=COLS), :].astype(BF16)
    wp[...] = jnp.zeros(wp.shape, F32)
    wp[0:50, 0:V] = stem[...].astype(F32)
    wp[0:50, 128:177] = dw[...].astype(F32)
    wp[0:50, 256 : 256 + FF] = up[...].astype(F32)
    wp[0:50, 256 + FP : 256 + FP + V] = head[...].astype(F32)
    wd[...] = jnp.zeros(wd.shape, F32)
    wd[0:C, 0:C] = down[...].astype(F32)
    ga[dp] = wp[:, 0:256].astype(BF16)
    gb[dp] = wp[:, 256 : 256 + FP + 128].astype(BF16)
    gd[dp] = wd[...].astype(BF16)

    pl.semaphore_wait(barrier, 32)

    halo = [
        remote(fbuf.at[pl.ds(8, 6)], fbuf.at[pl.ds(0, 6)], send_h.at[0], recv_h.at[0], right),
        remote(fbuf.at[pl.ds(6, 6)], fbuf.at[pl.ds(14, 6)], send_h.at[1], recv_h.at[1], left),
    ]
    gathers = []
    for a, buf in enumerate((ga, gb, gd)):
        group = []
        for k in range(1, 4):
            group.append(
                remote(
                    buf.at[dp], buf.at[dp], send_g.at[a * 3 + k - 1], recv_g.at[a * 3 + k - 1],
                    (lon, (dp + k) % 4),
                )
            )
        gathers.append(group)
    for copy in gathers[0]:
        copy.start()
    for copy in halo:
        copy.start()
    for copy in gathers[1] + gathers[2]:
        copy.start()

    def stage(index, count, peers, src, dst):
        for k in range(1, count):
            j, device = peers(k)
            remote(src(j), dst, send_s.at[index], recv_s.at[index], device).start()

    def stage_wait(index, count, buf):
        whole = buf.at[pl.ds(0, count - 1)]
        both = remote(whole, whole, send_s.at[index], recv_s.at[index], right)
        both.wait_recv()
        both.wait_send()

    row = lax.broadcasted_iota(jnp.int32, (CP, CP), 0)
    col = lax.broadcasted_iota(jnp.int32, (CP, CP), 1)
    from_padded = jnp.where((row < C) & (col == padded_row(row)), 1.0, 0.0).astype(BF16)
    to_padded = jnp.where((col < C) & (row == padded_row(col)), 1.0, 0.0).astype(BF16)
    lane = lax.broadcasted_iota(jnp.int32, (8, LAT), 1)
    keep = {b: (lane + b >= 0) & (lane + b < LAT) for b in range(-HALO, HALO + 1, 2)}

    for i in range(COLS):
        fm[:, (HALO + i) * LAT : (HALO + i + 1) * LAT] = fbuf[HALO + i]

    for copy in gathers[0]:
        copy.wait_recv()
    first = dot(from_padded, ga[...].reshape(CP, 256))
    stem_w[...] = first[:, 0:128].astype(BF16)
    stem_t[...] = first[:, 0:128].T.astype(BF16)
    kern_w[...] = first[0:C, 128:256]

    def stem_pair(s):
        out = dot(stem_w[:, 0:VP], fm[:, s * LAT : (s + 2) * LAT])[0:C].astype(BF16).astype(F32)
        xs[s] = out[:, 0:LAT]
        xs[s + 1] = out[:, LAT : 2 * LAT]

    for s in range(HALO, HALO + COLS, 2):
        stem_pair(s)
    for copy in halo:
        copy.wait_recv()
    for s in list(range(0, HALO)) + list(range(HALO + COLS, SLOTS)):
        fm[:, s * LAT : (s + 1) * LAT] = fbuf[s]
    for s in list(range(0, HALO, 2)) + list(range(HALO + COLS, SLOTS, 2)):
        stem_pair(s)

    def conv_forward(block, carry):
        here = pl.ds(pl.multiple_of(block * 8, 8), 8)
        x = [xs[s, here, :] for s in range(SLOTS)]
        weights = kern_w[here, :]
        out = [None] * COLS
        for q in range(SIDE):
            b = (q - 3) * 2
            w = [
                jnp.broadcast_to(weights[:, p * SIDE + q : p * SIDE + q + 1], (8, LAT))
                for p in range(SIDE)
            ]
            for i in range(COLS):
                total = w[0] * x[i]
                for p in range(1, SIDE):
                    total = total + w[p] * x[i + 2 * p]
                if b != 0:
                    total = jnp.where(keep[b], pltpu.roll(total, (-b) % LAT, 1), 0.0)
                out[i] = total if out[i] is None else out[i] + total
        for i in range(COLS):
            ms[i, here, :] = out[i]
        return carry

    lax.fori_loop(0, C // 8, conv_forward, 0)

    nh[...] = jnp.zeros(nh.shape, BF16)
    rstds = []
    for i in range(COLS):
        tile = ms[i]
        centred = tile - jnp.mean(tile, axis=0, keepdims=True)
        rstd = lax.rsqrt(jnp.mean(centred * centred, axis=0, keepdims=True) + 1e-06)
        normed = centred * rstd
        ms[i] = normed
        rstds.append(rstd)
        nh[0:C, i * LAT : (i + 1) * LAT] = normed.astype(BF16)

    for copy in gathers[1]:
        copy.wait_recv()
    second = dot(from_padded, gb[...].reshape(CP, FP + 128))
    up_w[...] = second[:, 0:FP].astype(BF16)
    up_t[...] = second[:, 0:FP].T.astype(BF16)
    head_w[...] = second[:, FP : FP + 128]
    head_t[...] = second[:, FP : FP + 128].T.astype(BF16)
    for copy in gathers[2]:
        copy.wait_recv()
    for d in range(4):
        down_f[C * d : C * (d + 1), :] = gd[d].astype(F32)[0:C]
    down_w[...] = down_f[...].astype(BF16)
    down_t[...] = down_f[...].T.astype(BF16)

    sq[...] = jnp.zeros(sq.shape, F32)
    bo[...] = jnp.zeros(bo.shape, BF16)
    for j in range(COLS // 2):
        part = pl.ds(j * 2 * LAT, 2 * LAT)
        for f in range(0, FF, FB):
            u = dot(up_t[f : f + FB, :], nh[:, part])
            u2 = u * u
            half = 0.5 + 0.5 * jnp.tanh(u * (GELU_K + (GELU_K * 0.044715) * u2))
            value = u * half
            act[f : f + FB, part] = value.astype(BF16)
            slope[f : f + FB, part] = half + value * (1.0 - half) * (
                2.0 * GELU_K + (6.0 * GELU_K * 0.044715) * u2
            )
        branch = dot(down_t[...], act[:, part])[0:C]
        centre = jnp.concatenate([xs[HALO + 2 * j], xs[HALO + 2 * j + 1]], axis=1)
        bo[0:C, part] = (centre + branch).astype(BF16)
        predicted = dot(head_t[0:VP, :], bo[:, part])
        for h in range(2):
            i = 2 * j + h
            ocean = land[i : i + 1, :].astype(F32)
            wanted = f32b[pl.ds(i, VP, stride=COLS), :]
            miss = (predicted[:, h * LAT : (h + 1) * LAT] - wanted) * ocean
            mis[:, i * LAT : (i + 1) * LAT] = miss.astype(BF16)
            sq[0:VP, :] = sq[0:VP, :] + miss * miss

    lanes = lax.broadcasted_iota(jnp.int32, (1, LAT), 1)
    ocean_local = jnp.sum(land[...].astype(F32))
    mine = jnp.sum(sq[...].T, axis=0, keepdims=True)
    sa[idx_a] = jnp.where(lanes == V, ocean_local, mine)
    stage(0, 16, peer_a, lambda j: sa.at[idx_a], sa.at[idx_a])

    nhp[...] = dot(to_padded, nh[...]).astype(BF16)
    small[:, 128:256] = jnp.zeros((CP, 128), F32)
    small[:, 128 : 128 + VP] = dot_nt(bo[...], mis[...])

    stage_wait(0, 16, sa)
    total = sa[0]
    for j in range(1, 16):
        total = total + sa[j]
    sb[idx_b] = total
    stage(1, 16, peer_b, lambda j: sb.at[idx_b], sb.at[idx_b])
    stage_wait(1, 16, sb)
    total = sb[0]
    for j in range(1, 16):
        total = total + sb[j]
    ocean_count = jnp.sum(jnp.where(lanes == V, total, 0.0), axis=1, keepdims=True)
    valid = lanes < V
    threshold = jnp.where(valid, clip[...].astype(F32) / 16.0, 1.0)
    mean_error = jnp.where(valid, total, 0.0) / ocean_count
    ratio = 1.0 + mean_error / threshold
    o_loss[...] = jnp.sum(jnp.where(valid, threshold * jnp.log(ratio), 0.0), axis=1, keepdims=True)
    factor = jnp.where(valid, 2.0 / (ocean_count * ratio), 0.0)

    small[:, 128:256] = small[:, 128:256] * factor
    scaled = (head_w[...] * factor).astype(BF16)
    for j in range(COLS // 2):
        part = pl.ds(j * 2 * LAT, 2 * LAT)
        grad = dot(scaled[:, 0:VP], mis[:, part])
        bg[:, part] = grad[0:C]
        bh[:, part] = grad.astype(BF16)
    gdn[FF : FF + 64, :] = jnp.zeros((64, CP), F32)
    for f in range(0, FF, FB):
        gdn[f : f + FB, :] = dot_nt(act[f : f + FB, :], bh[...])
    for d in range(4):
        for s in range(4):
            piece = (d % 2) * 8 + (d // 2) * 4 + s
            block = gdn[C * d + 64 * s : C * d + 64 * s + 64, :]
            ld[piece, 0:64, :] = block[:, 0:128].astype(BF16)
            ld[piece, 64:128, :] = block[:, 128:256].astype(BF16)
    away = pl.ds((1 - core) * 8, 8)
    copy_d = remote(ld.at[away], rd0, send_s.at[2], recv_s.at[2], sibling)
    copy_d.start()

    pre[FF:FP, :] = jnp.zeros((FP - FF, CELLS), BF16)
    for j in range(COLS // 2):
        part = pl.ds(j * 2 * LAT, 2 * LAT)
        for f in range(0, FF, FB):
            pre[f : f + FB, part] = (
                dot(down_w[f : f + FB, :], bh[:, part]) * slope[f : f + FB, part]
            ).astype(BF16)
    gup[...] = dot_nt(nhp[...], pre[...])
    for d in range(4):
        for s in range(4):
            piece = (d % 2) * 8 + (d // 2) * 4 + s
            for l in range(7):
                lu[piece, 16 * l : 16 * l + 16, :] = gup[
                    64 * d + 16 * s : 64 * d + 16 * s + 16, 128 * l : 128 * l + 128
                ].astype(BF16)
            lu[piece, 112:128, :] = jnp.zeros((16, 128), BF16)
    copy_u = remote(lu.at[away], ru0, send_s.at[3], recv_s.at[3], sibling)
    copy_u.start()

    for j in range(COLS // 2):
        part = pl.ds(j * 2 * LAT, 2 * LAT)
        grad = dot(up_w[...], pre[:, part])[0:C]
        for h in range(2):
            i = 2 * j + h
            g = grad[:, h * LAT : (h + 1) * LAT]
            normed = ms[i]
            mean_g = jnp.mean(g, axis=0, keepdims=True)
            mean_gn = jnp.mean(g * normed, axis=0, keepdims=True)
            ms[i] = (rstds[i] * (g - mean_g - normed * mean_gn)).astype(BF16).astype(F32)

    copy_d.wait_recv()
    copy_u.wait_recv()
    for j in range(8):
        ls1[j, 0:128, :] = (ld[core * 8 + j].astype(F32) + rd0[j].astype(F32)).astype(BF16)
        ls1[j, 128:256, :] = (lu[core * 8 + j].astype(F32) + ru0[j].astype(F32)).astype(BF16)
    stage(4, 8, peer_c, lambda j: ls1.at[j], rx1.at[idx_c])

    def conv_backward(block, carry):
        here = pl.ds(pl.multiple_of(block * 8, 8), 8)
        x = [xs[s, here, :] for s in range(SLOTS)]
        m = [ms[i, here, :] for i in range(COLS)]
        weights = kern_w[here, :]
        out = [None] * SLOTS
        kern = jnp.zeros((8, LAT), F32)
        for q in range(SIDE):
            b = (q - 3) * 2
            if b != 0:
                shifted = [jnp.where(keep[-b], pltpu.roll(t, b % LAT, 1), 0.0) for t in m]
            else:
                shifted = m
            for p in range(SIDE):
                t = p * SIDE + q
                w = jnp.broadcast_to(weights[:, t : t + 1], (8, LAT))
                corr = None
                for i in range(COLS):
                    s = i + 2 * p
                    term = w * shifted[i]
                    out[s] = term if out[s] is None else out[s] + term
                    prod = shifted[i] * x[s]
                    corr = prod if corr is None else corr + prod
                kern = jnp.where(lane == V + t, jnp.sum(corr, axis=1, keepdims=True), kern)
        for s in range(SLOTS):
            back[s, here, :] = out[s]
        small[here, 128:256] = small[here, 128:256] + kern
        return carry

    lax.fori_loop(0, C // 8, conv_backward, 0)

    stage_wait(4, 8, rx1)
    rx1[idx_c] = ls1[idx_c]
    large = rx1[0].astype(F32)
    for j in range(1, 8):
        large = large + rx1[j].astype(F32)
    s2[...] = large.astype(BF16).reshape(16, 16, 128)
    stage(5, 16, peer_b, lambda j: s2.at[j], rx2.at[idx_b])

    sh[C:CP, :] = jnp.zeros((CP - C, SLOTS * LAT), BF16)
    for s in range(SLOTS):
        value = back[s]
        if HALO <= s < HALO + COLS:
            value = value + bg[:, (s - HALO) * LAT : (s - HALO + 1) * LAT]
        sh[0:C, s * LAT : (s + 1) * LAT] = value.astype(BF16)
    small[:, 0:128] = jnp.zeros((CP, 128), F32)
    small[:, 0:VP] = dot_nt(sh[...], fm[...])
    smp[...] = dot(to_padded, small[...].astype(BF16)).astype(BF16)
    for d in range(4):
        for s in range(4):
            at = 64 * d + 16 * s
            stx[s * 4 + d, 0:16, :] = smp[at : at + 16, 0:128]
            stx[s * 4 + d, 16:32, :] = smp[at : at + 16, 128:256]
    stage(6, 16, peer_a, lambda j: stx.at[j], srx.at[idx_a])

    for s in list(range(0, HALO, 2)) + list(range(HALO + COLS, SLOTS, 2)):
        value = dot(stem_t[0:VP, :], sh[:, s * LAT : (s + 2) * LAT]).astype(BF16)
        sen[s if s < HALO else s - COLS] = value[:, 0:LAT]
        sen[s + 1 if s < HALO else s + 1 - COLS] = value[:, LAT : 2 * LAT]
    copy_l = remote(sen.at[pl.ds(0, 6)], hr, send_h.at[2], recv_h.at[2], left)
    copy_r = remote(sen.at[pl.ds(6, 6)], hl, send_h.at[3], recv_h.at[3], right)
    copy_l.start()
    copy_r.start()

    stage_wait(5, 16, rx2)
    rx2[idx_b] = s2[idx_b]
    part_sum = rx2[0].astype(F32)
    for j in range(1, 16):
        part_sum = part_sum + rx2[j].astype(F32)
    fin[idx_b] = part_sum.astype(BF16)
    stage(7, 16, peer_b, lambda j: fin.at[idx_b], fin.at[idx_b])

    stage_wait(6, 16, srx)
    srx[idx_a] = stx[idx_a]
    tiny = srx[0].astype(F32)
    for j in range(1, 16):
        tiny = tiny + srx[j].astype(F32)
    s2x[idx_b] = tiny.astype(BF16)
    stage(8, 16, peer_b, lambda j: s2x.at[idx_b], s2x.at[idx_b])

    stage_wait(7, 16, fin)
    lg[y] = fin[...].reshape(256, 128)
    stage(9, 4, peer_y, lambda j: lg.at[y], lg.at[y])

    stage_wait(8, 16, s2x)
    tiny = s2x[0].astype(F32)
    for j in range(1, 16):
        tiny = tiny + s2x[j].astype(F32)
    sfin[y] = tiny.astype(BF16)
    stage(10, 4, peer_y, lambda j: sfin.at[y], sfin.at[y])

    copy_l.wait_recv()
    copy_r.wait_recv()
    for j in range(COLS // 2):
        s = HALO + 2 * j
        value = dot(stem_t[0:VP, :], sh[:, s * LAT : (s + 2) * LAT])
        for h in range(2):
            i = 2 * j + h
            cells = value[:, h * LAT : (h + 1) * LAT]
            if i >= 2:
                cells = cells + hr[i - 2].astype(F32)
            if i < 6:
                cells = cells + hl[i].astype(F32)
            o_sens[pl.ds(i, V, stride=COLS), :] = (cells * ocean_count)[0:V]

    stage_wait(9, 4, lg)
    for s in range(4):
        rows = 16 if s < 3 else 2
        for l in range(7):
            width = min(128, FF - 128 * l)
            piece = lg[s, 128 + 16 * l : 144 + 16 * l, :].astype(F32)
            o_up[16 * s : 16 * s + rows, 128 * l : 128 * l + width] = piece[0:rows, 0:width]
        rows = 64 if s < 3 else 8
        piece = lg[s, 0:128, :].astype(F32)
        o_down[64 * s : 64 * s + rows, 0:128] = piece[0:rows]
        o_down[64 * s : 64 * s + rows, 128:C] = piece[64 : 64 + rows, 0 : C - 128]
    stage_wait(10, 4, sfin)
    for s in range(4):
        rows = 16 if s < 3 else 2
        piece = sfin[s].astype(F32)
        o_stem[16 * s : 16 * s + rows, :] = piece[0:rows, 0:V]
        o_head[16 * s : 16 * s + rows, :] = piece[16 : 16 + rows, 0:V]
        o_kern[16 * s : 16 * s + rows, :] = pltpu.roll(piece[16:32], LAT - V, 1)[0:rows, 0:49]

    for copy in gathers[0] + gathers[1] + gathers[2] + halo:
        copy.wait_send()
    for copy in (copy_d, copy_u, copy_l, copy_r):
        copy.wait_send()


SCRATCH = [
    ((VP * COLS, LAT), F32),
    ((VP * COLS, LAT), F32),
    ((SLOTS, VP, LAT), BF16),
    ((VP, SLOTS * LAT), BF16),
    ((64, 256 + FP + 128), F32),
    ((208, CP), F32),
    ((4, 64, 256), BF16),
    ((4, 64, FP + 128), BF16),
    ((4, 208, CP), BF16),
    ((CP, 128), BF16),
    ((128, CP), BF16),
    ((C, 128), F32),
    ((CP, FP), BF16),
    ((FP, CP), BF16),
    ((CP, 128), F32),
    ((128, CP), BF16),
    ((FF, CP), BF16),
    ((CP, FF), BF16),
    ((FF, CP), F32),
    ((SLOTS, C, LAT), F32),
    ((COLS, C, LAT), F32),
    ((CP, CELLS), BF16),
    ((CP, CELLS), BF16),
    ((FF, CELLS), BF16),
    ((FF, CELLS), F32),
    ((FP, CELLS), BF16),
    ((CP, CELLS), BF16),
    ((VP, CELLS), BF16),
    ((128, LAT), F32),
    ((16, 1, LAT), F32),
    ((16, 1, LAT), F32),
    ((C, CELLS), F32),
    ((CP, CELLS), BF16),
    ((FF + 64, CP), F32),
    ((CP, FP), F32),
    ((SLOTS, C, LAT), F32),
    ((CP, SLOTS * LAT), BF16),
    ((CP, 256), F32),
    ((CP, 256), BF16),
    ((16, 128, 128), BF16),
    ((16, 128, 128), BF16),
    ((8, 128, 128), BF16),
    ((8, 128, 128), BF16),
    ((8, 256, 128), BF16),
    ((8, 256, 128), BF16),
    ((16, 16, 128), BF16),
    ((16, 16, 128), BF16),
    ((16, 16, 128), BF16),
    ((4, 256, 128), BF16),
    ((16, 32, 128), BF16),
    ((16, 32, 128), BF16),
    ((16, 32, 128), BF16),
    ((4, 32, 128), BF16),
    ((12, VP, LAT), BF16),
    ((6, VP, LAT), BF16),
    ((6, VP, LAT), BF16),
]


def shards(
    fields, targets, land_sea, clip_level, stem_weight, dw_kernel, up_weight, down_weight, head_weight
):
    clip = jnp.pad(clip_level.reshape(1, V), ((0, 0), (0, LAT - V)), constant_values=16)
    shapes = [(50, V), (50, 49), (50, FF), (C, C), (50, V), (1, 1), (V * COLS, LAT)]
    vmem = pl.BlockSpec(memory_space=pltpu.VMEM)
    dma = pltpu.SemaphoreType.DMA
    outs = pl.pallas_call(
        body,
        out_shape=[jax.ShapeDtypeStruct(s, F32) for s in shapes],
        in_specs=[vmem] * 9,
        out_specs=[vmem] * 7,
        scratch_shapes=[pltpu.VMEM(s, t) for s, t in SCRATCH]
        + [dma((9,)), dma((9,)), dma((4,)), dma((4,)), dma((11,)), dma((11,))],
        compiler_params=pltpu.CompilerParams(
            collective_id=0, has_side_effects=True, vmem_limit_bytes=58 * 1024 * 1024
        ),
    )(
        fields.reshape(V, COLS, LAT),
        targets.reshape(V, COLS, LAT),
        land_sea,
        clip,
        stem_weight,
        dw_kernel,
        up_weight,
        down_weight,
        head_weight,
    )
    return (
        outs[0], outs[1], outs[2], outs[3], outs[4],
        outs[5].reshape(()),
        outs[6].reshape(1, V, COLS, LAT),
    )


def solution(mesh):
    placed = (
        P("dp", None, "lon", None),
        P("dp", None, "lon", None),
        P("lon", None),
        P(),
        P("dp", None),
        P("dp", None),
        P("dp", None),
        P("dp", None),
        P("dp", None),
    )
    return jax.shard_map(
        shards,
        mesh=mesh,
        in_specs=placed,
        out_specs=(
            P("dp", None),
            P("dp", None),
            P("dp", None),
            P("dp", None),
            P("dp", None),
            P(),
            P("dp", None, "lon", None),
        ),
        check_vma=False,
    )
```

```python
import jax
import jax.numpy as jnp
from jax import lax
from jax.experimental import pallas as pl
from jax.experimental.pallas import tpu as pltpu
from jax.sharding import PartitionSpec as P

MESH = pl.DeviceIdType.MESH
F32 = jnp.float32
BF16 = jnp.bfloat16

V = 77
VP = 80
C = 200
CP = 256
FF = 800
FP = 896
FB = 160
COLS = 8
LAT = 128
SIDE = 7
HALO = 6
SLOTS = COLS + 2 * HALO
CELLS = COLS * LAT
GELU_K = 0.7978845608


def dot(a, b):
    return jnp.dot(a, b, preferred_element_type=F32)


def dot_nt(a, b):
    return lax.dot_general(a, b, (((1,), (1,)), ((), ())), preferred_element_type=F32)


def remote(src, dst, send, recv, device):
    return pltpu.make_async_remote_copy(
        src_ref=src,
        dst_ref=dst,
        send_sem=send,
        recv_sem=recv,
        device_id=device,
        device_id_type=MESH,
    )


def padded_row(channel):
    step = (channel >= 50).astype(jnp.int32)
    step += (channel >= 100).astype(jnp.int32)
    step += (channel >= 150).astype(jnp.int32)
    return channel + 14 * step


def body(
    fields, targets, land, clip, stem, dw, up, down, head,
    o_large, o_tiny, o_cells, o_loss,
    f32a, f32b, fbuf, fm, wp, wd, ga, gb, gd,
    stem_w, stem_t, up_w, up_t, head_w, head_t, down_w, down_t, down_f,
    taps, corrs, xs, ms, nh, nhp, act, slope, pre, bo, mis, limits, sq, sa, sb,
    bg, bh, gdn, gup, back, sh, small, smp,
    ld, lu, rd0, ru0, ls1, rx1, s2, rx2, fin, lg,
    stx, srx, s2x, sfin, sen, hl, hr,
    send_g, recv_g, send_h, recv_h, send_s, recv_s,
):
    lon = lax.axis_index("lon")
    dp = lax.axis_index("dp")
    x_hi, y, z = lon // 32, (lon // 8) % 4, lon % 8
    x_lo, core = dp // 2, dp % 2
    right = ((lon + 1) % 64, dp)
    left = ((lon + 63) % 64, dp)
    sibling = (lon, x_lo * 2 + (1 - core))
    idx_a = y * 4 + dp
    idx_b = x_hi * 8 + z
    idx_c = x_lo * 4 + y

    def peer_a(k):
        j = (idx_a + k) % 16
        return j, (x_hi * 32 + (j // 4) * 8 + z, j % 4)

    def peer_b(k):
        j = (idx_b + k) % 16
        return j, ((j // 8) * 32 + y * 8 + j % 8, dp)

    def peer_c(k):
        j = (idx_c + k) % 8
        return j, (x_hi * 32 + (j % 4) * 8 + z, (j // 4) * 2 + core)

    def peer_y(k):
        j = (y + k) % 4
        return j, (x_hi * 32 + j * 8 + z, dp)

    barrier = pltpu.get_barrier_semaphore()
    for target in (right, left):
        pl.semaphore_signal(barrier, inc=1, device_id=target, device_id_type=MESH)
    for k in range(1, 16):
        pl.semaphore_signal(barrier, inc=1, device_id=peer_a(k)[1], device_id_type=MESH)
        pl.semaphore_signal(barrier, inc=1, device_id=peer_b(k)[1], device_id_type=MESH)

    f32a[0 : V * COLS, :] = fields[...].astype(F32).reshape(V * COLS, LAT)
    f32a[V * COLS : VP * COLS, :] = jnp.zeros(((VP - V) * COLS, LAT), F32)
    f32b[0 : V * COLS, :] = targets[...].astype(F32).reshape(V * COLS, LAT)
    f32b[V * COLS : VP * COLS, :] = jnp.zeros(((VP - V) * COLS, LAT), F32)
    for i in range(COLS):
        fbuf[HALO + i] = f32a[pl.ds(i, VP, stride=COLS), :].astype(BF16)
    wp[...] = jnp.zeros(wp.shape, F32)
    wp[0:50, 0:V] = stem[...].astype(F32)
    wp[0:50, 128:177] = dw[...].astype(F32)
    wp[0:50, 256 : 256 + FF] = up[...].astype(F32)
    wp[0:50, 256 + FP : 256 + FP + V] = head[...].astype(F32)
    wd[...] = jnp.zeros(wd.shape, F32)
    wd[0:C, 0:C] = down[...].astype(F32)
    ga[dp] = wp[:, 0:256].astype(BF16)
    gb[dp] = wp[:, 256 : 256 + FP + 128].astype(BF16)
    gd[dp] = wd[...].astype(BF16)

    pl.semaphore_wait(barrier, 32)

    halo = [
        remote(fbuf.at[pl.ds(8, 6)], fbuf.at[pl.ds(0, 6)], send_h.at[0], recv_h.at[0], right),
        remote(fbuf.at[pl.ds(6, 6)], fbuf.at[pl.ds(14, 6)], send_h.at[1], recv_h.at[1], left),
    ]
    first_weights = [
        remote(ga.at[dp], ga.at[dp], send_g.at[k - 1], recv_g.at[k - 1], (lon, (dp + k) % 4))
        for k in range(1, 4)
    ]
    for copy in first_weights + halo:
        copy.start()
    across = (lon, (1 - x_lo) * 2 + core)
    far = (1 - x_lo) * 2 + core
    large_weights = []
    for a, buf in enumerate((gb, gd)):
        at = 3 + 3 * a
        large_weights.append(
            (
                remote(buf.at[dp], buf.at[dp], send_g.at[at], recv_g.at[at], across),
                remote(buf.at[dp], buf.at[dp], send_g.at[at + 1], recv_g.at[at + 1], sibling),
                remote(buf.at[far], buf.at[far], send_g.at[at + 2], recv_g.at[at + 2], sibling),
            )
        )

    def stage(index, count, peers, src, dst):
        for k in range(1, count):
            j, device = peers(k)
            remote(src(j), dst, send_s.at[index], recv_s.at[index], device).start()

    def stage_wait(index, count, buf):
        whole = buf.at[pl.ds(0, count - 1)]
        both = remote(whole, whole, send_s.at[index], recv_s.at[index], right)
        both.wait_recv()
        both.wait_send()

    row = lax.broadcasted_iota(jnp.int32, (CP, CP), 0)
    col = lax.broadcasted_iota(jnp.int32, (CP, CP), 1)
    from_padded = jnp.where((row < C) & (col == padded_row(row)), 1.0, 0.0).astype(BF16)
    to_padded = jnp.where((col < C) & (row == padded_row(col)), 1.0, 0.0).astype(BF16)
    lane = lax.broadcasted_iota(jnp.int32, (8, LAT), 1)
    keep = {b: (lane + b >= 0) & (lane + b < LAT) for b in range(-HALO, HALO + 1, 2)}

    for i in range(COLS):
        fm[:, (HALO + i) * LAT : (HALO + i + 1) * LAT] = fbuf[HALO + i]

    for copy in first_weights:
        copy.wait_recv()
    for group in large_weights:
        group[0].start()
        group[1].start()
    first = dot(from_padded, ga[...].reshape(CP, 256))
    stem_w[...] = first[:, 0:128].astype(BF16)
    stem_t[...] = first[:, 0:128].T.astype(BF16)
    def stem_pair(s):
        out = dot(stem_w[:, 0:VP], fm[:, s * LAT : (s + 2) * LAT])[0:C].astype(BF16).astype(F32)
        xs[s] = out[:, 0:LAT]
        xs[s + 1] = out[:, LAT : 2 * LAT]

    for s in range(HALO, HALO + COLS, 2):
        stem_pair(s)
    kern_w = first[0:C, 128:256].astype(BF16)
    tap_row = lax.broadcasted_iota(jnp.int32, (LAT, 2 * LAT), 0)
    second_half = (lax.broadcasted_iota(jnp.int32, (LAT, 2 * LAT), 1) >= LAT).astype(jnp.int32)
    for t in range(0, SIDE * SIDE, 2):
        spread = dot(kern_w, jnp.where(tap_row == t + second_half, 1.0, 0.0).astype(BF16))
        taps[t] = spread[:, 0:LAT]
        if t + 1 < SIDE * SIDE:
            taps[t + 1] = spread[:, LAT : 2 * LAT]
    for copy in halo:
        copy.wait_recv()
    for s in list(range(0, HALO)) + list(range(HALO + COLS, SLOTS)):
        fm[:, s * LAT : (s + 1) * LAT] = fbuf[s]
    for s in list(range(0, HALO, 2)) + list(range(HALO + COLS, SLOTS, 2)):
        stem_pair(s)

    def conv_forward(block, carry):
        here = pl.ds(pl.multiple_of(block * 8, 8), 8)
        for first_col in (0, 4):
            x = [xs[first_col + s, here, :] for s in range(4 + 2 * HALO)]
            out = [None] * 4
            for q in range(SIDE):
                b = (q - 3) * 2
                w = [taps[p * SIDE + q, here, :] for p in range(SIDE)]
                for i in range(4):
                    total = w[0] * x[i]
                    for p in range(1, SIDE):
                        total = total + w[p] * x[i + 2 * p]
                    if b != 0:
                        total = jnp.where(keep[b], pltpu.roll(total, (-b) % LAT, 1), 0.0)
                    out[i] = total if out[i] is None else out[i] + total
            for i in range(4):
                ms[first_col + i, here, :] = out[i]
        return carry

    lax.fori_loop(0, 13, conv_forward, 0)
    large_weights[0][0].wait_recv()
    large_weights[0][2].start()
    lax.fori_loop(13, C // 8, conv_forward, 0)
    large_weights[1][0].wait_recv()
    large_weights[1][2].start()

    nh[...] = jnp.zeros(nh.shape, BF16)
    rstds = []
    for i in range(COLS):
        tile = ms[i]
        centred = tile - jnp.mean(tile, axis=0, keepdims=True)
        rstd = lax.rsqrt(jnp.mean(centred * centred, axis=0, keepdims=True) + 1e-06)
        normed = centred * rstd
        ms[i] = normed
        rstds.append(rstd)
        nh[0:C, i * LAT : (i + 1) * LAT] = normed.astype(BF16)

    large_weights[0][1].wait_recv()
    large_weights[0][2].wait_recv()
    second = dot(from_padded, gb[...].reshape(CP, FP + 128))
    up_w[...] = second[:, 0:FP].astype(BF16)
    up_t[...] = second[:, 0:FP].T.astype(BF16)
    head_w[...] = second[:, FP : FP + 128]
    head_t[...] = second[:, FP : FP + 128].T.astype(BF16)
    large_weights[1][1].wait_recv()
    large_weights[1][2].wait_recv()
    for d in range(4):
        down_f[C * d : C * (d + 1), :] = gd[d].astype(F32)[0:C]
    down_w[...] = down_f[...].astype(BF16)
    down_t[...] = down_f[...].T.astype(BF16)

    limits[...] = jnp.ones((1, LAT), F32)
    limits[:, 0:V] = clip[...].astype(F32) / 16.0
    sq[...] = jnp.zeros(sq.shape, F32)
    bo[...] = jnp.zeros(bo.shape, BF16)
    for j in range(COLS // 2):
        part = pl.ds(j * 2 * LAT, 2 * LAT)
        for f in range(0, FF, FB):
            u = dot(up_t[f : f + FB, :], nh[:, part])
            u2 = u * u
            half = 0.5 + 0.5 * jnp.tanh(u * (GELU_K + (GELU_K * 0.044715) * u2))
            value = u * half
            act[f : f + FB, part] = value.astype(BF16)
            slope[f : f + FB, part] = half + value * (1.0 - half) * (
                2.0 * GELU_K + (6.0 * GELU_K * 0.044715) * u2
            )
        branch = dot(down_t[...], act[:, part])[0:C]
        centre = jnp.concatenate([xs[HALO + 2 * j], xs[HALO + 2 * j + 1]], axis=1)
        bo[0:C, part] = (centre + branch).astype(BF16)
        predicted = dot(head_t[0:VP, :], bo[:, part])
        for h in range(2):
            i = 2 * j + h
            ocean = land[i : i + 1, :].astype(F32)
            wanted = f32b[pl.ds(i, VP, stride=COLS), :]
            miss = (predicted[:, h * LAT : (h + 1) * LAT] - wanted) * ocean
            mis[:, i * LAT : (i + 1) * LAT] = miss.astype(BF16)
            sq[0:VP, :] = sq[0:VP, :] + miss * miss

    lanes = lax.broadcasted_iota(jnp.int32, (1, LAT), 1)
    ocean_local = jnp.sum(land[...].astype(F32))
    mine = jnp.sum(sq[...].T, axis=0, keepdims=True)
    sa[idx_a] = jnp.where(lanes == V, ocean_local, mine)
    stage(0, 16, peer_a, lambda j: sa.at[idx_a], sa.at[idx_a])

    nhp[...] = dot(to_padded, nh[...]).astype(BF16)
    small[:, 128:256] = jnp.zeros((CP, 128), F32)
    small[:, 128 : 128 + VP] = dot_nt(bo[...], mis[...])

    stage_wait(0, 16, sa)
    total = sa[0]
    for j in range(1, 16):
        total = total + sa[j]
    sb[idx_b] = total
    stage(1, 16, peer_b, lambda j: sb.at[idx_b], sb.at[idx_b])
    stage_wait(1, 16, sb)
    total = sb[0]
    for j in range(1, 16):
        total = total + sb[j]
    ocean_count = jnp.sum(jnp.where(lanes == V, total, 0.0), axis=1, keepdims=True)
    valid = lanes < V
    threshold = limits[...]
    mean_error = jnp.where(valid, total, 0.0) / ocean_count
    ratio = 1.0 + mean_error / threshold
    o_loss[...] = jnp.sum(jnp.where(valid, threshold * jnp.log(ratio), 0.0), axis=1, keepdims=True)
    factor = jnp.where(valid, 2.0 / (ocean_count * ratio), 0.0)

    small[:, 128:256] = small[:, 128:256] * factor
    scaled = (head_w[...] * factor).astype(BF16)
    for j in range(COLS // 2):
        part = pl.ds(j * 2 * LAT, 2 * LAT)
        grad = dot(scaled[:, 0:VP], mis[:, part])
        bg[:, part] = grad[0:C]
        bh[:, part] = grad.astype(BF16)
    gdn[FF : FF + 64, :] = jnp.zeros((64, CP), F32)
    for f in range(0, FF, FB):
        gdn[f : f + FB, :] = dot_nt(act[f : f + FB, :], bh[...])
    for d in range(4):
        for s in range(4):
            piece = (d % 2) * 8 + (d // 2) * 4 + s
            block = gdn[C * d + 64 * s : C * d + 64 * s + 64, :]
            ld[piece, 0:64, :] = block[:, 0:128].astype(BF16)
            ld[piece, 64:128, :] = block[:, 128:256].astype(BF16)
    away = pl.ds((1 - core) * 8, 8)
    copy_d = remote(ld.at[away], rd0, send_s.at[2], recv_s.at[2], sibling)
    copy_d.start()

    pre[FF:FP, :] = jnp.zeros((FP - FF, CELLS), BF16)
    for j in range(COLS // 2):
        part = pl.ds(j * 2 * LAT, 2 * LAT)
        for f in range(0, FF, FB):
            pre[f : f + FB, part] = (
                dot(down_w[f : f + FB, :], bh[:, part]) * slope[f : f + FB, part]
            ).astype(BF16)
    gup[...] = dot_nt(nhp[...], pre[...])
    for d in range(4):
        for s in range(4):
            piece = (d % 2) * 8 + (d // 2) * 4 + s
            for l in range(7):
                lu[piece, 16 * l : 16 * l + 16, :] = gup[
                    64 * d + 16 * s : 64 * d + 16 * s + 16, 128 * l : 128 * l + 128
                ].astype(BF16)
            lu[piece, 112:128, :] = jnp.zeros((16, 128), BF16)
    copy_u = remote(lu.at[away], ru0, send_s.at[3], recv_s.at[3], sibling)
    copy_u.start()

    for j in range(COLS // 2):
        part = pl.ds(j * 2 * LAT, 2 * LAT)
        grad = dot(up_w[...], pre[:, part])[0:C]
        for h in range(2):
            i = 2 * j + h
            g = grad[:, h * LAT : (h + 1) * LAT]
            normed = ms[i]
            mean_g = jnp.mean(g, axis=0, keepdims=True)
            mean_gn = jnp.mean(g * normed, axis=0, keepdims=True)
            ms[i] = (rstds[i] * (g - mean_g - normed * mean_gn)).astype(BF16).astype(F32)

    def conv_backward(block, carry):
        here = pl.ds(pl.multiple_of(block * 8, 8), 8)
        x = [xs[s, here, :] for s in range(SLOTS)]
        m = [ms[i, here, :] for i in range(COLS)]
        out = [None] * SLOTS
        for q in range(SIDE):
            b = (q - 3) * 2
            if b != 0:
                shifted = [jnp.where(keep[-b], pltpu.roll(t, b % LAT, 1), 0.0) for t in m]
            else:
                shifted = m
            for p in range(SIDE):
                t = p * SIDE + q
                w = taps[t, here, :]
                corr = None
                for i in range(COLS):
                    s = i + 2 * p
                    term = w * shifted[i]
                    out[s] = term if out[s] is None else out[s] + term
                    prod = shifted[i] * x[s]
                    corr = prod if corr is None else corr + prod
                corrs[t, here, :] = corr
        for s in range(SLOTS):
            back[s, here, :] = out[s]
        return carry

    lax.fori_loop(0, 6, conv_backward, 0)
    copy_d.wait_recv()
    copy_u.wait_recv()
    for j in range(8):
        ls1[j, 0:128, :] = (ld[core * 8 + j].astype(F32) + rd0[j].astype(F32)).astype(BF16)
        ls1[j, 128:256, :] = (lu[core * 8 + j].astype(F32) + ru0[j].astype(F32)).astype(BF16)
    stage(4, 8, peer_c, lambda j: ls1.at[j], rx1.at[idx_c])
    lax.fori_loop(6, C // 8, conv_backward, 0)
    tap_col = lax.broadcasted_iota(jnp.int32, (2 * LAT, LAT), 1)
    lower_half = (lax.broadcasted_iota(jnp.int32, (2 * LAT, LAT), 0) >= LAT).astype(jnp.int32)
    kern = None
    for t in range(0, SIDE * SIDE, 2):
        place = jnp.where(tap_col == V + t + lower_half, 1.0, 0.0).astype(BF16)
        terms = corrs[t].astype(BF16)
        if t + 1 < SIDE * SIDE:
            terms = jnp.concatenate([terms, corrs[t + 1].astype(BF16)], axis=1)
        else:
            place = place[0:LAT]
        part_sum = dot(terms, place)
        kern = part_sum if kern is None else kern + part_sum
    small[0:C, 128:256] = small[0:C, 128:256] + kern

    stage_wait(4, 8, rx1)
    rx1[idx_c] = ls1[idx_c]
    large = rx1[0].astype(F32)
    for j in range(1, 8):
        large = large + rx1[j].astype(F32)
    s2[...] = large.astype(BF16).reshape(16, 16, 128)
    stage(5, 16, peer_b, lambda j: s2.at[j], rx2.at[idx_b])

    sh[C:CP, :] = jnp.zeros((CP - C, SLOTS * LAT), BF16)
    for s in range(SLOTS):
        value = back[s]
        if HALO <= s < HALO + COLS:
            value = value + bg[:, (s - HALO) * LAT : (s - HALO + 1) * LAT]
        sh[0:C, s * LAT : (s + 1) * LAT] = value.astype(BF16)
    small[:, 0:128] = jnp.zeros((CP, 128), F32)
    small[:, 0:VP] = dot_nt(sh[...], fm[...])
    smp[...] = dot(to_padded, small[...].astype(BF16)).astype(BF16)
    for d in range(4):
        for s in range(4):
            at = 64 * d + 16 * s
            stx[s * 4 + d, 0:16, :] = smp[at : at + 16, 0:128]
            stx[s * 4 + d, 16:32, :] = smp[at : at + 16, 128:256]
    stage(6, 16, peer_a, lambda j: stx.at[j], srx.at[idx_a])

    for s in list(range(0, HALO, 2)) + list(range(HALO + COLS, SLOTS, 2)):
        value = dot(stem_t[0:VP, :], sh[:, s * LAT : (s + 2) * LAT]).astype(BF16)
        sen[s if s < HALO else s - COLS] = value[:, 0:LAT]
        sen[s + 1 if s < HALO else s + 1 - COLS] = value[:, LAT : 2 * LAT]
    copy_l = remote(sen.at[pl.ds(0, 6)], hr, send_h.at[2], recv_h.at[2], left)
    copy_r = remote(sen.at[pl.ds(6, 6)], hl, send_h.at[3], recv_h.at[3], right)
    copy_l.start()
    copy_r.start()

    stage_wait(5, 16, rx2)
    rx2[idx_b] = s2[idx_b]
    part_sum = rx2[0].astype(F32)
    for j in range(1, 16):
        part_sum = part_sum + rx2[j].astype(F32)
    fin[idx_b] = part_sum.astype(BF16)
    stage(7, 16, peer_b, lambda j: fin.at[idx_b], fin.at[idx_b])

    stage_wait(6, 16, srx)
    srx[idx_a] = stx[idx_a]
    tiny = srx[0].astype(F32)
    for j in range(1, 16):
        tiny = tiny + srx[j].astype(F32)
    s2x[idx_b] = tiny.astype(BF16)
    stage(8, 16, peer_b, lambda j: s2x.at[idx_b], s2x.at[idx_b])

    stage_wait(7, 16, fin)
    lg[y] = fin[...].reshape(256, 128)
    stage(9, 4, peer_y, lambda j: lg.at[y], lg.at[y])

    for j in range(COLS // 2):
        s = HALO + 2 * j
        value = dot(stem_t[0:VP, :], sh[:, s * LAT : (s + 2) * LAT])
        o_cells[2 * j] = value[:, 0:LAT]
        o_cells[2 * j + 1] = value[:, LAT : 2 * LAT]

    stage_wait(8, 16, s2x)
    tiny = s2x[0].astype(F32)
    for j in range(1, 16):
        tiny = tiny + s2x[j].astype(F32)
    sfin[y] = tiny.astype(BF16)
    stage(10, 4, peer_y, lambda j: sfin.at[y], sfin.at[y])

    copy_l.wait_recv()
    copy_r.wait_recv()
    for i in range(COLS):
        cells = o_cells[i]
        if i >= 2:
            cells = cells + hr[i - 2].astype(F32)
        if i < 6:
            cells = cells + hl[i].astype(F32)
        o_cells[i] = cells * ocean_count

    for copy in first_weights + halo + list(large_weights[0] + large_weights[1]):
        copy.wait_send()
    for copy in (copy_d, copy_u, copy_l, copy_r):
        copy.wait_send()
    stage_wait(9, 4, lg)
    o_large[...] = lg[...]
    stage_wait(10, 4, sfin)
    o_tiny[...] = sfin[...]


def write_outputs(large, tiny, cells, loss, o_stem, o_kern, o_up, o_down, o_head, o_loss, o_sens):
    o_loss[...] = loss[...]
    for i in range(COLS):
        o_sens[pl.ds(i, V, stride=COLS), :] = cells[i][0:V]
    for s in range(4):
        rows = 16 if s < 3 else 2
        for l in range(7):
            width = min(128, FF - 128 * l)
            piece = large[s, 128 + 16 * l : 144 + 16 * l, :].astype(F32)
            o_up[16 * s : 16 * s + rows, 128 * l : 128 * l + width] = piece[0:rows, 0:width]
        piece = tiny[s].astype(F32)
        o_stem[16 * s : 16 * s + rows, :] = piece[0:rows, 0:V]
        o_head[16 * s : 16 * s + rows, :] = piece[16 : 16 + rows, 0:V]
        o_kern[16 * s : 16 * s + rows, :] = pltpu.roll(piece[16:32], LAT - V, 1)[0:rows, 0:49]
        rows = 64 if s < 3 else 8
        piece = large[s, 0:128, :].astype(F32)
        o_down[64 * s : 64 * s + rows, 0:128] = piece[0:rows]
        o_down[64 * s : 64 * s + rows, 128:C] = piece[64 : 64 + rows, 0 : C - 128]


SCRATCH = [
    ((VP * COLS, LAT), F32),
    ((VP * COLS, LAT), F32),
    ((SLOTS, VP, LAT), BF16),
    ((VP, SLOTS * LAT), BF16),
    ((64, 256 + FP + 128), F32),
    ((208, CP), F32),
    ((4, 64, 256), BF16),
    ((4, 64, FP + 128), BF16),
    ((4, 208, CP), BF16),
    ((CP, 128), BF16),
    ((128, CP), BF16),
    ((CP, FP), BF16),
    ((FP, CP), BF16),
    ((CP, 128), F32),
    ((128, CP), BF16),
    ((FF, CP), BF16),
    ((CP, FF), BF16),
    ((FF, CP), F32),
    ((SIDE * SIDE, C, LAT), F32),
    ((SIDE * SIDE, C, LAT), F32),
    ((SLOTS, C, LAT), F32),
    ((COLS, C, LAT), F32),
    ((CP, CELLS), BF16),
    ((CP, CELLS), BF16),
    ((FF, CELLS), BF16),
    ((FF, CELLS), F32),
    ((FP, CELLS), BF16),
    ((CP, CELLS), BF16),
    ((VP, CELLS), BF16),
    ((1, LAT), F32),
    ((128, LAT), F32),
    ((16, 1, LAT), F32),
    ((16, 1, LAT), F32),
    ((C, CELLS), F32),
    ((CP, CELLS), BF16),
    ((FF + 64, CP), F32),
    ((CP, FP), F32),
    ((SLOTS, C, LAT), F32),
    ((CP, SLOTS * LAT), BF16),
    ((CP, 256), F32),
    ((CP, 256), BF16),
    ((16, 128, 128), BF16),
    ((16, 128, 128), BF16),
    ((8, 128, 128), BF16),
    ((8, 128, 128), BF16),
    ((8, 256, 128), BF16),
    ((8, 256, 128), BF16),
    ((16, 16, 128), BF16),
    ((16, 16, 128), BF16),
    ((16, 16, 128), BF16),
    ((4, 256, 128), BF16),
    ((16, 32, 128), BF16),
    ((16, 32, 128), BF16),
    ((16, 32, 128), BF16),
    ((4, 32, 128), BF16),
    ((12, VP, LAT), BF16),
    ((6, VP, LAT), BF16),
    ((6, VP, LAT), BF16),
]


def shards(
    fields, targets, land_sea, clip_level, stem_weight, dw_kernel, up_weight, down_weight, head_weight
):
    vmem = pl.BlockSpec(memory_space=pltpu.VMEM)
    dma = pltpu.SemaphoreType.DMA
    made = pl.pallas_call(
        body,
        out_shape=[
            jax.ShapeDtypeStruct((4, 256, 128), BF16),
            jax.ShapeDtypeStruct((4, 32, 128), BF16),
            jax.ShapeDtypeStruct((COLS, VP, LAT), F32),
            jax.ShapeDtypeStruct((1, 1), F32),
        ],
        in_specs=[vmem] * 9,
        out_specs=[vmem] * 4,
        scratch_shapes=[pltpu.VMEM(s, t) for s, t in SCRATCH]
        + [dma((9,)), dma((9,)), dma((4,)), dma((4,)), dma((11,)), dma((11,))],
        compiler_params=pltpu.CompilerParams(
            collective_id=0, has_side_effects=True, vmem_limit_bytes=58 * 1024 * 1024
        ),
    )(
        fields.reshape(V, COLS, LAT),
        targets.reshape(V, COLS, LAT),
        land_sea,
        clip_level.reshape(1, V),
        stem_weight,
        dw_kernel,
        up_weight,
        down_weight,
        head_weight,
    )
    shapes = [(50, V), (50, 49), (50, FF), (C, C), (50, V), (1, 1), (V * COLS, LAT)]
    outs = pl.pallas_call(
        write_outputs,
        out_shape=[jax.ShapeDtypeStruct(s, F32) for s in shapes],
        in_specs=[vmem] * 4,
        out_specs=[vmem] * 7,
    )(*made)
    return (
        outs[0], outs[1], outs[2], outs[3], outs[4],
        outs[5].reshape(()),
        outs[6].reshape(1, V, COLS, LAT),
    )


def solution(mesh):
    placed = (
        P("dp", None, "lon", None),
        P("dp", None, "lon", None),
        P("lon", None),
        P(),
        P("dp", None),
        P("dp", None),
        P("dp", None),
        P("dp", None),
        P("dp", None),
    )
    return jax.shard_map(
        shards,
        mesh=mesh,
        in_specs=placed,
        out_specs=(
            P("dp", None),
            P("dp", None),
            P("dp", None),
            P("dp", None),
            P("dp", None),
            P(),
            P("dp", None, "lon", None),
        ),
        check_vma=False,
    )
```

```python
import jax
import jax.numpy as jnp
from jax import lax
from jax.experimental import pallas as pl
from jax.experimental.pallas import tpu as pltpu
from jax.sharding import PartitionSpec as P

MESH = pl.DeviceIdType.MESH
F32 = jnp.float32
BF16 = jnp.bfloat16

V = 77
VP = 80
C = 200
CP = 256
FF = 800
FP = 896
FB = 160
COLS = 8
LAT = 128
SIDE = 7
HALO = 6
SLOTS = COLS + 2 * HALO
CELLS = COLS * LAT
GELU_K = 0.7978845608


def dot(a, b):
    return jnp.dot(a, b, preferred_element_type=F32)


def dot_nt(a, b):
    return lax.dot_general(a, b, (((1,), (1,)), ((), ())), preferred_element_type=F32)


def remote(src, dst, send, recv, device):
    return pltpu.make_async_remote_copy(
        src_ref=src,
        dst_ref=dst,
        send_sem=send,
        recv_sem=recv,
        device_id=device,
        device_id_type=MESH,
    )


def padded_row(channel):
    step = (channel >= 50).astype(jnp.int32)
    step += (channel >= 100).astype(jnp.int32)
    step += (channel >= 150).astype(jnp.int32)
    return channel + 14 * step


def body(*refs):
    inputs, outputs, rest = refs[:9], refs[9:16], refs[16:]
    held, made = rest[:9], rest[9:16]
    o_stem, o_kern, o_up, o_down, o_head, o_loss, o_sens = made
    fields, targets, land, clip, stem, dw, up, down, head = held
    (
    f32a, f32b, fbuf, fm, wp, wd, ga, gb, gd,
        stem_w, stem_t, up_w, up_t, head_w, head_t, down_w, down_t, down_f,
        taps, corrs, xs, ms, nh, nhp, act, slope, pre, bo, mis, limits, sq, sa, sb,
        bg, bh, gdn, gup, back, sh, small, smp,
        ld, lu, rd0, ru0, ls_d, ls_u, rx_d, rx_u, part_large, lg,
        stx, srx, s2x, sfin, sen, hl, hr, cells,
        send_g, recv_g, send_h, recv_h, send_s, recv_s, load_sem, store_sem,
    ) = rest[16:]
    lon = lax.axis_index("lon")
    dp = lax.axis_index("dp")
    x_hi, y, z = lon // 32, (lon // 8) % 4, lon % 8
    x_lo, core = dp // 2, dp % 2
    right = ((lon + 1) % 64, dp)
    left = ((lon + 63) % 64, dp)
    sibling = (lon, x_lo * 2 + (1 - core))
    idx_p = (x_hi * 4 + y) * 4 + dp
    idx_m = (x_lo * 4 + y) * 2 + x_hi
    idx_h = x_hi * 4 + y

    def peer_p(k):
        j = (idx_p + k) % 32
        return j, ((j // 4) * 8 + z, j % 4)

    def peer_z(k):
        j = (z + k) % 8
        return j, (x_hi * 32 + y * 8 + j, dp)

    def peer_m(k):
        j = (idx_m + k) % 16
        return j, ((j % 2) * 32 + ((j // 2) % 4) * 8 + z, (j // 8) * 2 + core)

    def peer_h(k):
        j = (idx_h + k) % 8
        return j, (j * 8 + z, dp)

    loads = [
        pltpu.make_async_copy(src, dst, load_sem.at[n])
        for n, (src, dst) in enumerate(zip(inputs, held))
    ]
    for copy in loads:
        copy.start()
    stores = [
        pltpu.make_async_copy(src, dst, store_sem.at[n])
        for n, (src, dst) in enumerate(zip(made, outputs))
    ]

    barrier = pltpu.get_barrier_semaphore()
    for target in (right, left):
        pl.semaphore_signal(barrier, inc=1, device_id=target, device_id_type=MESH)
    for k in range(1, 32):
        pl.semaphore_signal(barrier, inc=1, device_id=peer_p(k)[1], device_id_type=MESH)
    for k in range(1, 8):
        pl.semaphore_signal(barrier, inc=1, device_id=peer_z(k)[1], device_id_type=MESH)

    for copy in loads:
        copy.wait()
    f32a[0 : V * COLS, :] = fields[...].astype(F32).reshape(V * COLS, LAT)
    f32a[V * COLS : VP * COLS, :] = jnp.zeros(((VP - V) * COLS, LAT), F32)
    f32b[0 : V * COLS, :] = targets[...].astype(F32).reshape(V * COLS, LAT)
    f32b[V * COLS : VP * COLS, :] = jnp.zeros(((VP - V) * COLS, LAT), F32)
    for i in range(COLS):
        fbuf[HALO + i] = f32a[pl.ds(i, VP, stride=COLS), :].astype(BF16)
    wp[...] = jnp.zeros(wp.shape, F32)
    wp[0:50, 0:V] = stem[...].astype(F32)
    wp[0:50, 128:177] = dw[...].astype(F32)
    wp[0:50, 256 : 256 + FF] = up[...].astype(F32)
    wp[0:50, 256 + FP : 256 + FP + V] = head[...].astype(F32)
    wd[...] = jnp.zeros(wd.shape, F32)
    wd[0:C, 0:C] = down[...].astype(F32)
    ga[dp] = wp[:, 0:256].astype(BF16)
    gb[dp] = wp[:, 256 : 256 + FP + 128].astype(BF16)
    gd[dp] = wd[...].astype(BF16)

    pl.semaphore_wait(barrier, 40)

    halo = [
        remote(fbuf.at[pl.ds(8, 6)], fbuf.at[pl.ds(0, 6)], send_h.at[0], recv_h.at[0], right),
        remote(fbuf.at[pl.ds(6, 6)], fbuf.at[pl.ds(14, 6)], send_h.at[1], recv_h.at[1], left),
    ]
    first_weights = [
        remote(ga.at[dp], ga.at[dp], send_g.at[k - 1], recv_g.at[k - 1], (lon, (dp + k) % 4))
        for k in range(1, 4)
    ]
    for copy in first_weights:
        copy.start()
    across = (lon, (1 - x_lo) * 2 + core)
    far = (1 - x_lo) * 2 + core
    large_weights = []
    for a, buf in enumerate((gb, gd)):
        at = 3 + 3 * a
        large_weights.append(
            (
                remote(buf.at[dp], buf.at[dp], send_g.at[at], recv_g.at[at], across),
                remote(buf.at[dp], buf.at[dp], send_g.at[at + 1], recv_g.at[at + 1], sibling),
                remote(buf.at[far], buf.at[far], send_g.at[at + 2], recv_g.at[at + 2], sibling),
            )
        )

    def pass_on(a):
        large_weights[a][0].wait_recv()
        large_weights[a][2].start()

    pending = []

    def stage(index, count, peers, src, dst):
        for k in range(1, count):
            j, device = peers(k)
            remote(src(j), dst, send_s.at[index], recv_s.at[index], device).start()

    def stage_wait(index, count, buf):
        whole = buf.at[pl.ds(0, count - 1)]
        both = remote(whole, whole, send_s.at[index], recv_s.at[index], right)
        both.wait_recv()
        pending.append(both)

    row = lax.broadcasted_iota(jnp.int32, (CP, CP), 0)
    col = lax.broadcasted_iota(jnp.int32, (CP, CP), 1)
    from_padded = jnp.where((row < C) & (col == padded_row(row)), 1.0, 0.0).astype(BF16)
    to_padded = jnp.where((col < C) & (row == padded_row(col)), 1.0, 0.0).astype(BF16)
    lane = lax.broadcasted_iota(jnp.int32, (8, LAT), 1)
    keep = {b: (lane + b >= 0) & (lane + b < LAT) for b in range(-HALO, HALO + 1, 2)}

    for i in range(COLS):
        fm[:, (HALO + i) * LAT : (HALO + i + 1) * LAT] = fbuf[HALO + i]

    for copy in halo:
        copy.start()
    for copy in first_weights:
        copy.wait_recv()
    large_weights[0][0].start()
    large_weights[0][1].start()
    large_weights[1][1].start()
    first = dot(from_padded, ga[...].reshape(CP, 256))
    stem_w[...] = first[:, 0:128].astype(BF16)
    stem_t[...] = first[:, 0:128].T.astype(BF16)
    def stem_pair(s):
        out = dot(stem_w[:, 0:VP], fm[:, s * LAT : (s + 2) * LAT])[0:C].astype(BF16).astype(F32)
        xs[s] = out[:, 0:LAT]
        xs[s + 1] = out[:, LAT : 2 * LAT]

    for s in range(HALO, HALO + COLS, 2):
        stem_pair(s)
    kern_w = first[0:C, 128:256].astype(BF16)
    tap_row = lax.broadcasted_iota(jnp.int32, (LAT, 2 * LAT), 0)
    second_half = (lax.broadcasted_iota(jnp.int32, (LAT, 2 * LAT), 1) >= LAT).astype(jnp.int32)
    for t in range(0, SIDE * SIDE, 2):
        spread = dot(kern_w, jnp.where(tap_row == t + second_half, 1.0, 0.0).astype(BF16))
        taps[t] = spread[:, 0:LAT]
        if t + 1 < SIDE * SIDE:
            taps[t + 1] = spread[:, LAT : 2 * LAT]
    for copy in halo:
        copy.wait_recv()
    for s in list(range(0, HALO)) + list(range(HALO + COLS, SLOTS)):
        fm[:, s * LAT : (s + 1) * LAT] = fbuf[s]
    for s in list(range(0, HALO, 2)) + list(range(HALO + COLS, SLOTS, 2)):
        stem_pair(s)

    def conv_forward(block, carry):
        here = pl.ds(pl.multiple_of(block * 8, 8), 8)
        for first_col in (0, 4):
            x = [xs[first_col + s, here, :] for s in range(4 + 2 * HALO)]
            out = [None] * 4
            for q in range(SIDE):
                b = (q - 3) * 2
                w = [taps[p * SIDE + q, here, :] for p in range(SIDE)]
                for i in range(4):
                    total = w[0] * x[i]
                    for p in range(1, SIDE):
                        total = total + w[p] * x[i + 2 * p]
                    if b != 0:
                        total = jnp.where(keep[b], pltpu.roll(total, (-b) % LAT, 1), 0.0)
                    out[i] = total if out[i] is None else out[i] + total
            for i in range(4):
                ms[first_col + i, here, :] = out[i]
        return carry

    lax.fori_loop(0, 13, conv_forward, 0)
    pass_on(0)
    large_weights[1][0].start()
    lax.fori_loop(13, C // 8, conv_forward, 0)

    nh[...] = jnp.zeros(nh.shape, BF16)
    rstds = []
    for i in range(COLS):
        tile = ms[i]
        centred = tile - jnp.mean(tile, axis=0, keepdims=True)
        rstd = lax.rsqrt(jnp.mean(centred * centred, axis=0, keepdims=True) + 1e-06)
        normed = centred * rstd
        ms[i] = normed
        rstds.append(rstd)
        nh[0:C, i * LAT : (i + 1) * LAT] = normed.astype(BF16)

    large_weights[0][1].wait_recv()
    large_weights[0][2].wait_recv()
    second = dot(from_padded, gb[...].reshape(CP, FP + 128))
    up_w[...] = second[:, 0:FP].astype(BF16)
    up_t[...] = second[:, 0:FP].T.astype(BF16)
    head_w[...] = second[:, FP : FP + 128]
    head_t[...] = second[:, FP : FP + 128].T.astype(BF16)
    limits[...] = jnp.ones((1, LAT), F32)
    limits[:, 0:V] = clip[...].astype(F32) / 16.0
    sq[...] = jnp.zeros(sq.shape, F32)
    bo[...] = jnp.zeros(bo.shape, BF16)
    for j in range(0, 2):
        part = pl.ds(j * 2 * LAT, 2 * LAT)
        for f in range(0, FF, FB):
            u = dot(up_t[f : f + FB, :], nh[:, part])
            u2 = u * u
            half = 0.5 + 0.5 * jnp.tanh(u * (GELU_K + (GELU_K * 0.044715) * u2))
            value = u * half
            act[f : f + FB, part] = value.astype(BF16)
            slope[f : f + FB, part] = half + value * (1.0 - half) * (
                2.0 * GELU_K + (6.0 * GELU_K * 0.044715) * u2
            )
    pass_on(1)
    for j in range(2, 4):
        part = pl.ds(j * 2 * LAT, 2 * LAT)
        for f in range(0, FF, FB):
            u = dot(up_t[f : f + FB, :], nh[:, part])
            u2 = u * u
            half = 0.5 + 0.5 * jnp.tanh(u * (GELU_K + (GELU_K * 0.044715) * u2))
            value = u * half
            act[f : f + FB, part] = value.astype(BF16)
            slope[f : f + FB, part] = half + value * (1.0 - half) * (
                2.0 * GELU_K + (6.0 * GELU_K * 0.044715) * u2
            )
    large_weights[1][1].wait_recv()
    large_weights[1][2].wait_recv()
    for d in range(4):
        down_f[C * d : C * (d + 1), :] = gd[d].astype(F32)[0:C]
    down_w[...] = down_f[...].astype(BF16)
    down_t[...] = down_f[...].T.astype(BF16)

    for j in range(COLS // 2):
        part = pl.ds(j * 2 * LAT, 2 * LAT)
        branch = dot(down_t[...], act[:, part])[0:C]
        centre = jnp.concatenate([xs[HALO + 2 * j], xs[HALO + 2 * j + 1]], axis=1)
        bo[0:C, part] = (centre + branch).astype(BF16)
    for j in range(COLS // 2):
        part = pl.ds(j * 2 * LAT, 2 * LAT)
        predicted = dot(head_t[0:VP, :], bo[:, part])
        for h in range(2):
            i = 2 * j + h
            ocean = land[i : i + 1, :].astype(F32)
            wanted = f32b[pl.ds(i, VP, stride=COLS), :]
            miss = (predicted[:, h * LAT : (h + 1) * LAT] - wanted) * ocean
            mis[:, i * LAT : (i + 1) * LAT] = miss.astype(BF16)
            sq[0:VP, :] = sq[0:VP, :] + miss * miss

    lanes = lax.broadcasted_iota(jnp.int32, (1, LAT), 1)
    ocean_local = jnp.sum(land[...].astype(F32))
    mine = jnp.sum(sq[...].T, axis=0, keepdims=True)
    sa[idx_p] = jnp.where(lanes == V, ocean_local, mine)
    stage(0, 32, peer_p, lambda j: sa.at[idx_p], sa.at[idx_p])

    nhp[...] = dot(to_padded, nh[...]).astype(BF16)
    small[:, 128:256] = jnp.zeros((CP, 128), F32)
    small[:, 128 : 128 + VP] = dot_nt(bo[...], mis[...])

    stage_wait(0, 32, sa)
    total = sa[0]
    for j in range(1, 32):
        total = total + sa[j]
    sb[z] = total
    stage(1, 8, peer_z, lambda j: sb.at[z], sb.at[z])
    stage_wait(1, 8, sb)
    total = sb[0]
    for j in range(1, 8):
        total = total + sb[j]
    ocean_count = jnp.sum(jnp.where(lanes == V, total, 0.0), axis=1, keepdims=True)
    valid = lanes < V
    threshold = limits[...]
    mean_error = jnp.where(valid, total, 0.0) / ocean_count
    ratio = 1.0 + mean_error / threshold
    o_loss[...] = jnp.sum(jnp.where(valid, threshold * jnp.log(ratio), 0.0), axis=1, keepdims=True)
    stores[5].start()
    factor = jnp.where(valid, 2.0 / (ocean_count * ratio), 0.0)

    small[:, 128:256] = small[:, 128:256] * factor
    scaled = (head_w[...] * factor).astype(BF16)
    for j in range(COLS // 2):
        part = pl.ds(j * 2 * LAT, 2 * LAT)
        grad = dot(scaled[:, 0:VP], mis[:, part])
        bg[:, part] = grad[0:C]
        bh[:, part] = grad.astype(BF16)
    gdn[FF : FF + 64, :] = jnp.zeros((64, CP), F32)
    for f in range(0, FF, FB):
        gdn[f : f + FB, :] = dot_nt(act[f : f + FB, :], bh[...])
    for d in range(4):
        for s in range(4):
            piece = (d % 2) * 16 + (d // 2) * 8 + s * 2
            block = gdn[C * d + 64 * s : C * d + 64 * s + 64, :]
            ld[piece] = block[:, 0:128].astype(BF16)
            ld[piece + 1] = block[:, 128:256].astype(BF16)
    away = pl.ds((1 - core) * 16, 16)
    copy_d = remote(ld.at[away], rd0, send_s.at[2], recv_s.at[2], sibling)
    copy_d.start()

    pre[FF:FP, :] = jnp.zeros((FP - FF, CELLS), BF16)
    for j in range(COLS // 2):
        part = pl.ds(j * 2 * LAT, 2 * LAT)
        for f in range(0, FF, FB):
            pre[f : f + FB, part] = (
                dot(down_w[f : f + FB, :], bh[:, part]) * slope[f : f + FB, part]
            ).astype(BF16)
    gup[...] = dot_nt(nhp[...], pre[...])
    for d in range(4):
        for s in range(4):
            piece = (d % 2) * 16 + (d // 2) * 8 + s * 2
            for l in range(7):
                lu[piece + l // 4, 16 * (l % 4) : 16 * (l % 4) + 16, :] = gup[
                    64 * d + 16 * s : 64 * d + 16 * s + 16, 128 * l : 128 * l + 128
                ].astype(BF16)
            lu[piece + 1, 48:64, :] = jnp.zeros((16, 128), BF16)
    copy_u = remote(lu.at[away], ru0, send_s.at[3], recv_s.at[3], sibling)
    copy_u.start()

    for j in range(COLS // 2):
        part = pl.ds(j * 2 * LAT, 2 * LAT)
        grad = dot(up_w[...], pre[:, part])[0:C]
        for h in range(2):
            i = 2 * j + h
            g = grad[:, h * LAT : (h + 1) * LAT]
            normed = ms[i]
            mean_g = jnp.mean(g, axis=0, keepdims=True)
            mean_gn = jnp.mean(g * normed, axis=0, keepdims=True)
            ms[i] = (rstds[i] * (g - mean_g - normed * mean_gn)).astype(BF16).astype(F32)

    copy_d.wait_recv()
    for j in range(16):
        ls_d[j] = (ld[core * 16 + j].astype(F32) + rd0[j].astype(F32)).astype(BF16)
    stage(4, 16, peer_m, lambda j: ls_d.at[j], rx_d.at[idx_m])
    def conv_backward(block, carry):
        here = pl.ds(pl.multiple_of(block * 8, 8), 8)
        x = [xs[s, here, :] for s in range(SLOTS)]
        m = [ms[i, here, :] for i in range(COLS)]
        out = [None] * SLOTS
        for q in range(SIDE):
            b = (q - 3) * 2
            if b != 0:
                shifted = [jnp.where(keep[-b], pltpu.roll(t, b % LAT, 1), 0.0) for t in m]
            else:
                shifted = m
            for p in range(SIDE):
                t = p * SIDE + q
                w = taps[t, here, :]
                corr = None
                for i in range(COLS):
                    s = i + 2 * p
                    term = w * shifted[i]
                    out[s] = term if out[s] is None else out[s] + term
                    prod = shifted[i] * x[s]
                    corr = prod if corr is None else corr + prod
                corrs[t, here, :] = corr
        for s in range(SLOTS):
            back[s, here, :] = out[s]
        return carry

    lax.fori_loop(0, 3, conv_backward, 0)
    copy_u.wait_recv()
    for j in range(16):
        ls_u[j] = (lu[core * 16 + j].astype(F32) + ru0[j].astype(F32)).astype(BF16)
    stage(11, 16, peer_m, lambda j: ls_u.at[j], rx_u.at[idx_m])
    lax.fori_loop(3, C // 8, conv_backward, 0)
    stage_wait(4, 16, rx_d)
    rx_d[idx_m] = ls_d[idx_m]
    large = rx_d[0].astype(F32)
    for j in range(1, 16):
        large = large + rx_d[j].astype(F32)
    part_large[z, 0:64] = large.astype(BF16)
    stage_wait(11, 16, rx_u)
    rx_u[idx_m] = ls_u[idx_m]
    large = rx_u[0].astype(F32)
    for j in range(1, 16):
        large = large + rx_u[j].astype(F32)
    part_large[z, 64:128] = large.astype(BF16)
    stage(5, 8, peer_z, lambda j: part_large.at[z], part_large.at[z])
    tap_col = lax.broadcasted_iota(jnp.int32, (2 * LAT, LAT), 1)
    lower_half = (lax.broadcasted_iota(jnp.int32, (2 * LAT, LAT), 0) >= LAT).astype(jnp.int32)
    kern = None
    for t in range(0, SIDE * SIDE, 2):
        place = jnp.where(tap_col == V + t + lower_half, 1.0, 0.0).astype(BF16)
        terms = corrs[t].astype(BF16)
        if t + 1 < SIDE * SIDE:
            terms = jnp.concatenate([terms, corrs[t + 1].astype(BF16)], axis=1)
        else:
            place = place[0:LAT]
        part_sum = dot(terms, place)
        kern = part_sum if kern is None else kern + part_sum
    small[0:C, 128:256] = small[0:C, 128:256] + kern

    sh[C:CP, :] = jnp.zeros((CP - C, SLOTS * LAT), BF16)
    for s in range(SLOTS):
        value = back[s]
        if HALO <= s < HALO + COLS:
            value = value + bg[:, (s - HALO) * LAT : (s - HALO + 1) * LAT]
        sh[0:C, s * LAT : (s + 1) * LAT] = value.astype(BF16)
    small[:, 0:128] = jnp.zeros((CP, 128), F32)
    small[:, 0:VP] = dot_nt(sh[...], fm[...])
    smp[...] = dot(to_padded, small[...].astype(BF16)).astype(BF16)
    for d in range(4):
        for s in range(4):
            at = 64 * d + 16 * s
            stx[s * 4 + d] = smp[at : at + 16, 0:128]
            stx[16 + s * 4 + d] = smp[at : at + 16, 128:256]
    stage(6, 32, peer_p, lambda j: stx.at[j], srx.at[idx_p])

    for s in list(range(0, HALO, 2)) + list(range(HALO + COLS, SLOTS, 2)):
        value = dot(stem_t[0:VP, :], sh[:, s * LAT : (s + 2) * LAT]).astype(BF16)
        sen[s if s < HALO else s - COLS] = value[:, 0:LAT]
        sen[s + 1 if s < HALO else s + 1 - COLS] = value[:, LAT : 2 * LAT]
    copy_l = remote(sen.at[pl.ds(0, 6)], hr, send_h.at[2], recv_h.at[2], left)
    copy_r = remote(sen.at[pl.ds(6, 6)], hl, send_h.at[3], recv_h.at[3], right)
    copy_l.start()
    copy_r.start()

    for j in range(COLS // 2):
        s = HALO + 2 * j
        value = dot(stem_t[0:VP, :], sh[:, s * LAT : (s + 2) * LAT])
        cells[2 * j] = value[:, 0:LAT]
        cells[2 * j + 1] = value[:, LAT : 2 * LAT]

    stage_wait(6, 32, srx)
    srx[idx_p] = stx[idx_p]
    tiny = srx[0].astype(F32)
    for j in range(1, 32):
        tiny = tiny + srx[j].astype(F32)
    s2x[z] = tiny.astype(BF16)
    stage(8, 8, peer_z, lambda j: s2x.at[z], s2x.at[z])

    stage_wait(5, 8, part_large)
    large = part_large[0].astype(F32)
    for j in range(1, 8):
        large = large + part_large[j].astype(F32)
    lg[idx_h] = large.astype(BF16)
    stage(9, 8, peer_h, lambda j: lg.at[idx_h], lg.at[idx_h])

    stage_wait(8, 8, s2x)
    tiny = s2x[0].astype(F32)
    for j in range(1, 8):
        tiny = tiny + s2x[j].astype(F32)
    sfin[idx_h] = tiny.astype(BF16)
    stage(10, 8, peer_h, lambda j: sfin.at[idx_h], sfin.at[idx_h])

    copy_l.wait_recv()
    copy_r.wait_recv()
    for i in range(COLS):
        value = cells[i]
        if i >= 2:
            value = value + hr[i - 2].astype(F32)
        if i < 6:
            value = value + hl[i].astype(F32)
        o_sens[pl.ds(i, V, stride=COLS), :] = (value * ocean_count)[0:V]
    stores[6].start()

    stage_wait(9, 8, lg)
    for s in range(4):
        rows = 16 if s < 3 else 2
        for l in range(7):
            width = min(128, FF - 128 * l)
            at = 64 + 16 * (l % 4)
            piece = lg[s + 4 * (l // 4), at : at + 16, :].astype(F32)
            o_up[16 * s : 16 * s + rows, 128 * l : 128 * l + width] = piece[0:rows, 0:width]
        rows = 64 if s < 3 else 8
        o_down[64 * s : 64 * s + rows, 0:128] = lg[s, 0:64, :].astype(F32)[0:rows]
        o_down[64 * s : 64 * s + rows, 128:C] = lg[s + 4, 0:64, :].astype(F32)[0:rows, 0 : C - 128]
    stores[2].start()
    stores[3].start()
    stage_wait(10, 8, sfin)
    for s in range(4):
        rows = 16 if s < 3 else 2
        o_stem[16 * s : 16 * s + rows, :] = sfin[s].astype(F32)[0:rows, 0:V]
        piece = sfin[4 + s].astype(F32)
        o_head[16 * s : 16 * s + rows, :] = piece[0:rows, 0:V]
        o_kern[16 * s : 16 * s + rows, :] = pltpu.roll(piece, LAT - V, 1)[0:rows, 0:49]
    for n in (0, 1, 4):
        stores[n].start()
    for copy in first_weights + halo + list(large_weights[0] + large_weights[1]):
        copy.wait_send()
    for copy in [copy_d, copy_u, copy_l, copy_r] + pending:
        copy.wait_send()
    for copy in stores:
        copy.wait()


def hand_over(*refs):
    ins, outs, held, sems = refs[:7], refs[7:14], refs[14:21], refs[21]
    into = [pltpu.make_async_copy(ins[n], held[n], sems.at[n]) for n in range(7)]
    away = [pltpu.make_async_copy(held[n], outs[n], sems.at[7 + n]) for n in range(7)]
    for copy in into:
        copy.start()
    for n in range(7):
        into[n].wait()
        away[n].start()
    for copy in away:
        copy.wait()


SCRATCH = [
    ((V, COLS, LAT), BF16),
    ((V, COLS, LAT), BF16),
    ((COLS, LAT), jnp.int32),
    ((1, V), jnp.int32),
    ((50, V), BF16),
    ((50, SIDE * SIDE), BF16),
    ((50, FF), BF16),
    ((C, C), BF16),
    ((50, V), BF16),
    ((50, V), F32),
    ((50, SIDE * SIDE), F32),
    ((50, FF), F32),
    ((C, C), F32),
    ((50, V), F32),
    ((1, 1), F32),
    ((V * COLS, LAT), F32),
    ((VP * COLS, LAT), F32),
    ((VP * COLS, LAT), F32),
    ((SLOTS, VP, LAT), BF16),
    ((VP, SLOTS * LAT), BF16),
    ((64, 256 + FP + 128), F32),
    ((208, CP), F32),
    ((4, 64, 256), BF16),
    ((4, 64, FP + 128), BF16),
    ((4, 208, CP), BF16),
    ((CP, 128), BF16),
    ((128, CP), BF16),
    ((CP, FP), BF16),
    ((FP, CP), BF16),
    ((CP, 128), F32),
    ((128, CP), BF16),
    ((FF, CP), BF16),
    ((CP, FF), BF16),
    ((FF, CP), F32),
    ((SIDE * SIDE, C, LAT), F32),
    ((SIDE * SIDE, C, LAT), F32),
    ((SLOTS, C, LAT), F32),
    ((COLS, C, LAT), F32),
    ((CP, CELLS), BF16),
    ((CP, CELLS), BF16),
    ((FF, CELLS), BF16),
    ((FF, CELLS), F32),
    ((FP, CELLS), BF16),
    ((CP, CELLS), BF16),
    ((VP, CELLS), BF16),
    ((1, LAT), F32),
    ((128, LAT), F32),
    ((32, 1, LAT), F32),
    ((8, 1, LAT), F32),
    ((C, CELLS), F32),
    ((CP, CELLS), BF16),
    ((FF + 64, CP), F32),
    ((CP, FP), F32),
    ((SLOTS, C, LAT), F32),
    ((CP, SLOTS * LAT), BF16),
    ((CP, 256), F32),
    ((CP, 256), BF16),
    ((32, 64, 128), BF16),
    ((32, 64, 128), BF16),
    ((16, 64, 128), BF16),
    ((16, 64, 128), BF16),
    ((16, 64, 128), BF16),
    ((16, 64, 128), BF16),
    ((16, 64, 128), BF16),
    ((16, 64, 128), BF16),
    ((8, 128, 128), BF16),
    ((8, 128, 128), BF16),
    ((32, 16, 128), BF16),
    ((32, 16, 128), BF16),
    ((8, 16, 128), BF16),
    ((8, 16, 128), BF16),
    ((12, VP, LAT), BF16),
    ((6, VP, LAT), BF16),
    ((6, VP, LAT), BF16),
    ((COLS, VP, LAT), F32),
]


def shards(
    fields, targets, land_sea, clip_level, stem_weight, dw_kernel, up_weight, down_weight, head_weight
):
    anywhere = pl.BlockSpec(memory_space=pl.ANY)
    dma = pltpu.SemaphoreType.DMA
    shapes = [(50, V), (50, 49), (50, FF), (C, C), (50, V), (1, 1), (V * COLS, LAT)]
    results = [jax.ShapeDtypeStruct(s, F32) for s in shapes]
    made = pl.pallas_call(
        body,
        out_shape=results,
        in_specs=[anywhere] * 9,
        out_specs=[anywhere] * 7,
        scratch_shapes=[pltpu.VMEM(s, t) for s, t in SCRATCH]
        + [dma((n,)) for n in (9, 9, 4, 4, 12, 12, 9, 7)],
        compiler_params=pltpu.CompilerParams(
            collective_id=0, has_side_effects=True, vmem_limit_bytes=58 * 1024 * 1024
        ),
    )(
        fields.reshape(V, COLS, LAT),
        targets.reshape(V, COLS, LAT),
        land_sea,
        clip_level.reshape(1, V),
        stem_weight,
        dw_kernel,
        up_weight,
        down_weight,
        head_weight,
    )
    outs = pl.pallas_call(
        hand_over,
        out_shape=results,
        in_specs=[anywhere] * 7,
        out_specs=[anywhere] * 7,
        scratch_shapes=[pltpu.VMEM(s, F32) for s in shapes] + [dma((14,))],
    )(*made)
    return (
        outs[0], outs[1], outs[2], outs[3], outs[4],
        outs[5].reshape(()),
        outs[6].reshape(1, V, COLS, LAT),
    )


def solution(mesh):
    placed = (
        P("dp", None, "lon", None),
        P("dp", None, "lon", None),
        P("lon", None),
        P(),
        P("dp", None),
        P("dp", None),
        P("dp", None),
        P("dp", None),
        P("dp", None),
    )
    return jax.shard_map(
        shards,
        mesh=mesh,
        in_specs=placed,
        out_specs=(
            P("dp", None),
            P("dp", None),
            P("dp", None),
            P("dp", None),
            P("dp", None),
            P(),
            P("dp", None, "lon", None),
        ),
        check_vma=False,
    )
```

```python
import jax
import jax.numpy as jnp
from jax import lax
from jax.experimental import pallas as pl
from jax.experimental.pallas import tpu as pltpu
from jax.sharding import PartitionSpec as P

MESH = pl.DeviceIdType.MESH
F32 = jnp.float32
BF16 = jnp.bfloat16

V = 77
VP = 80
C = 200
CP = 256
FF = 800
FP = 896
FB = 160
COLS = 8
LAT = 128
SIDE = 7
HALO = 6
SLOTS = COLS + 2 * HALO
CELLS = COLS * LAT
GELU_K = 0.7978845608


def dot(a, b):
    return jnp.dot(a, b, preferred_element_type=F32)


def dot_nt(a, b):
    return lax.dot_general(a, b, (((1,), (1,)), ((), ())), preferred_element_type=F32)


def remote(src, dst, send, recv, device):
    return pltpu.make_async_remote_copy(
        src_ref=src,
        dst_ref=dst,
        send_sem=send,
        recv_sem=recv,
        device_id=device,
        device_id_type=MESH,
    )


def padded_row(channel):
    step = (channel >= 50).astype(jnp.int32)
    step += (channel >= 100).astype(jnp.int32)
    step += (channel >= 150).astype(jnp.int32)
    return channel + 14 * step


def body(*refs):
    inputs, made, rest = refs[:9], refs[9:16], refs[16:]
    held = rest[:9]
    o_stem, o_kern, o_up, o_down, o_head, o_loss, o_sens = made
    fields, targets, land, clip, stem, dw, up, down, head = held
    (
    f32a, f32b, fbuf, fm, wp, wd, ga, gb, gd,
        stem_w, stem_t, up_w, up_t, head_w, head_s, head_t, down_w, down_t, down_f,
        taps, corrs, xs, ms, nh, nhp, act, slope, pre, bo, mis, limits, sq, sa, sb,
        bg, bh, gdn, gup, back, sh, small, dsum,
        ld, lu, rd0, ru0, ls_d, ls_u, rx_d, rx_u, s2, rx2, fin, lg,
        stx, srx, s2x, sfin, sen, hl, hr, cells,
        send_g, recv_g, send_h, recv_h, send_s, recv_s, load_sem,
    ) = rest[9:]
    lon = lax.axis_index("lon")
    dp = lax.axis_index("dp")
    x_hi, y, z = lon // 32, (lon // 8) % 4, lon % 8
    x_lo, core = dp // 2, dp % 2
    right = ((lon + 1) % 64, dp)
    left = ((lon + 63) % 64, dp)
    sibling = (lon, x_lo * 2 + (1 - core))
    idx_p = (x_hi * 4 + y) * 4 + dp
    idx_m = (x_lo * 4 + y) * 2 + x_hi
    idx_h = x_hi * 4 + y
    idx_e = x_hi * 4 + dp

    def peer_p(k):
        j = (idx_p + k) % 32
        return j, ((j // 4) * 8 + z, j % 4)

    def peer_e(k):
        j = (idx_e + k) % 8
        return j, ((j // 4) * 32 + y * 8 + z, j % 4)

    def peer_z(k):
        j = (z + k) % 8
        return j, (x_hi * 32 + y * 8 + j, dp)

    def peer_m(k):
        j = (idx_m + k) % 16
        return j, ((j % 2) * 32 + ((j // 2) % 4) * 8 + z, (j // 8) * 2 + core)

    def peer_h(k):
        j = (idx_h + k) % 8
        return j, (j * 8 + z, dp)

    loads = [
        pltpu.make_async_copy(src, dst, load_sem.at[n])
        for n, (src, dst) in enumerate(zip(inputs, held))
    ]
    for copy in loads:
        copy.start()
    barrier = pltpu.get_barrier_semaphore()
    for target in (right, left):
        pl.semaphore_signal(barrier, inc=1, device_id=target, device_id_type=MESH)
    for k in range(1, 32):
        pl.semaphore_signal(barrier, inc=1, device_id=peer_p(k)[1], device_id_type=MESH)
    for k in range(1, 8):
        pl.semaphore_signal(barrier, inc=1, device_id=peer_z(k)[1], device_id_type=MESH)

    for copy in loads:
        copy.wait()
    f32a[0 : V * COLS, :] = fields[...].astype(F32).reshape(V * COLS, LAT)
    f32a[V * COLS : VP * COLS, :] = jnp.zeros(((VP - V) * COLS, LAT), F32)
    f32b[0 : V * COLS, :] = targets[...].astype(F32).reshape(V * COLS, LAT)
    f32b[V * COLS : VP * COLS, :] = jnp.zeros(((VP - V) * COLS, LAT), F32)
    for i in range(COLS):
        fbuf[HALO + i] = f32a[pl.ds(i, VP, stride=COLS), :].astype(BF16)
    wp[...] = jnp.zeros(wp.shape, F32)
    wp[0:50, 0:V] = stem[...].astype(F32)
    wp[0:50, 128:177] = dw[...].astype(F32)
    wp[0:50, 256 : 256 + FF] = up[...].astype(F32)
    wp[0:50, 256 + FP : 256 + FP + V] = head[...].astype(F32)
    wd[...] = jnp.zeros(wd.shape, F32)
    wd[0:C, 0:C] = down[...].astype(F32)
    ga[dp] = (wp[:, 0:128] + pltpu.roll(wp[:, 128:256], V, 1)).astype(BF16)
    gb[dp] = wp[:, 256 : 256 + FP + 128].astype(BF16)
    gd[dp] = wd[...].astype(BF16)

    pl.semaphore_wait(barrier, 40)

    halo = [
        remote(fbuf.at[pl.ds(8, 6)], fbuf.at[pl.ds(0, 6)], send_h.at[0], recv_h.at[0], right),
        remote(fbuf.at[pl.ds(6, 6)], fbuf.at[pl.ds(14, 6)], send_h.at[1], recv_h.at[1], left),
    ]
    first_weights = [
        remote(ga.at[dp], ga.at[dp], send_g.at[k - 1], recv_g.at[k - 1], (lon, (dp + k) % 4))
        for k in range(1, 4)
    ]
    for copy in first_weights:
        copy.start()
    across = (lon, (1 - x_lo) * 2 + core)
    far = (1 - x_lo) * 2 + core
    large_weights = []
    for a, buf in enumerate((gb, gd)):
        at = 3 + 3 * a
        large_weights.append(
            (
                remote(buf.at[dp], buf.at[dp], send_g.at[at], recv_g.at[at], across),
                remote(buf.at[dp], buf.at[dp], send_g.at[at + 1], recv_g.at[at + 1], sibling),
                remote(buf.at[far], buf.at[far], send_g.at[at + 2], recv_g.at[at + 2], sibling),
            )
        )

    def pass_on(a):
        large_weights[a][0].wait_recv()
        large_weights[a][2].start()

    pending = []

    def stage(index, count, peers, src, dst):
        for k in range(1, count):
            j, device = peers(k)
            remote(src(j), dst, send_s.at[index], recv_s.at[index], device).start()

    def stage_wait(index, count, buf):
        whole = buf.at[pl.ds(0, count - 1)]
        both = remote(whole, whole, send_s.at[index], recv_s.at[index], right)
        both.wait_recv()
        pending.append(both)

    row = lax.broadcasted_iota(jnp.int32, (CP, CP), 0)
    col = lax.broadcasted_iota(jnp.int32, (CP, CP), 1)
    from_padded = jnp.where((row < C) & (col == padded_row(row)), 1.0, 0.0).astype(BF16)
    to_padded = jnp.where((col < C) & (row == padded_row(col)), 1.0, 0.0).astype(BF16)
    lane = lax.broadcasted_iota(jnp.int32, (8, LAT), 1)
    keep = {b: (lane + b >= 0) & (lane + b < LAT) for b in range(-HALO, HALO + 1, 2)}

    for i in range(COLS):
        fm[:, (HALO + i) * LAT : (HALO + i + 1) * LAT] = fbuf[HALO + i]

    for copy in halo:
        copy.start()
    for copy in first_weights:
        copy.wait_recv()
    large_weights[0][0].start()
    large_weights[0][1].start()
    large_weights[1][1].start()
    stem_w[...] = dot(from_padded, ga[...].reshape(CP, 128)).astype(BF16)
    def stem_pair(s):
        out = dot(stem_w[:, 0:VP], fm[:, s * LAT : (s + 2) * LAT])[0:C].astype(BF16).astype(F32)
        xs[s] = out[:, 0:LAT]
        xs[s + 1] = out[:, LAT : 2 * LAT]

    for s in range(HALO, HALO + COLS, 2):
        stem_pair(s)
    kern_w = stem_w[0:208, :]
    tap_row = lax.broadcasted_iota(jnp.int32, (LAT, 2 * LAT), 0)
    second_half = (lax.broadcasted_iota(jnp.int32, (LAT, 2 * LAT), 1) >= LAT).astype(jnp.int32)
    for t in range(0, SIDE * SIDE, 2):
        spread = dot(kern_w, jnp.where(tap_row == V + t + second_half, 1.0, 0.0).astype(BF16))[0:C]
        taps[t] = spread[:, 0:LAT]
        if t + 1 < SIDE * SIDE:
            taps[t + 1] = spread[:, LAT : 2 * LAT]
    for copy in halo:
        copy.wait_recv()
    for s in list(range(0, HALO)) + list(range(HALO + COLS, SLOTS)):
        fm[:, s * LAT : (s + 1) * LAT] = fbuf[s]
    for s in list(range(0, HALO, 2)) + list(range(HALO + COLS, SLOTS, 2)):
        stem_pair(s)

    large_weights[1][0].start()
    def conv_forward(block, carry):
        here = pl.ds(pl.multiple_of(block * 8, 8), 8)
        for first_col in (0, 4):
            x = [xs[first_col + s, here, :] for s in range(4 + 2 * HALO)]
            out = [None] * 4
            for q in range(SIDE):
                b = (q - 3) * 2
                w = [taps[p * SIDE + q, here, :] for p in range(SIDE)]
                for i in range(4):
                    total = w[0] * x[i]
                    for p in range(1, SIDE):
                        total = total + w[p] * x[i + 2 * p]
                    if b != 0:
                        total = jnp.where(keep[b], pltpu.roll(total, (-b) % LAT, 1), 0.0)
                    out[i] = total if out[i] is None else out[i] + total
            for i in range(4):
                ms[first_col + i, here, :] = out[i]
        return carry

    lax.fori_loop(0, 13, conv_forward, 0)
    pass_on(0)
    lax.fori_loop(13, C // 8, conv_forward, 0)

    pass_on(1)
    nh[...] = jnp.zeros(nh.shape, BF16)
    rstds = []
    for i in range(COLS):
        tile = ms[i]
        centred = tile - jnp.mean(tile, axis=0, keepdims=True)
        rstd = lax.rsqrt(jnp.mean(centred * centred, axis=0, keepdims=True) + 1e-06)
        normed = centred * rstd
        ms[i] = normed
        rstds.append(rstd)
        nh[0:C, i * LAT : (i + 1) * LAT] = normed.astype(BF16)

    large_weights[0][1].wait_recv()
    large_weights[0][2].wait_recv()
    second = dot(from_padded, gb[...].reshape(CP, FP + 128))
    up_w[...] = second[:, 0:FP].astype(BF16)
    up_t[...] = second[:, 0:FP].T.astype(BF16)
    head_w[...] = second[:, FP : FP + 128]
    head_t[...] = second[:, FP : FP + 128].T.astype(BF16)
    limits[...] = jnp.ones((1, LAT), F32)
    limits[:, 0:V] = clip[...].astype(F32) / 16.0
    sq[...] = jnp.zeros(sq.shape, F32)
    bo[...] = jnp.zeros(bo.shape, BF16)
    for j in range(0, 2):
        part = pl.ds(j * 2 * LAT, 2 * LAT)
        for f in range(0, FF, FB):
            u = dot(up_t[f : f + FB, :], nh[:, part])
            u2 = u * u
            half = 0.5 + 0.5 * jnp.tanh(u * (GELU_K + (GELU_K * 0.044715) * u2))
            value = u * half
            act[f : f + FB, part] = value.astype(BF16)
            slope[f : f + FB, part] = half + value * (1.0 - half) * (
                2.0 * GELU_K + (6.0 * GELU_K * 0.044715) * u2
            )
    for j in range(2, 4):
        part = pl.ds(j * 2 * LAT, 2 * LAT)
        for f in range(0, FF, FB):
            u = dot(up_t[f : f + FB, :], nh[:, part])
            u2 = u * u
            half = 0.5 + 0.5 * jnp.tanh(u * (GELU_K + (GELU_K * 0.044715) * u2))
            value = u * half
            act[f : f + FB, part] = value.astype(BF16)
            slope[f : f + FB, part] = half + value * (1.0 - half) * (
                2.0 * GELU_K + (6.0 * GELU_K * 0.044715) * u2
            )
    large_weights[1][1].wait_recv()
    large_weights[1][2].wait_recv()
    for d in range(4):
        down_f[C * d : C * (d + 1), :] = gd[d].astype(F32)[0:C]
    down_w[...] = down_f[...].astype(BF16)
    down_t[...] = down_f[...].T.astype(BF16)

    for j in range(COLS // 2):
        part = pl.ds(j * 2 * LAT, 2 * LAT)
        branch = dot(down_t[...], act[:, part])[0:C]
        centre = jnp.concatenate([xs[HALO + 2 * j], xs[HALO + 2 * j + 1]], axis=1)
        bo[0:C, part] = (centre + branch).astype(BF16)
    for j in range(COLS // 2):
        part = pl.ds(j * 2 * LAT, 2 * LAT)
        predicted = dot(head_t[0:VP, :], bo[:, part])
        for h in range(2):
            i = 2 * j + h
            ocean = land[i : i + 1, :].astype(F32)
            wanted = f32b[pl.ds(i, VP, stride=COLS), :]
            miss = (predicted[:, h * LAT : (h + 1) * LAT] - wanted) * ocean
            mis[:, i * LAT : (i + 1) * LAT] = miss.astype(BF16)
            sq[0:VP, :] = sq[0:VP, :] + miss * miss

    lanes = lax.broadcasted_iota(jnp.int32, (1, LAT), 1)
    ocean_local = jnp.sum(land[...].astype(F32))
    mine = jnp.sum(sq[...].T, axis=0, keepdims=True)
    sa[idx_p] = jnp.where(lanes == V, ocean_local, mine)
    stage(0, 32, peer_p, lambda j: sa.at[idx_p], sa.at[idx_p])

    gdn[...] = jnp.zeros(gdn.shape, F32)
    own_down = dot_nt(act[...], mis[...])
    for d in range(4):
        gdn[CP * d : CP * d + C, 0:VP] = own_down[C * d : C * d + C]
    own_head = dot_nt(bo[...], mis[...]).astype(BF16)
    own_head = dot(to_padded, own_head)
    for d in range(4):
        gdn[CP * d + C : CP * d + C + 56, 0:VP] = own_head[64 * d : 64 * d + 56]
    for d in range(4):
        for r in range(8):
            piece = (d % 2) * 16 + (d // 2) * 8 + r
            ld[piece] = gdn[CP * d + 32 * r : CP * d + 32 * r + 32, :].astype(BF16)
    away = pl.ds((1 - core) * 16, 16)
    copy_d = remote(ld.at[away], rd0, send_s.at[2], recv_s.at[2], sibling)
    copy_d.start()
    nhp[...] = dot(to_padded, nh[...]).astype(BF16)
    stem_t[...] = stem_w[...].astype(F32).T.astype(BF16)

    stage_wait(0, 32, sa)
    total = sa[0]
    for j in range(1, 32):
        total = total + sa[j]
    sb[z] = total
    stage(1, 8, peer_z, lambda j: sb.at[z], sb.at[z])
    copy_d.wait_recv()
    for j in range(16):
        ls_d[j] = (ld[core * 16 + j].astype(F32) + rd0[j].astype(F32)).astype(BF16)
    stage(4, 16, peer_m, lambda j: ls_d.at[j], rx_d.at[idx_m])
    stage_wait(1, 8, sb)
    total = sb[0]
    for j in range(1, 8):
        total = total + sb[j]
    ocean_count = jnp.sum(jnp.where(lanes == V, total, 0.0), axis=1, keepdims=True)
    valid = lanes < V
    threshold = limits[...]
    mean_error = jnp.where(valid, total, 0.0) / ocean_count
    ratio = 1.0 + mean_error / threshold
    o_loss[...] = jnp.sum(jnp.where(valid, threshold * jnp.log(ratio), 0.0), axis=1, keepdims=True)
    factor = jnp.where(valid, 2.0 / (ocean_count * ratio), 0.0)

    head_s[...] = (head_w[...] * factor).astype(BF16)
    scaled = head_s[...]
    for j in range(COLS // 2):
        part = pl.ds(j * 2 * LAT, 2 * LAT)
        grad = dot(scaled[:, 0:VP], mis[:, part])
        bg[:, part] = grad[0:C]
        bh[:, part] = grad.astype(BF16)
    pre[FF:FP, :] = jnp.zeros((FP - FF, CELLS), BF16)
    for j in range(COLS // 2):
        part = pl.ds(j * 2 * LAT, 2 * LAT)
        for f in range(0, FF, FB):
            pre[f : f + FB, part] = (
                dot(down_w[f : f + FB, :], bh[:, part]) * slope[f : f + FB, part]
            ).astype(BF16)
    gup[...] = dot_nt(nhp[...], pre[...])
    for d in range(4):
        for s in range(4):
            piece = (d % 2) * 16 + (d // 2) * 8 + s * 2
            for l in range(7):
                lu[piece + l // 4, 16 * (l % 4) : 16 * (l % 4) + 16, :] = gup[
                    64 * d + 16 * s : 64 * d + 16 * s + 16, 128 * l : 128 * l + 128
                ].astype(BF16)
            lu[piece + 1, 48:64, :] = jnp.zeros((16, 128), BF16)
    copy_u = remote(lu.at[away], ru0, send_s.at[3], recv_s.at[3], sibling)
    copy_u.start()

    for j in range(COLS // 2):
        part = pl.ds(j * 2 * LAT, 2 * LAT)
        grad = dot(up_w[...], pre[:, part])[0:C]
        for h in range(2):
            i = 2 * j + h
            g = grad[:, h * LAT : (h + 1) * LAT]
            normed = ms[i]
            mean_g = jnp.mean(g, axis=0, keepdims=True)
            mean_gn = jnp.mean(g * normed, axis=0, keepdims=True)
            ms[i] = (rstds[i] * (g - mean_g - normed * mean_gn)).astype(BF16).astype(F32)

    def conv_backward(block, carry):
        here = pl.ds(pl.multiple_of(block * 8, 8), 8)
        x = [xs[s, here, :] for s in range(SLOTS)]
        m = [ms[i, here, :] for i in range(COLS)]
        out = [None] * SLOTS
        for q in range(SIDE):
            b = (q - 3) * 2
            if b != 0:
                shifted = [jnp.where(keep[-b], pltpu.roll(t, b % LAT, 1), 0.0) for t in m]
            else:
                shifted = m
            for p in range(SIDE):
                t = p * SIDE + q
                w = taps[t, here, :]
                corr = None
                for i in range(COLS):
                    s = i + 2 * p
                    term = w * shifted[i]
                    out[s] = term if out[s] is None else out[s] + term
                    prod = shifted[i] * x[s]
                    corr = prod if corr is None else corr + prod
                corrs[t, here, :] = corr
        for s in range(SLOTS):
            back[s, here, :] = out[s]
        return carry

    lax.fori_loop(0, 3, conv_backward, 0)
    copy_u.wait_recv()
    for j in range(16):
        ls_u[j] = (lu[core * 16 + j].astype(F32) + ru0[j].astype(F32)).astype(BF16)
    stage(11, 16, peer_m, lambda j: ls_u.at[j], rx_u.at[idx_m])
    lax.fori_loop(3, C // 8, conv_backward, 0)
    tap_col = lax.broadcasted_iota(jnp.int32, (2 * LAT, LAT), 1)
    lower_half = (lax.broadcasted_iota(jnp.int32, (2 * LAT, LAT), 0) >= LAT).astype(jnp.int32)
    kern = None
    for t in range(0, SIDE * SIDE, 2):
        place = jnp.where(tap_col == V + t + lower_half, 1.0, 0.0).astype(BF16)
        terms = corrs[t].astype(BF16)
        if t + 1 < SIDE * SIDE:
            terms = jnp.concatenate([terms, corrs[t + 1].astype(BF16)], axis=1)
        else:
            place = place[0:LAT]
        part_sum = dot(terms, place)
        kern = part_sum if kern is None else kern + part_sum

    stage_wait(11, 16, rx_u)
    rx_u[idx_m] = ls_u[idx_m]
    large = rx_u[0].astype(F32)
    for j in range(1, 16):
        large = large + rx_u[j].astype(F32)
    s2[0:4] = large.astype(BF16).reshape(4, 16, 128)
    stage_wait(4, 16, rx_d)
    rx_d[idx_m] = ls_d[idx_m]
    large = rx_d[0].astype(F32)
    for j in range(1, 16):
        large = large + rx_d[j].astype(F32)
    s2[4:6] = large.astype(BF16).reshape(2, 16, 128)
    s2[6:8] = jnp.zeros((2, 16, 128), BF16)
    stage(5, 8, peer_z, lambda j: s2.at[j], rx2.at[z])
    sh[C:CP, :] = jnp.zeros((CP - C, SLOTS * LAT), BF16)
    for s in range(SLOTS):
        value = back[s]
        if HALO <= s < HALO + COLS:
            value = value + bg[:, (s - HALO) * LAT : (s - HALO + 1) * LAT]
        sh[0:C, s * LAT : (s + 1) * LAT] = value.astype(BF16)
    small[...] = jnp.zeros(small.shape, F32)
    small[:, 0:VP] = dot_nt(sh[...], fm[...])
    small[0:C, :] = small[0:C, :] + kern
    tiny = dot(to_padded, small[...].astype(BF16))
    for j in range(8):
        at = 64 * (j % 4) + 32 * (j // 4)
        stx[j] = tiny[at : at + 32].astype(BF16)
    stage(6, 8, peer_e, lambda j: stx.at[j], srx.at[idx_e])

    for s in list(range(0, HALO, 2)) + list(range(HALO + COLS, SLOTS, 2)):
        value = dot(stem_t[0:VP, :], sh[:, s * LAT : (s + 2) * LAT]).astype(BF16)
        sen[s if s < HALO else s - COLS] = value[:, 0:LAT]
        sen[s + 1 if s < HALO else s + 1 - COLS] = value[:, LAT : 2 * LAT]
    copy_l = remote(sen.at[pl.ds(0, 6)], hr, send_h.at[2], recv_h.at[2], left)
    copy_r = remote(sen.at[pl.ds(6, 6)], hl, send_h.at[3], recv_h.at[3], right)
    copy_l.start()
    copy_r.start()

    for j in range(COLS // 2):
        s = HALO + 2 * j
        value = dot(stem_t[0:VP, :], sh[:, s * LAT : (s + 2) * LAT])
        cells[2 * j] = value[:, 0:LAT]
        cells[2 * j + 1] = value[:, LAT : 2 * LAT]

    stage_wait(5, 8, rx2)
    rx2[z] = s2[z]
    part_sum = rx2[0].astype(F32)
    for j in range(1, 8):
        part_sum = part_sum + rx2[j].astype(F32)
    fin[z] = part_sum.astype(BF16)
    stage(7, 8, peer_z, lambda j: fin.at[z], fin.at[z])
    stage_wait(6, 8, srx)
    srx[idx_e] = stx[idx_e]
    tiny = srx[0].astype(F32)
    for j in range(1, 8):
        tiny = tiny + srx[j].astype(F32)
    s2x[z] = tiny.astype(BF16)
    stage(8, 8, peer_z, lambda j: s2x.at[z], s2x.at[z])

    stage_wait(7, 8, fin)
    lg[idx_h] = fin[0:6].reshape(96, 128)
    stage(9, 8, peer_h, lambda j: lg.at[idx_h], lg.at[idx_h])

    stage_wait(8, 8, s2x)
    tiny = s2x[0].astype(F32)
    for j in range(1, 8):
        tiny = tiny + s2x[j].astype(F32)
    sfin[idx_h] = tiny.astype(BF16)
    stage(10, 8, peer_h, lambda j: sfin.at[idx_h], sfin.at[idx_h])

    copy_l.wait_recv()
    copy_r.wait_recv()
    for i in range(COLS):
        value = cells[i]
        if i >= 2:
            value = value + hr[i - 2].astype(F32)
        if i < 6:
            value = value + hl[i].astype(F32)
        o_sens[pl.ds(i, V, stride=COLS), :] = (value * ocean_count)[0:V]

    stage_wait(9, 8, lg)
    for s in range(4):
        rows = 16 if s < 3 else 2
        for l in range(7):
            width = min(128, FF - 128 * l)
            at = 16 * (l % 4)
            piece = lg[s + 4 * (l // 4), at : at + 16, :].astype(F32)
            o_up[16 * s : 16 * s + rows, 128 * l : 128 * l + width] = piece[0:rows, 0:width]
    for r in range(8):
        dsum[32 * r : 32 * r + 32, :] = lg[(r % 2) * 4 + r // 2, 64:96, :]
    o_down[...] = dot_nt(dsum[...], head_s[...])[0:C, 0:C]
    o_head[...] = (dsum[...].astype(F32)[C : C + 50] * factor)[:, 0:V]
    stage_wait(10, 8, sfin)
    for h, rows in ((0, 32), (1, 18)):
        tiny = sfin[4 * h].astype(F32)
        for j in range(1, 4):
            tiny = tiny + sfin[4 * h + j].astype(F32)
        o_stem[32 * h : 32 * h + rows, :] = tiny[0:rows, 0:V]
        o_kern[32 * h : 32 * h + rows, :] = pltpu.roll(tiny, LAT - V, 1)[0:rows, 0:49]
    for copy in first_weights + halo + list(large_weights[0] + large_weights[1]):
        copy.wait_send()
    for copy in [copy_d, copy_u, copy_l, copy_r] + pending:
        copy.wait_send()


def hand_over(*refs):
    copies = [pltpu.make_async_copy(refs[n], refs[7 + n], refs[14].at[n]) for n in range(7)]
    for copy in copies:
        copy.start()
    for copy in copies:
        copy.wait()


SCRATCH = [
    ((V, COLS, LAT), BF16),
    ((V, COLS, LAT), BF16),
    ((COLS, LAT), jnp.int32),
    ((1, V), jnp.int32),
    ((50, V), BF16),
    ((50, SIDE * SIDE), BF16),
    ((50, FF), BF16),
    ((C, C), BF16),
    ((50, V), BF16),
    ((VP * COLS, LAT), F32),
    ((VP * COLS, LAT), F32),
    ((SLOTS, VP, LAT), BF16),
    ((VP, SLOTS * LAT), BF16),
    ((64, 256 + FP + 128), F32),
    ((208, CP), F32),
    ((4, 64, 128), BF16),
    ((4, 64, FP + 128), BF16),
    ((4, 208, CP), BF16),
    ((CP, 128), BF16),
    ((128, CP), BF16),
    ((CP, FP), BF16),
    ((FP, CP), BF16),
    ((CP, 128), F32),
    ((CP, 128), BF16),
    ((128, CP), BF16),
    ((FF, CP), BF16),
    ((CP, FF), BF16),
    ((FF, CP), F32),
    ((SIDE * SIDE, C, LAT), F32),
    ((SIDE * SIDE, C, LAT), F32),
    ((SLOTS, C, LAT), F32),
    ((COLS, C, LAT), F32),
    ((CP, CELLS), BF16),
    ((CP, CELLS), BF16),
    ((FF, CELLS), BF16),
    ((FF, CELLS), F32),
    ((FP, CELLS), BF16),
    ((CP, CELLS), BF16),
    ((VP, CELLS), BF16),
    ((1, LAT), F32),
    ((128, LAT), F32),
    ((32, 1, LAT), F32),
    ((8, 1, LAT), F32),
    ((C, CELLS), F32),
    ((CP, CELLS), BF16),
    ((4 * CP, 128), F32),
    ((CP, FP), F32),
    ((SLOTS, C, LAT), F32),
    ((CP, SLOTS * LAT), BF16),
    ((CP, 128), F32),
    ((CP, 128), BF16),
    ((32, 32, 128), BF16),
    ((32, 64, 128), BF16),
    ((16, 32, 128), BF16),
    ((16, 64, 128), BF16),
    ((16, 32, 128), BF16),
    ((16, 64, 128), BF16),
    ((16, 32, 128), BF16),
    ((16, 64, 128), BF16),
    ((8, 16, 128), BF16),
    ((8, 16, 128), BF16),
    ((8, 16, 128), BF16),
    ((8, 96, 128), BF16),
    ((8, 32, 128), BF16),
    ((8, 32, 128), BF16),
    ((8, 32, 128), BF16),
    ((8, 32, 128), BF16),
    ((12, VP, LAT), BF16),
    ((6, VP, LAT), BF16),
    ((6, VP, LAT), BF16),
    ((COLS, VP, LAT), F32),
]


def shards(
    fields, targets, land_sea, clip_level, stem_weight, dw_kernel, up_weight, down_weight, head_weight
):
    anywhere = pl.BlockSpec(memory_space=pl.ANY)
    vmem = pl.BlockSpec(memory_space=pltpu.VMEM)
    dma = pltpu.SemaphoreType.DMA
    shapes = [(50, V), (50, 49), (50, FF), (C, C), (50, V), (1, 1), (V * COLS, LAT)]
    results = [jax.ShapeDtypeStruct(s, F32) for s in shapes]
    made = pl.pallas_call(
        body,
        out_shape=[pltpu.VMEM(s, F32) for s in shapes],
        in_specs=[anywhere] * 9,
        out_specs=[vmem] * 7,
        scratch_shapes=[pltpu.VMEM(s, t) for s, t in SCRATCH]
        + [dma((n,)) for n in (9, 9, 4, 4, 12, 12, 9)],
        compiler_params=pltpu.CompilerParams(
            collective_id=0, has_side_effects=True, vmem_limit_bytes=58 * 1024 * 1024
        ),
    )(
        fields.reshape(V, COLS, LAT),
        targets.reshape(V, COLS, LAT),
        land_sea,
        clip_level.reshape(1, V),
        stem_weight,
        dw_kernel,
        up_weight,
        down_weight,
        head_weight,
    )
    outs = pl.pallas_call(
        hand_over,
        out_shape=results,
        in_specs=[vmem] * 7,
        out_specs=[anywhere] * 7,
        scratch_shapes=[dma((7,))],
    )(*[pltpu.with_memory_space_constraint(m, pltpu.VMEM) for m in made])
    return (
        outs[0], outs[1], outs[2], outs[3], outs[4],
        outs[5].reshape(()),
        outs[6].reshape(1, V, COLS, LAT),
    )


def solution(mesh):
    placed = (
        P("dp", None, "lon", None),
        P("dp", None, "lon", None),
        P("lon", None),
        P(),
        P("dp", None),
        P("dp", None),
        P("dp", None),
        P("dp", None),
        P("dp", None),
    )
    return jax.shard_map(
        shards,
        mesh=mesh,
        in_specs=placed,
        out_specs=(
            P("dp", None),
            P("dp", None),
            P("dp", None),
            P("dp", None),
            P("dp", None),
            P(),
            P("dp", None, "lon", None),
        ),
        check_vma=False,
    )
```

```python
import itertools

import jax
import jax.numpy as jnp
from jax import lax
from jax.experimental import pallas as pl
from jax.experimental.pallas import tpu as pltpu
from jax.sharding import PartitionSpec as P

MESH = pl.DeviceIdType.MESH
F32 = jnp.float32
BF16 = jnp.bfloat16

V = 77
VP = 80
C = 200
CP = 256
FF = 800
FP = 896
FB = 400
COLS = 8
LAT = 128
SIDE = 7
HALO = 6
SLOTS = COLS + 2 * HALO
CELLS = COLS * LAT
GELU_K = 0.7978845608


def dot(a, b):
    return jnp.dot(a, b, preferred_element_type=F32)


def dot_nt(a, b):
    return lax.dot_general(a, b, (((1,), (1,)), ((), ())), preferred_element_type=F32)


def remote(src, dst, send, recv, device):
    return pltpu.make_async_remote_copy(
        src_ref=src,
        dst_ref=dst,
        send_sem=send,
        recv_sem=recv,
        device_id=device,
        device_id_type=MESH,
    )


def hops(offset):
    a, b, c, d, e = offset
    x = {(0, 0): 0, (0, 1): 1, (1, 0): 2, (1, 1): 1}[a, d]
    return x + min(b, 4 - b) + min(c, 8 - c) + 0.5 * e


def group(*sizes):
    offsets = itertools.product(*(range(n) for n in sizes))
    return sorted((o for o in offsets if any(o)), key=lambda o: -hops(o))


def padded_row(channel):
    step = (channel >= 50).astype(jnp.int32)
    step += (channel >= 100).astype(jnp.int32)
    step += (channel >= 150).astype(jnp.int32)
    return channel + 14 * step


def body(*refs):
    inputs, made, rest = refs[:9], refs[9:16], refs[16:]
    held = rest[:9]
    o_stem, o_kern, o_up, o_down, o_head, o_loss, o_sens = made
    fields, targets, land, clip, stem, dw, up, down, head = held
    (
    f32a, f32b, fbuf, fm, wp, wd, ga, gb, gd,
        stem_w, stem_t, up_w, up_t, head_w, head_s, head_t, down_w, down_t, down_f,
        taps, partial, corrs, xs, ms, nh, act, slope, pre, bo, mis, limits, sq, sa, sb,
        bg, bh, gdn, gup, flat, back, sh, small, dsum,
        ld, lu, rd0, ru0, ls_d, ls_u, rx_d, rx_u, part_u, lg_u, part_d, lg_d,
        stx, srx, s2x, sfin, sen, hl, hr, cells,
        send_g, recv_g, send_h, recv_h, send_s, recv_s, load_sem,
    ) = rest[9:]
    lon = lax.axis_index("lon")
    dp = lax.axis_index("dp")
    x_hi, y, z = lon // 32, (lon // 8) % 4, lon % 8
    x_lo, core = dp // 2, dp % 2
    right = ((lon + 1) % 64, dp)
    left = ((lon + 63) % 64, dp)
    sibling = (lon, x_lo * 2 + (1 - core))
    idx_p = (x_hi * 4 + y) * 4 + dp
    idx_m = (x_lo * 4 + y) * 2 + x_hi
    idx_h = x_hi * 4 + y
    idx_e = x_hi * 4 + dp

    busy = ((y == 3) & (z == 0)) | ((y == 0) & (z == 7))
    helper = ((y == 2) & (z == 0)) | ((y == 1) & (z == 7))
    alone, plain = jnp.logical_not(busy), jnp.logical_not(busy | helper)
    helped = (x_hi * 32 + ((y + jnp.where(z == 0, 1, 3)) % 4) * 8 + z, dp)

    def peer(offset):
        a, b, c, d, e = offset
        return (x_hi + a) % 2, (y + b) % 4, (z + c) % 8, (x_lo + d) % 2, (core + e) % 2

    def device(at):
        return at[0] * 32 + at[1] * 8 + at[2], at[3] * 2 + at[4]

    PLANE = group(2, 4, 1, 2, 2), lambda at: (at[0] * 4 + at[1]) * 4 + at[3] * 2 + at[4]
    RING = group(1, 1, 8, 1, 1), lambda at: at[2]
    CORES = group(2, 4, 1, 2, 1), lambda at: (at[3] * 4 + at[1]) * 2 + at[0]
    SHARE = group(2, 4, 1, 1, 1), lambda at: at[0] * 4 + at[1]
    ROW = group(2, 1, 1, 2, 2), lambda at: at[0] * 4 + at[3] * 2 + at[4]

    loads = [
        pltpu.make_async_copy(src, dst, load_sem.at[n])
        for n, (src, dst) in enumerate(zip(inputs, held))
    ]
    for copy in loads:
        copy.start()
    barrier = pltpu.get_barrier_semaphore()
    for offset in RING[0]:
        pl.semaphore_signal(
            barrier, inc=1, device_id=device(peer(offset)), device_id_type=MESH
        )
    for target in (right, left):
        pl.semaphore_signal(barrier, inc=1, device_id=target, device_id_type=MESH)
    for offset in PLANE[0]:
        pl.semaphore_signal(
            barrier, inc=1, device_id=device(peer(offset)), device_id_type=MESH
        )

    for copy in loads:
        copy.wait()
    f32a[0 : V * COLS, :] = fields[...].astype(F32).reshape(V * COLS, LAT)
    f32a[V * COLS : VP * COLS, :] = jnp.zeros(((VP - V) * COLS, LAT), F32)
    f32b[0 : V * COLS, :] = targets[...].astype(F32).reshape(V * COLS, LAT)
    f32b[V * COLS : VP * COLS, :] = jnp.zeros(((VP - V) * COLS, LAT), F32)
    for i in range(COLS):
        fbuf[HALO + i] = f32a[pl.ds(i, VP, stride=COLS), :].astype(BF16)
    wp[...] = jnp.zeros(wp.shape, F32)
    wp[0:50, 0:V] = stem[...].astype(F32)
    wp[0:50, 128:177] = dw[...].astype(F32)
    wp[0:50, 256 : 256 + FF] = up[...].astype(F32)
    wp[0:50, 256 + FP : 256 + FP + V] = head[...].astype(F32)
    wd[...] = jnp.zeros(wd.shape, F32)
    wd[0:C, 0:C] = down[...].astype(F32)
    ga[dp] = (wp[:, 0:128] + pltpu.roll(wp[:, 128:256], V, 1)).astype(BF16)
    gb[dp] = wp[:, 256 : 256 + FP + 128].astype(BF16)
    gd[dp] = wd[...].astype(BF16)

    pl.semaphore_wait(barrier, 40)

    halo = [
        remote(fbuf.at[pl.ds(8, 6)], fbuf.at[pl.ds(0, 6)], send_h.at[0], recv_h.at[0], right),
        remote(fbuf.at[pl.ds(6, 6)], fbuf.at[pl.ds(14, 6)], send_h.at[1], recv_h.at[1], left),
    ]
    first_weights = [
        remote(ga.at[dp], ga.at[dp], send_g.at[k - 1], recv_g.at[k - 1], (lon, (dp + k) % 4))
        for k in range(1, 4)
    ]
    for copy in first_weights:
        copy.start()
    across = (lon, (1 - x_lo) * 2 + core)
    far = (1 - x_lo) * 2 + core
    large_weights = []
    for a, buf in enumerate((gb, gd)):
        at = 3 + 3 * a
        large_weights.append(
            (
                remote(buf.at[dp], buf.at[dp], send_g.at[at], recv_g.at[at], across),
                remote(buf.at[dp], buf.at[dp], send_g.at[at + 1], recv_g.at[at + 1], sibling),
                remote(buf.at[far], buf.at[far], send_g.at[at + 2], recv_g.at[at + 2], sibling),
            )
        )

    for copy in halo:
        copy.start()
    pl.when(alone)(large_weights[0][0].start)

    help_copies = [
        remote(buf.at[far], buf.at[far], send_g.at[9 + a], recv_g.at[3 + 3 * a], helped)
        for a, buf in enumerate((gb, gd))
    ]

    def pass_on(a):
        large_weights[a][0].wait_recv()
        large_weights[a][2].start()

    def help_on(a):
        pass_on(a)
        help_copies[a].start()

    pending = []

    def stage(index, count, peers, src, dst):
        for offset in peers[0][: count - 1]:
            at = peer(offset)
            remote(
                src(peers[1](at)), dst, send_s.at[index], recv_s.at[index], device(at)
            ).start()

    def stage_wait(index, count, buf):
        whole = buf.at[pl.ds(0, count - 1)]
        both = remote(whole, whole, send_s.at[index], recv_s.at[index], right)
        both.wait_recv()
        pending.append(both)

    row = lax.broadcasted_iota(jnp.int32, (CP, CP), 0)
    col = lax.broadcasted_iota(jnp.int32, (CP, CP), 1)
    from_padded = jnp.where((row < C) & (col == padded_row(row)), 1.0, 0.0).astype(BF16)
    to_padded = jnp.where((col < C) & (row == padded_row(col)), 1.0, 0.0).astype(BF16)
    lane = lax.broadcasted_iota(jnp.int32, (8, LAT), 1)
    keep = {b: (lane + b >= 0) & (lane + b < LAT) for b in range(-HALO, HALO + 1, 2)}

    for i in range(COLS):
        fm[:, (HALO + i) * LAT : (HALO + i + 1) * LAT] = fbuf[HALO + i]

    for copy in first_weights:
        copy.wait_recv()
    large_weights[0][1].start()
    stem_w[...] = dot(from_padded, ga[...].reshape(CP, 128)).astype(BF16)
    def stem_pair(s):
        out = dot(stem_w[:, 0:VP], fm[:, s * LAT : (s + 2) * LAT])[0:C].astype(BF16).astype(F32)
        xs[s] = out[:, 0:LAT]
        xs[s + 1] = out[:, LAT : 2 * LAT]

    for s in range(HALO, HALO + COLS, 2):
        stem_pair(s)
    kern_w = stem_w[0:208, :]
    tap_row = lax.broadcasted_iota(jnp.int32, (LAT, 2 * LAT), 0)
    second_half = (lax.broadcasted_iota(jnp.int32, (LAT, 2 * LAT), 1) >= LAT).astype(jnp.int32)
    for t in range(0, SIDE * SIDE, 2):
        spread = dot(kern_w, jnp.where(tap_row == V + t + second_half, 1.0, 0.0).astype(BF16))[0:C]
        taps[t] = spread[:, 0:LAT]
        if t + 1 < SIDE * SIDE:
            taps[t + 1] = spread[:, LAT : 2 * LAT]
    def own_taps(i):
        return [p for p in range(SIDE) if HALO <= i + 2 * p < HALO + COLS]

    def conv_own(block, carry):
        here = pl.ds(pl.multiple_of(block * 8, 8), 8)
        x = {s: xs[s, here, :] for s in range(HALO, HALO + COLS)}
        for q in range(SIDE):
            w = [taps[p * SIDE + q, here, :] for p in range(SIDE)]
            for i in range(COLS):
                total = None
                for p in own_taps(i):
                    term = w[p] * x[i + 2 * p]
                    total = term if total is None else total + term
                partial[q * COLS + i, here, :] = total
        return carry

    pl.when(alone)(large_weights[1][0].start)
    large_weights[1][1].start()
    pl.when(helper)(lambda: help_on(0))
    lax.fori_loop(0, C // 8, conv_own, 0)
    pl.when(plain)(lambda: pass_on(0))
    for copy in halo:
        copy.wait_recv()
    for s in list(range(0, HALO)) + list(range(HALO + COLS, SLOTS)):
        fm[:, s * LAT : (s + 1) * LAT] = fbuf[s]
    for s in list(range(0, HALO, 2)) + list(range(HALO + COLS, SLOTS, 2)):
        stem_pair(s)

    def conv_forward(block, carry):
        here = pl.ds(pl.multiple_of(block * 8, 8), 8)
        x = {s: xs[s, here, :] for s in range(SLOTS) if not HALO <= s < HALO + COLS}
        out = [None] * COLS
        for q in range(SIDE):
            b = (q - 3) * 2
            w = [taps[p * SIDE + q, here, :] for p in range(SIDE)]
            for i in range(COLS):
                total = partial[q * COLS + i, here, :]
                for p in range(SIDE):
                    if p not in own_taps(i):
                        total = total + w[p] * x[i + 2 * p]
                if b != 0:
                    total = jnp.where(keep[b], pltpu.roll(total, (-b) % LAT, 1), 0.0)
                out[i] = total if out[i] is None else out[i] + total
        for i in range(COLS):
            ms[i, here, :] = out[i]
        return carry

    lax.fori_loop(0, 13, conv_forward, 0)
    pl.when(helper)(lambda: help_on(1))
    pl.when(busy)(lambda: pass_on(0))
    lax.fori_loop(13, C // 8, conv_forward, 0)

    nh[...] = jnp.zeros(nh.shape, BF16)
    rstds = []
    for i in range(COLS):
        tile = ms[i]
        centred = tile - jnp.mean(tile, axis=0, keepdims=True)
        rstd = lax.rsqrt(jnp.mean(centred * centred, axis=0, keepdims=True) + 1e-06)
        normed = centred * rstd
        ms[i] = normed
        rstds.append(rstd)
        nh[0:C, i * LAT : (i + 1) * LAT] = normed.astype(BF16)

    large_weights[0][1].wait_recv()
    large_weights[0][2].wait_recv()
    second = dot(from_padded, gb[...].reshape(CP, FP + 128))
    up_w[...] = second[:, 0:FP].astype(BF16)
    up_t[...] = second[:, 0:FP].T.astype(BF16)
    head_w[...] = second[:, FP : FP + 128]
    head_t[...] = second[:, FP : FP + 128].T.astype(BF16)
    pl.when(plain)(lambda: pass_on(1))
    limits[...] = jnp.ones((1, LAT), F32)
    limits[:, 0:V] = clip[...].astype(F32) / 16.0
    sq[...] = jnp.zeros(sq.shape, F32)
    bo[...] = jnp.zeros(bo.shape, BF16)
    for j in range(0, 2):
        part = pl.ds(j * 2 * LAT, 2 * LAT)
        for f in range(0, FF, FB):
            u = dot(up_t[f : f + FB, :], nh[:, part])
            u2 = u * u
            half = 0.5 + 0.5 * jnp.tanh(u * (GELU_K + (GELU_K * 0.044715) * u2))
            value = u * half
            act[f : f + FB, part] = value.astype(BF16)
            slope[f : f + FB, part] = half + value * (1.0 - half) * (
                2.0 * GELU_K + (6.0 * GELU_K * 0.044715) * u2
            )
    pl.when(busy)(lambda: pass_on(1))
    for j in range(2, 4):
        part = pl.ds(j * 2 * LAT, 2 * LAT)
        for f in range(0, FF, FB):
            u = dot(up_t[f : f + FB, :], nh[:, part])
            u2 = u * u
            half = 0.5 + 0.5 * jnp.tanh(u * (GELU_K + (GELU_K * 0.044715) * u2))
            value = u * half
            act[f : f + FB, part] = value.astype(BF16)
            slope[f : f + FB, part] = half + value * (1.0 - half) * (
                2.0 * GELU_K + (6.0 * GELU_K * 0.044715) * u2
            )
    large_weights[1][1].wait_recv()
    large_weights[1][2].wait_recv()
    for d in range(4):
        down_f[C * d : C * (d + 1), :] = gd[d].astype(F32)[0:C]
    down_w[...] = down_f[...].astype(BF16)
    down_t[...] = down_f[...].T.astype(BF16)

    for j in range(COLS // 2):
        part = pl.ds(j * 2 * LAT, 2 * LAT)
        branch = dot(down_t[...], act[:, part])[0:C]
        centre = jnp.concatenate([xs[HALO + 2 * j], xs[HALO + 2 * j + 1]], axis=1)
        bo[0:C, part] = (centre + branch).astype(BF16)
    for j in range(COLS // 2):
        part = pl.ds(j * 2 * LAT, 2 * LAT)
        predicted = dot(head_t[0:VP, :], bo[:, part])
        for h in range(2):
            i = 2 * j + h
            ocean = land[i : i + 1, :].astype(F32)
            wanted = f32b[pl.ds(i, VP, stride=COLS), :]
            miss = (predicted[:, h * LAT : (h + 1) * LAT] - wanted) * ocean
            mis[:, i * LAT : (i + 1) * LAT] = miss.astype(BF16)
            sq[0:VP, :] = sq[0:VP, :] + miss * miss

    lanes = lax.broadcasted_iota(jnp.int32, (1, LAT), 1)
    ocean_local = jnp.sum(land[...].astype(F32))
    mine = jnp.sum(sq[...].T, axis=0, keepdims=True)
    sa[idx_p] = jnp.where(lanes == V, ocean_local, mine)
    stage(0, 32, PLANE, lambda j: sa.at[idx_p], sa.at[idx_p])

    gdn[...] = jnp.zeros(gdn.shape, F32)
    own_down = dot_nt(act[...], mis[...])
    for d in range(4):
        gdn[CP * d : CP * d + C, 0:VP] = own_down[C * d : C * d + C]
    own_head = dot_nt(bo[...], mis[...]).astype(BF16)
    own_head = dot(to_padded, own_head)
    for d in range(4):
        gdn[CP * d + C : CP * d + C + 56, 0:VP] = own_head[64 * d : 64 * d + 56]
    for d in range(4):
        for r in range(8):
            piece = (d % 2) * 16 + (d // 2) * 8 + r
            ld[piece] = gdn[CP * d + 32 * r : CP * d + 32 * r + 32, :].astype(BF16)
    away = pl.ds((1 - core) * 16, 16)
    copy_d = remote(ld.at[away], rd0, send_s.at[2], recv_s.at[2], sibling)
    copy_d.start()
    flat[...] = jnp.zeros(flat.shape, F32)
    stem_t[...] = stem_w[...].astype(F32).T.astype(BF16)

    stage_wait(0, 32, sa)
    total = sa[0]
    for j in range(1, 32):
        total = total + sa[j]
    sb[z] = total
    stage(1, 8, RING, lambda j: sb.at[z], sb.at[z])
    copy_d.wait_recv()
    for j in range(16):
        ls_d[j] = (ld[core * 16 + j].astype(F32) + rd0[j].astype(F32)).astype(BF16)
    stage(4, 16, CORES, lambda j: ls_d.at[j], rx_d.at[idx_m])
    stage_wait(1, 8, sb)
    total = sb[0]
    for j in range(1, 8):
        total = total + sb[j]
    ocean_count = jnp.sum(jnp.where(lanes == V, total, 0.0), axis=1, keepdims=True)
    valid = lanes < V
    threshold = limits[...]
    mean_error = jnp.where(valid, total, 0.0) / ocean_count
    ratio = 1.0 + mean_error / threshold
    o_loss[...] = jnp.sum(jnp.where(valid, threshold * jnp.log(ratio), 0.0), axis=1, keepdims=True)
    factor = jnp.where(valid, 2.0 / (ocean_count * ratio), 0.0)

    head_s[...] = (head_w[...] * factor).astype(BF16)
    scaled = head_s[...]
    for j in range(COLS // 2):
        part = pl.ds(j * 2 * LAT, 2 * LAT)
        grad = dot(scaled[:, 0:VP], mis[:, part])
        bg[:, part] = grad[0:C]
        bh[:, part] = grad.astype(BF16)
    pre[FF:FP, :] = jnp.zeros((FP - FF, CELLS), BF16)
    for j in range(COLS // 2):
        part = pl.ds(j * 2 * LAT, 2 * LAT)
        for f in range(0, FF, FB):
            pre[f : f + FB, part] = (
                dot(down_w[f : f + FB, :], bh[:, part]) * slope[f : f + FB, part]
            ).astype(BF16)
    up_grad = dot_nt(nh[...], pre[...])
    for l in range(7):
        gup[l] = up_grad[:, 128 * l : 128 * l + 128]
    for d in range(4):
        for l in range(7):
            at = 384 * d + 50 * l
            flat[at : at + 50, :] = gup[l, 50 * d : 50 * d + 50, :]
    for d in range(4):
        for r in range(8):
            piece = (d % 2) * 16 + (d // 2) * 8 + r
            lu[piece] = flat[384 * d + 48 * r : 384 * d + 48 * r + 48, :].astype(BF16)
    copy_u = remote(lu.at[away], ru0, send_s.at[3], recv_s.at[3], sibling)
    copy_u.start()

    for j in range(COLS // 2):
        part = pl.ds(j * 2 * LAT, 2 * LAT)
        grad = dot(up_w[...], pre[:, part])[0:C]
        for h in range(2):
            i = 2 * j + h
            g = grad[:, h * LAT : (h + 1) * LAT]
            normed = ms[i]
            mean_g = jnp.mean(g, axis=0, keepdims=True)
            mean_gn = jnp.mean(g * normed, axis=0, keepdims=True)
            ms[i] = (rstds[i] * (g - mean_g - normed * mean_gn)).astype(BF16).astype(F32)

    stage_wait(4, 16, rx_d)
    rx_d[idx_m] = ls_d[idx_m]
    large = rx_d[0].astype(F32)
    for j in range(1, 16):
        large = large + rx_d[j].astype(F32)
    part_d[z] = large.astype(BF16)
    stage(7, 8, RING, lambda j: part_d.at[z], part_d.at[z])

    def conv_backward(block, carry):
        here = pl.ds(pl.multiple_of(block * 8, 8), 8)
        x = [xs[s, here, :] for s in range(SLOTS)]
        m = [ms[i, here, :] for i in range(COLS)]
        out = [None] * SLOTS
        for q in range(SIDE):
            b = (q - 3) * 2
            if b != 0:
                shifted = [jnp.where(keep[-b], pltpu.roll(t, b % LAT, 1), 0.0) for t in m]
            else:
                shifted = m
            for p in range(SIDE):
                t = p * SIDE + q
                w = taps[t, here, :]
                corr = None
                for i in range(COLS):
                    s = i + 2 * p
                    term = w * shifted[i]
                    out[s] = term if out[s] is None else out[s] + term
                    prod = shifted[i] * x[s]
                    corr = prod if corr is None else corr + prod
                corrs[t, here, :] = corr
        for s in range(SLOTS):
            back[s, here, :] = out[s]
        return carry

    lax.fori_loop(0, 3, conv_backward, 0)
    copy_u.wait_recv()
    for j in range(16):
        ls_u[j] = (lu[core * 16 + j].astype(F32) + ru0[j].astype(F32)).astype(BF16)
    stage(11, 16, CORES, lambda j: ls_u.at[j], rx_u.at[idx_m])
    lax.fori_loop(3, 22, conv_backward, 0)

    stage_wait(7, 8, part_d)
    large = part_d[0].astype(F32)
    for j in range(1, 8):
        large = large + part_d[j].astype(F32)
    lg_d[idx_h] = large.astype(BF16)
    stage(12, 8, SHARE, lambda j: lg_d.at[idx_h], lg_d.at[idx_h])
    stage_wait(11, 16, rx_u)
    rx_u[idx_m] = ls_u[idx_m]
    large = rx_u[0].astype(F32)
    for j in range(1, 16):
        large = large + rx_u[j].astype(F32)
    part_u[z] = large.astype(BF16)
    stage(5, 8, RING, lambda j: part_u.at[z], part_u.at[z])

    lax.fori_loop(22, C // 8, conv_backward, 0)
    tap_col = lax.broadcasted_iota(jnp.int32, (2 * LAT, LAT), 1)
    lower_half = (lax.broadcasted_iota(jnp.int32, (2 * LAT, LAT), 0) >= LAT).astype(jnp.int32)
    kern = None
    for t in range(0, SIDE * SIDE, 2):
        place = jnp.where(tap_col == V + t + lower_half, 1.0, 0.0).astype(BF16)
        terms = corrs[t].astype(BF16)
        if t + 1 < SIDE * SIDE:
            terms = jnp.concatenate([terms, corrs[t + 1].astype(BF16)], axis=1)
        else:
            place = place[0:LAT]
        part_sum = dot(terms, place)
        kern = part_sum if kern is None else kern + part_sum

    sh[C:CP, :] = jnp.zeros((CP - C, SLOTS * LAT), BF16)
    for s in range(SLOTS):
        value = back[s]
        if HALO <= s < HALO + COLS:
            value = value + bg[:, (s - HALO) * LAT : (s - HALO + 1) * LAT]
        sh[0:C, s * LAT : (s + 1) * LAT] = value.astype(BF16)
    small[...] = jnp.zeros(small.shape, F32)
    small[:, 0:VP] = dot_nt(sh[...], fm[...])
    small[0:C, :] = small[0:C, :] + kern
    tiny = dot(to_padded, small[...].astype(BF16))
    for j in range(8):
        at = 64 * (j % 4) + 32 * (j // 4)
        stx[j] = tiny[at : at + 32].astype(BF16)
    stage(6, 8, ROW, lambda j: stx.at[j], srx.at[idx_e])

    for s in list(range(0, HALO, 2)) + list(range(HALO + COLS, SLOTS, 2)):
        value = dot(stem_t[0:VP, :], sh[:, s * LAT : (s + 2) * LAT]).astype(BF16)
        sen[s if s < HALO else s - COLS] = value[:, 0:LAT]
        sen[s + 1 if s < HALO else s + 1 - COLS] = value[:, LAT : 2 * LAT]
    copy_l = remote(sen.at[pl.ds(0, 6)], hr, send_h.at[2], recv_h.at[2], left)
    copy_r = remote(sen.at[pl.ds(6, 6)], hl, send_h.at[3], recv_h.at[3], right)
    copy_l.start()
    copy_r.start()

    for j in range(COLS // 2):
        s = HALO + 2 * j
        value = dot(stem_t[0:VP, :], sh[:, s * LAT : (s + 2) * LAT])
        cells[2 * j] = value[:, 0:LAT]
        cells[2 * j + 1] = value[:, LAT : 2 * LAT]

    stage_wait(6, 8, srx)
    srx[idx_e] = stx[idx_e]
    tiny = srx[0].astype(F32)
    for j in range(1, 8):
        tiny = tiny + srx[j].astype(F32)
    s2x[z] = tiny.astype(BF16)
    stage(8, 8, RING, lambda j: s2x.at[z], s2x.at[z])

    stage_wait(5, 8, part_u)
    large = part_u[0].astype(F32)
    for j in range(1, 8):
        large = large + part_u[j].astype(F32)
    lg_u[idx_h] = large.astype(BF16)
    stage(9, 8, SHARE, lambda j: lg_u.at[idx_h], lg_u.at[idx_h])

    stage_wait(12, 8, lg_d)
    for r in range(8):
        dsum[32 * r : 32 * r + 32, :] = lg_d[(r % 2) * 4 + r // 2]
    o_down[...] = dot_nt(dsum[...], head_s[...])[0:C, 0:C]
    o_head[...] = (dsum[...].astype(F32)[C : C + 50] * factor)[:, 0:V]

    stage_wait(8, 8, s2x)
    tiny = s2x[0].astype(F32)
    for j in range(1, 8):
        tiny = tiny + s2x[j].astype(F32)
    sfin[idx_h] = tiny.astype(BF16)
    stage(10, 8, SHARE, lambda j: sfin.at[idx_h], sfin.at[idx_h])

    copy_l.wait_recv()
    copy_r.wait_recv()
    for i in range(COLS):
        value = cells[i]
        if i >= 2:
            value = value + hr[i - 2].astype(F32)
        if i < 6:
            value = value + hl[i].astype(F32)
        o_sens[pl.ds(i, V, stride=COLS), :] = (value * ocean_count)[0:V]

    stage_wait(9, 8, lg_u)
    for r in range(8):
        flat[48 * r : 48 * r + 48, :] = lg_u[(r % 2) * 4 + r // 2].astype(F32)
    for l in range(7):
        width = min(128, FF - 128 * l)
        o_up[:, 128 * l : 128 * l + width] = flat[50 * l : 50 * l + 50, 0:width]
    stage_wait(10, 8, sfin)
    for h, rows in ((0, 32), (1, 18)):
        tiny = sfin[4 * h].astype(F32)
        for j in range(1, 4):
            tiny = tiny + sfin[4 * h + j].astype(F32)
        o_stem[32 * h : 32 * h + rows, :] = tiny[0:rows, 0:V]
        o_kern[32 * h : 32 * h + rows, :] = pltpu.roll(tiny, LAT - V, 1)[0:rows, 0:49]
    for copy in first_weights + halo + [large_weights[a][i] for a in (0, 1) for i in (1, 2)]:
        copy.wait_send()

    @pl.when(alone)
    def _():
        large_weights[0][0].wait_send()
        large_weights[1][0].wait_send()

    @pl.when(helper)
    def _():
        help_copies[0].wait_send()
        help_copies[1].wait_send()

    for copy in [copy_d, copy_u, copy_l, copy_r] + pending:
        copy.wait_send()


def hand_over(*refs):
    copies = [pltpu.make_async_copy(refs[n], refs[7 + n], refs[14].at[n]) for n in range(7)]
    for n in (6, 2, 3, 0, 1, 4, 5):
        copies[n].start()
    for copy in copies:
        copy.wait()


SCRATCH = [
    ((V, COLS, LAT), BF16),
    ((V, COLS, LAT), BF16),
    ((COLS, LAT), jnp.int32),
    ((1, V), jnp.int32),
    ((50, V), BF16),
    ((50, SIDE * SIDE), BF16),
    ((50, FF), BF16),
    ((C, C), BF16),
    ((50, V), BF16),
    ((VP * COLS, LAT), F32),
    ((VP * COLS, LAT), F32),
    ((SLOTS, VP, LAT), BF16),
    ((VP, SLOTS * LAT), BF16),
    ((64, 256 + FP + 128), F32),
    ((208, CP), F32),
    ((4, 64, 128), BF16),
    ((4, 64, FP + 128), BF16),
    ((4, 208, CP), BF16),
    ((CP, 128), BF16),
    ((128, CP), BF16),
    ((CP, FP), BF16),
    ((FP, CP), BF16),
    ((CP, 128), F32),
    ((CP, 128), BF16),
    ((128, CP), BF16),
    ((FF, CP), BF16),
    ((CP, FF), BF16),
    ((FF, CP), F32),
    ((SIDE * SIDE, C, LAT), F32),
    ((SIDE * COLS, C, LAT), F32),
    ((SIDE * SIDE, C, LAT), F32),
    ((SLOTS, C, LAT), F32),
    ((COLS, C, LAT), F32),
    ((CP, CELLS), BF16),
    ((FF, CELLS), BF16),
    ((FF, CELLS), F32),
    ((FP, CELLS), BF16),
    ((CP, CELLS), BF16),
    ((VP, CELLS), BF16),
    ((1, LAT), F32),
    ((128, LAT), F32),
    ((32, 1, LAT), F32),
    ((8, 1, LAT), F32),
    ((C, CELLS), F32),
    ((CP, CELLS), BF16),
    ((4 * CP, 128), F32),
    ((7, CP, 128), F32),
    ((4 * 384, 128), F32),
    ((SLOTS, C, LAT), F32),
    ((CP, SLOTS * LAT), BF16),
    ((CP, 128), F32),
    ((CP, 128), BF16),
    ((32, 32, 128), BF16),
    ((32, 48, 128), BF16),
    ((16, 32, 128), BF16),
    ((16, 48, 128), BF16),
    ((16, 32, 128), BF16),
    ((16, 48, 128), BF16),
    ((16, 32, 128), BF16),
    ((16, 48, 128), BF16),
    ((8, 48, 128), BF16),
    ((8, 48, 128), BF16),
    ((8, 32, 128), BF16),
    ((8, 32, 128), BF16),
    ((8, 32, 128), BF16),
    ((8, 32, 128), BF16),
    ((8, 32, 128), BF16),
    ((8, 32, 128), BF16),
    ((12, VP, LAT), BF16),
    ((6, VP, LAT), BF16),
    ((6, VP, LAT), BF16),
    ((COLS, VP, LAT), F32),
]


def shards(
    fields, targets, land_sea, clip_level, stem_weight, dw_kernel, up_weight, down_weight, head_weight
):
    anywhere = pl.BlockSpec(memory_space=pl.ANY)
    vmem = pl.BlockSpec(memory_space=pltpu.VMEM)
    dma = pltpu.SemaphoreType.DMA
    shapes = [(50, V), (50, 49), (50, FF), (C, C), (50, V), (1, 1), (V * COLS, LAT)]
    results = [jax.ShapeDtypeStruct(s, F32) for s in shapes]
    made = pl.pallas_call(
        body,
        out_shape=[pltpu.VMEM(s, F32) for s in shapes],
        in_specs=[anywhere] * 9,
        out_specs=[vmem] * 7,
        scratch_shapes=[pltpu.VMEM(s, t) for s, t in SCRATCH]
        + [dma((n,)) for n in (11, 9, 4, 4, 13, 13, 9)],
        compiler_params=pltpu.CompilerParams(
            collective_id=0, has_side_effects=True, vmem_limit_bytes=58 * 1024 * 1024
        ),
    )(
        fields.reshape(V, COLS, LAT),
        targets.reshape(V, COLS, LAT),
        land_sea,
        clip_level.reshape(1, V),
        stem_weight,
        dw_kernel,
        up_weight,
        down_weight,
        head_weight,
    )
    outs = pl.pallas_call(
        hand_over,
        out_shape=results,
        in_specs=[vmem] * 7,
        out_specs=[anywhere] * 7,
        scratch_shapes=[dma((7,))],
    )(*[pltpu.with_memory_space_constraint(m, pltpu.VMEM) for m in made])
    return (
        outs[0], outs[1], outs[2], outs[3], outs[4],
        outs[5].reshape(()),
        outs[6].reshape(1, V, COLS, LAT),
    )


def solution(mesh):
    placed = (
        P("dp", None, "lon", None),
        P("dp", None, "lon", None),
        P("lon", None),
        P(),
        P("dp", None),
        P("dp", None),
        P("dp", None),
        P("dp", None),
        P("dp", None),
    )
    return jax.shard_map(
        shards,
        mesh=mesh,
        in_specs=placed,
        out_specs=(
            P("dp", None),
            P("dp", None),
            P("dp", None),
            P("dp", None),
            P("dp", None),
            P(),
            P("dp", None, "lon", None),
        ),
        check_vma=False,
    )
```

```python
import itertools

import jax
import jax.numpy as jnp
from jax import lax
from jax.experimental import pallas as pl
from jax.experimental.pallas import tpu as pltpu
from jax.sharding import PartitionSpec as P

MESH = pl.DeviceIdType.MESH
F32 = jnp.float32
BF16 = jnp.bfloat16

V = 77
VP = 80
C = 200
CP = 256
CR = 208
FF = 800
FP = 896
FB = 400
COLS = 8
LAT = 128
SIDE = 7
HALO = 6
SLOTS = COLS + 2 * HALO
CELLS = COLS * LAT
GELU_K = 0.7978845608


def dot(a, b):
    return jnp.dot(a, b, preferred_element_type=F32)


def dot_nt(a, b):
    return lax.dot_general(a, b, (((1,), (1,)), ((), ())), preferred_element_type=F32)


def remote(src, dst, send, recv, device):
    return pltpu.make_async_remote_copy(
        src_ref=src,
        dst_ref=dst,
        send_sem=send,
        recv_sem=recv,
        device_id=device,
        device_id_type=MESH,
    )


def hops(offset):
    a, b, c, d, e = offset
    x = {(0, 0): 0, (0, 1): 1, (1, 0): 2, (1, 1): 1}[a, d]
    return x + min(b, 4 - b) + min(c, 8 - c) + 0.5 * e


def group(*sizes):
    offsets = itertools.product(*(range(n) for n in sizes))
    return sorted((o for o in offsets if any(o)), key=lambda o: -hops(o))


def padded_row(channel):
    step = (channel >= 50).astype(jnp.int32)
    step += (channel >= 100).astype(jnp.int32)
    step += (channel >= 150).astype(jnp.int32)
    return channel + 14 * step


def body(*refs):
    inputs, made, rest = refs[:9], refs[9:16], refs[16:]
    held = rest[:9]
    o_stem, o_kern, o_up, o_down, o_head, o_loss, o_sens = made
    fields, targets, land, clip, stem, dw, up, down, head = held
    (
    f32a, f32b, fbuf, fm, wp, wd, ga, gb, gd,
        stem_w, stem_t, up_w, up_t, head_w, head_s, head_t, down_w, down_t, down_f,
        taps, partial, corrs, xs, ms, nh, act, slope, pre, bo, mis, limits, sq, sa, sb,
        bg, bh, gdn, gup, flat, back, sh, small, dsum,
        ld, lu, rd0, ru0, ls_d, ls_u, rx_d, rx_u, part_u, lg_u, part_d, lg_d,
        stx, srx, s2x, sfin, sen, hl, hr, cells,
        send_g, recv_g, send_h, recv_h, send_s, recv_s, load_sem,
    ) = rest[9:]
    lon = lax.axis_index("lon")
    dp = lax.axis_index("dp")
    x_hi, y, z = lon // 32, (lon // 8) % 4, lon % 8
    x_lo, core = dp // 2, dp % 2
    right = ((lon + 1) % 64, dp)
    left = ((lon + 63) % 64, dp)
    sibling = (lon, x_lo * 2 + (1 - core))
    idx_p = (x_hi * 4 + y) * 4 + dp
    idx_m = (x_lo * 4 + y) * 2 + x_hi
    idx_h = x_hi * 4 + y
    idx_e = x_hi * 4 + dp

    busy = ((y == 3) & (z == 0)) | ((y == 0) & (z == 7))
    helper = ((y == 2) & (z == 0)) | ((y == 1) & (z == 7))
    alone, plain = jnp.logical_not(busy), jnp.logical_not(busy | helper)
    helped = (x_hi * 32 + ((y + jnp.where(z == 0, 1, 3)) % 4) * 8 + z, dp)

    def peer(offset):
        a, b, c, d, e = offset
        return (x_hi + a) % 2, (y + b) % 4, (z + c) % 8, (x_lo + d) % 2, (core + e) % 2

    def device(at):
        return at[0] * 32 + at[1] * 8 + at[2], at[3] * 2 + at[4]

    PLANE = group(2, 4, 1, 2, 2), lambda at: (at[0] * 4 + at[1]) * 4 + at[3] * 2 + at[4]
    RING = group(1, 1, 8, 1, 1), lambda at: at[2]
    CORES = group(2, 4, 1, 2, 1), lambda at: (at[3] * 4 + at[1]) * 2 + at[0]
    SHARE = group(2, 4, 1, 1, 1), lambda at: at[0] * 4 + at[1]
    ROW = group(2, 1, 1, 2, 2), lambda at: at[0] * 4 + at[3] * 2 + at[4]

    loads = [
        pltpu.make_async_copy(src, dst, load_sem.at[n])
        for n, (src, dst) in enumerate(zip(inputs, held))
    ]
    for copy in loads:
        copy.start()
    barrier = pltpu.get_barrier_semaphore()
    for offset in RING[0]:
        pl.semaphore_signal(
            barrier, inc=1, device_id=device(peer(offset)), device_id_type=MESH
        )
    for target in (right, left):
        pl.semaphore_signal(barrier, inc=1, device_id=target, device_id_type=MESH)
    for offset in PLANE[0]:
        pl.semaphore_signal(
            barrier, inc=1, device_id=device(peer(offset)), device_id_type=MESH
        )

    for copy in loads:
        copy.wait()
    f32a[0 : V * COLS, :] = fields[...].astype(F32).reshape(V * COLS, LAT)
    f32a[V * COLS : VP * COLS, :] = jnp.zeros(((VP - V) * COLS, LAT), F32)
    f32b[0 : V * COLS, :] = targets[...].astype(F32).reshape(V * COLS, LAT)
    f32b[V * COLS : VP * COLS, :] = jnp.zeros(((VP - V) * COLS, LAT), F32)
    for i in range(COLS):
        fbuf[HALO + i] = f32a[pl.ds(i, VP, stride=COLS), :].astype(BF16)
    wp[...] = jnp.zeros(wp.shape, F32)
    wp[0:50, 0:V] = stem[...].astype(F32)
    wp[0:50, 128:177] = dw[...].astype(F32)
    wp[0:50, 256 : 256 + FF] = up[...].astype(F32)
    wp[0:50, 256 + FP : 256 + FP + V] = head[...].astype(F32)
    wd[...] = jnp.zeros(wd.shape, F32)
    wd[0:C, 0:C] = down[...].astype(F32)
    ga[dp] = (wp[:, 0:128] + pltpu.roll(wp[:, 128:256], V, 1)).astype(BF16)
    gb[dp] = wp[:, 256 : 256 + FP + 128].astype(BF16)
    gd[dp] = wd[...].astype(BF16)

    pl.semaphore_wait(barrier, 40)

    halo = [
        remote(fbuf.at[pl.ds(8, 6)], fbuf.at[pl.ds(0, 6)], send_h.at[0], recv_h.at[0], right),
        remote(fbuf.at[pl.ds(6, 6)], fbuf.at[pl.ds(14, 6)], send_h.at[1], recv_h.at[1], left),
    ]
    first_weights = [
        remote(ga.at[dp], ga.at[dp], send_g.at[k - 1], recv_g.at[k - 1], (lon, (dp + k) % 4))
        for k in range(1, 4)
    ]
    for copy in first_weights:
        copy.start()
    across = (lon, (1 - x_lo) * 2 + core)
    far = (1 - x_lo) * 2 + core
    large_weights = []
    for a, buf in enumerate((gb, gd)):
        at = 3 + 3 * a
        large_weights.append(
            (
                remote(buf.at[dp], buf.at[dp], send_g.at[at], recv_g.at[at], across),
                remote(buf.at[dp], buf.at[dp], send_g.at[at + 1], recv_g.at[at + 1], sibling),
                remote(buf.at[far], buf.at[far], send_g.at[at + 2], recv_g.at[at + 2], sibling),
            )
        )

    for copy in halo:
        copy.start()
    pl.when(alone)(large_weights[0][0].start)

    help_copies = [
        remote(buf.at[far], buf.at[far], send_g.at[9 + a], recv_g.at[3 + 3 * a], helped)
        for a, buf in enumerate((gb, gd))
    ]

    def pass_on(a):
        large_weights[a][0].wait_recv()
        large_weights[a][2].start()

    def help_on(a):
        pass_on(a)
        help_copies[a].start()

    pending = []

    def stage(index, count, peers, src, dst):
        for offset in peers[0][: count - 1]:
            at = peer(offset)
            remote(
                src(peers[1](at)), dst, send_s.at[index], recv_s.at[index], device(at)
            ).start()

    def stage_wait(index, count, buf):
        whole = buf.at[pl.ds(0, count - 1)]
        both = remote(whole, whole, send_s.at[index], recv_s.at[index], right)
        both.wait_recv()
        pending.append(both)

    row = lax.broadcasted_iota(jnp.int32, (CP, CP), 0)
    col = lax.broadcasted_iota(jnp.int32, (CP, CP), 1)
    from_padded = jnp.where((row < C) & (col == padded_row(row)), 1.0, 0.0).astype(BF16)
    to_padded = jnp.where((col < C) & (row == padded_row(col)), 1.0, 0.0).astype(BF16)
    lane = lax.broadcasted_iota(jnp.int32, (8, LAT), 1)
    keep = {b: (lane + b >= 0) & (lane + b < LAT) for b in range(-HALO, HALO + 1, 2)}

    for i in range(COLS):
        fm[:, (HALO + i) * LAT : (HALO + i + 1) * LAT] = fbuf[HALO + i]

    for copy in first_weights:
        copy.wait_recv()
    large_weights[0][1].start()
    stem_w[...] = dot(from_padded, ga[...].reshape(CP, 128)).astype(BF16)
    def stem_pair(s):
        out = dot(stem_w[0:CR, 0:VP], fm[:, s * LAT : (s + 2) * LAT])[0:C].astype(BF16).astype(F32)
        xs[s] = out[:, 0:LAT]
        xs[s + 1] = out[:, LAT : 2 * LAT]

    for s in range(HALO, HALO + COLS, 2):
        stem_pair(s)
    kern_w = stem_w[0:CR, :]
    tap_row = lax.broadcasted_iota(jnp.int32, (LAT, 2 * LAT), 0)
    second_half = (lax.broadcasted_iota(jnp.int32, (LAT, 2 * LAT), 1) >= LAT).astype(jnp.int32)
    for t in range(0, SIDE * SIDE, 2):
        spread = dot(kern_w, jnp.where(tap_row == V + t + second_half, 1.0, 0.0).astype(BF16))[0:C]
        taps[t] = spread[:, 0:LAT]
        if t + 1 < SIDE * SIDE:
            taps[t + 1] = spread[:, LAT : 2 * LAT]
    def several(step):
        def steps(group, carry):
            for n in range(5):
                step(group * 5 + n, carry)
            return carry

        return steps

    def own_taps(i):
        return [p for p in range(SIDE) if HALO <= i + 2 * p < HALO + COLS]

    def conv_own(block, carry):
        here = pl.ds(pl.multiple_of(block * 8, 8), 8)
        x = {s: xs[s, here, :] for s in range(HALO, HALO + COLS)}
        for q in range(SIDE):
            w = [taps[p * SIDE + q, here, :] for p in range(SIDE)]
            for i in range(COLS):
                total = None
                for p in own_taps(i):
                    term = w[p] * x[i + 2 * p]
                    total = term if total is None else total + term
                partial[q * COLS + i, here, :] = total
        return carry

    pl.when(alone)(large_weights[1][0].start)
    large_weights[1][1].start()
    pl.when(helper)(lambda: help_on(0))
    lax.fori_loop(0, 5, several(conv_own), 0)
    pl.when(plain)(lambda: pass_on(0))
    for copy in halo:
        copy.wait_recv()
    for s in list(range(0, HALO)) + list(range(HALO + COLS, SLOTS)):
        fm[:, s * LAT : (s + 1) * LAT] = fbuf[s]
    for s in list(range(0, HALO, 2)) + list(range(HALO + COLS, SLOTS, 2)):
        stem_pair(s)

    def conv_forward(block, carry):
        here = pl.ds(pl.multiple_of(block * 8, 8), 8)
        x = {s: xs[s, here, :] for s in range(SLOTS) if not HALO <= s < HALO + COLS}
        out = [None] * COLS
        for q in range(SIDE):
            b = (q - 3) * 2
            w = [taps[p * SIDE + q, here, :] for p in range(SIDE)]
            for i in range(COLS):
                total = partial[q * COLS + i, here, :]
                for p in range(SIDE):
                    if p not in own_taps(i):
                        total = total + w[p] * x[i + 2 * p]
                if b != 0:
                    total = jnp.where(keep[b], pltpu.roll(total, (-b) % LAT, 1), 0.0)
                out[i] = total if out[i] is None else out[i] + total
        for i in range(COLS):
            ms[i, here, :] = out[i]
        return carry

    lax.fori_loop(0, 3, several(conv_forward), 0)
    pl.when(helper)(lambda: help_on(1))
    pl.when(busy)(lambda: pass_on(0))
    lax.fori_loop(3, 5, several(conv_forward), 0)

    nh[...] = jnp.zeros(nh.shape, BF16)
    rstds = []
    for i in range(COLS):
        tile = ms[i]
        centred = tile - jnp.mean(tile, axis=0, keepdims=True)
        rstd = lax.rsqrt(jnp.mean(centred * centred, axis=0, keepdims=True) + 1e-06)
        normed = centred * rstd
        ms[i] = normed
        rstds.append(rstd)
        nh[0:C, i * LAT : (i + 1) * LAT] = normed.astype(BF16)

    large_weights[0][1].wait_recv()
    large_weights[0][2].wait_recv()
    second = dot(from_padded, gb[...].reshape(CP, FP + 128))
    up_w[...] = second[:, 0:FP].astype(BF16)
    up_t[...] = second[:, 0:FP].T.astype(BF16)
    head_w[...] = second[:, FP : FP + 128]
    head_t[...] = second[:, FP : FP + 128].T.astype(BF16)
    pl.when(plain | busy)(lambda: pass_on(1))
    limits[...] = jnp.ones((1, LAT), F32)
    limits[:, 0:V] = clip[...].astype(F32) / 16.0
    sq[...] = jnp.zeros(sq.shape, F32)
    bo[...] = jnp.zeros(bo.shape, BF16)
    for j in range(COLS // 2):
        part = pl.ds(j * 2 * LAT, 2 * LAT)
        for f in range(0, FF, FB):
            u = dot(up_t[f : f + FB, :], nh[:, part])
            u2 = u * u
            half = 0.5 + 0.5 * jnp.tanh(u * (GELU_K + (GELU_K * 0.044715) * u2))
            value = u * half
            act[f : f + FB, part] = value.astype(BF16)
            slope[f : f + FB, part] = half + value * (1.0 - half) * (
                2.0 * GELU_K + (6.0 * GELU_K * 0.044715) * u2
            )
    large_weights[1][1].wait_recv()
    large_weights[1][2].wait_recv()
    for d in range(4):
        down_f[C * d : C * (d + 1), :] = gd[d].astype(F32)[0:C]
    down_w[...] = down_f[...].astype(BF16)
    down_t[...] = down_f[...].T.astype(BF16)

    for j in range(COLS // 2):
        part = pl.ds(j * 2 * LAT, 2 * LAT)
        branch = dot(down_t[0:CR, :], act[:, part])[0:C]
        centre = jnp.concatenate([xs[HALO + 2 * j], xs[HALO + 2 * j + 1]], axis=1)
        bo[0:C, part] = (centre + branch).astype(BF16)
    for j in range(COLS // 2):
        part = pl.ds(j * 2 * LAT, 2 * LAT)
        predicted = dot(head_t[0:VP, :], bo[:, part])
        for h in range(2):
            i = 2 * j + h
            ocean = land[i : i + 1, :].astype(F32)
            wanted = f32b[pl.ds(i, VP, stride=COLS), :]
            miss = (predicted[:, h * LAT : (h + 1) * LAT] - wanted) * ocean
            mis[:, i * LAT : (i + 1) * LAT] = miss.astype(BF16)
            sq[0:VP, :] = sq[0:VP, :] + miss * miss

    lanes = lax.broadcasted_iota(jnp.int32, (1, LAT), 1)
    ocean_local = jnp.sum(land[...].astype(F32))
    mine = jnp.sum(sq[...].T, axis=0, keepdims=True)
    sa[idx_p] = jnp.where(lanes == V, ocean_local, mine)
    stage(0, 32, PLANE, lambda j: sa.at[idx_p], sa.at[idx_p])

    gdn[...] = jnp.zeros(gdn.shape, F32)
    own_down = dot_nt(act[...], mis[...])
    for d in range(4):
        gdn[CP * d : CP * d + C, 0:VP] = own_down[C * d : C * d + C]
    own_head = dot_nt(bo[...], mis[...]).astype(BF16)
    own_head = dot(to_padded, own_head)
    for d in range(4):
        gdn[CP * d + C : CP * d + C + 56, 0:VP] = own_head[64 * d : 64 * d + 56]
    for d in range(4):
        for r in range(8):
            piece = (d % 2) * 16 + (d // 2) * 8 + r
            ld[piece] = gdn[CP * d + 32 * r : CP * d + 32 * r + 32, :].astype(BF16)
    away = pl.ds((1 - core) * 16, 16)
    copy_d = remote(ld.at[away], rd0, send_s.at[2], recv_s.at[2], sibling)
    copy_d.start()
    flat[...] = jnp.zeros(flat.shape, F32)
    bh[CR:CP, :] = jnp.zeros((CP - CR, CELLS), BF16)
    stem_t[...] = stem_w[...].astype(F32).T.astype(BF16)

    stage_wait(0, 32, sa)
    total = sa[0]
    for j in range(1, 32):
        total = total + sa[j]
    sb[z] = total
    stage(1, 8, RING, lambda j: sb.at[z], sb.at[z])
    copy_d.wait_recv()
    for j in range(16):
        ls_d[j] = (ld[core * 16 + j].astype(F32) + rd0[j].astype(F32)).astype(BF16)
    stage(4, 16, CORES, lambda j: ls_d.at[j], rx_d.at[idx_m])
    stage_wait(1, 8, sb)
    total = sb[0]
    for j in range(1, 8):
        total = total + sb[j]
    ocean_count = jnp.sum(jnp.where(lanes == V, total, 0.0), axis=1, keepdims=True)
    valid = lanes < V
    threshold = limits[...]
    mean_error = jnp.where(valid, total, 0.0) / ocean_count
    ratio = 1.0 + mean_error / threshold
    o_loss[...] = jnp.sum(jnp.where(valid, threshold * jnp.log(ratio), 0.0), axis=1, keepdims=True)
    factor = jnp.where(valid, 2.0 / (ocean_count * ratio), 0.0)

    head_s[...] = (head_w[...] * factor).astype(BF16)
    scaled = head_s[...]
    for j in range(COLS // 2):
        part = pl.ds(j * 2 * LAT, 2 * LAT)
        grad = dot(scaled[0:CR, 0:VP], mis[:, part])
        bg[:, part] = grad[0:C]
        bh[0:CR, part] = grad.astype(BF16)
    pre[FF:FP, :] = jnp.zeros((FP - FF, CELLS), BF16)
    for j in range(COLS // 2):
        part = pl.ds(j * 2 * LAT, 2 * LAT)
        for f in range(0, FF, 160):
            pre[f : f + 160, part] = (
                dot(down_w[f : f + 160, :], bh[:, part]) * slope[f : f + 160, part]
            ).astype(BF16)
    up_grad = dot_nt(nh[0:CR, :], pre[...])
    for l in range(7):
        gup[l] = up_grad[:, 128 * l : 128 * l + 128]
    for d in range(4):
        for l in range(7):
            at = 384 * d + 50 * l
            flat[at : at + 50, :] = gup[l, 50 * d : 50 * d + 50, :]
    for d in range(4):
        for r in range(8):
            piece = (d % 2) * 16 + (d // 2) * 8 + r
            lu[piece] = flat[384 * d + 48 * r : 384 * d + 48 * r + 48, :].astype(BF16)
    copy_u = remote(lu.at[away], ru0, send_s.at[3], recv_s.at[3], sibling)
    copy_u.start()

    for j in range(COLS // 2):
        part = pl.ds(j * 2 * LAT, 2 * LAT)
        grad = dot(up_w[0:CR, :], pre[:, part])[0:C]
        for h in range(2):
            i = 2 * j + h
            g = grad[:, h * LAT : (h + 1) * LAT]
            normed = ms[i]
            mean_g = jnp.mean(g, axis=0, keepdims=True)
            mean_gn = jnp.mean(g * normed, axis=0, keepdims=True)
            ms[i] = (rstds[i] * (g - mean_g - normed * mean_gn)).astype(BF16).astype(F32)

    stage_wait(4, 16, rx_d)
    rx_d[idx_m] = ls_d[idx_m]
    large = rx_d[0].astype(F32)
    for j in range(1, 16):
        large = large + rx_d[j].astype(F32)
    part_d[z] = large.astype(BF16)
    stage(7, 8, RING, lambda j: part_d.at[z], part_d.at[z])

    def conv_backward(block, carry):
        here = pl.ds(pl.multiple_of(block * 8, 8), 8)
        x = [xs[s, here, :] for s in range(SLOTS)]
        m = [ms[i, here, :] for i in range(COLS)]
        out = [None] * SLOTS
        for q in range(SIDE):
            b = (q - 3) * 2
            if b != 0:
                shifted = [jnp.where(keep[-b], pltpu.roll(t, b % LAT, 1), 0.0) for t in m]
            else:
                shifted = m
            for p in range(SIDE):
                t = p * SIDE + q
                w = taps[t, here, :]
                corr = None
                for i in range(COLS):
                    s = i + 2 * p
                    term = w * shifted[i]
                    out[s] = term if out[s] is None else out[s] + term
                    prod = shifted[i] * x[s]
                    corr = prod if corr is None else corr + prod
                corrs[t, here, :] = corr
        for s in range(SLOTS):
            back[s, here, :] = out[s]
        return carry

    lax.fori_loop(0, 1, several(conv_backward), 0)
    copy_u.wait_recv()
    for j in range(16):
        ls_u[j] = (lu[core * 16 + j].astype(F32) + ru0[j].astype(F32)).astype(BF16)
    stage(11, 16, CORES, lambda j: ls_u.at[j], rx_u.at[idx_m])
    lax.fori_loop(1, 5, several(conv_backward), 0)

    stage_wait(7, 8, part_d)
    large = part_d[0].astype(F32)
    for j in range(1, 8):
        large = large + part_d[j].astype(F32)
    lg_d[idx_h] = large.astype(BF16)
    stage(12, 8, SHARE, lambda j: lg_d.at[idx_h], lg_d.at[idx_h])
    stage_wait(11, 16, rx_u)
    rx_u[idx_m] = ls_u[idx_m]
    large = rx_u[0].astype(F32)
    for j in range(1, 16):
        large = large + rx_u[j].astype(F32)
    part_u[z] = large.astype(BF16)
    stage(5, 8, RING, lambda j: part_u.at[z], part_u.at[z])

    tap_col = lax.broadcasted_iota(jnp.int32, (2 * LAT, LAT), 1)
    lower_half = (lax.broadcasted_iota(jnp.int32, (2 * LAT, LAT), 0) >= LAT).astype(jnp.int32)
    kern = None
    for t in range(0, SIDE * SIDE, 2):
        place = jnp.where(tap_col == V + t + lower_half, 1.0, 0.0).astype(BF16)
        terms = corrs[t].astype(BF16)
        if t + 1 < SIDE * SIDE:
            terms = jnp.concatenate([terms, corrs[t + 1].astype(BF16)], axis=1)
        else:
            place = place[0:LAT]
        part_sum = dot(terms, place)
        kern = part_sum if kern is None else kern + part_sum

    sh[C:CP, :] = jnp.zeros((CP - C, SLOTS * LAT), BF16)
    for s in range(SLOTS):
        value = back[s]
        if HALO <= s < HALO + COLS:
            value = value + bg[:, (s - HALO) * LAT : (s - HALO + 1) * LAT]
        sh[0:C, s * LAT : (s + 1) * LAT] = value.astype(BF16)
    small[...] = jnp.zeros(small.shape, F32)
    small[0:CR, 0:VP] = dot_nt(sh[0:CR, :], fm[...])
    small[0:C, :] = small[0:C, :] + kern
    for j in range(8):
        at = 50 * (j % 4) + 32 * (j // 4)
        stx[j] = small[at : at + 32, :].astype(BF16)
    stage(6, 8, ROW, lambda j: stx.at[j], srx.at[idx_e])

    for s in list(range(0, HALO, 2)) + list(range(HALO + COLS, SLOTS, 2)):
        value = dot(stem_t[0:VP, :], sh[:, s * LAT : (s + 2) * LAT]).astype(BF16)
        sen[s if s < HALO else s - COLS] = value[:, 0:LAT]
        sen[s + 1 if s < HALO else s + 1 - COLS] = value[:, LAT : 2 * LAT]
    copy_l = remote(sen.at[pl.ds(0, 6)], hr, send_h.at[2], recv_h.at[2], left)
    copy_r = remote(sen.at[pl.ds(6, 6)], hl, send_h.at[3], recv_h.at[3], right)
    copy_l.start()
    copy_r.start()

    for j in range(COLS // 2):
        s = HALO + 2 * j
        value = dot(stem_t[0:VP, :], sh[:, s * LAT : (s + 2) * LAT])
        cells[2 * j] = value[:, 0:LAT]
        cells[2 * j + 1] = value[:, LAT : 2 * LAT]

    stage_wait(6, 8, srx)
    srx[idx_e] = stx[idx_e]
    tiny = srx[0].astype(F32)
    for j in range(1, 8):
        tiny = tiny + srx[j].astype(F32)
    s2x[z] = tiny.astype(BF16)
    stage(8, 8, RING, lambda j: s2x.at[z], s2x.at[z])

    stage_wait(5, 8, part_u)
    large = part_u[0].astype(F32)
    for j in range(1, 8):
        large = large + part_u[j].astype(F32)
    lg_u[idx_h] = large.astype(BF16)
    stage(9, 8, SHARE, lambda j: lg_u.at[idx_h], lg_u.at[idx_h])

    stage_wait(12, 8, lg_d)
    for r in range(8):
        dsum[32 * r : 32 * r + 32, :] = lg_d[(r % 2) * 4 + r // 2]
    o_down[...] = dot_nt(dsum[...], head_s[...])[0:C, 0:C]
    o_head[...] = (dsum[...].astype(F32)[C : C + 50] * factor)[:, 0:V]

    stage_wait(8, 8, s2x)
    tiny = s2x[0].astype(F32)
    for j in range(1, 8):
        tiny = tiny + s2x[j].astype(F32)
    sfin[idx_h] = tiny.astype(BF16)
    stage(10, 8, SHARE, lambda j: sfin.at[idx_h], sfin.at[idx_h])

    copy_l.wait_recv()
    copy_r.wait_recv()
    for i in range(COLS):
        value = cells[i]
        if i >= 2:
            value = value + hr[i - 2].astype(F32)
        if i < 6:
            value = value + hl[i].astype(F32)
        o_sens[pl.ds(i, V, stride=COLS), :] = (value * ocean_count)[0:V]

    stage_wait(9, 8, lg_u)
    for r in range(8):
        flat[48 * r : 48 * r + 48, :] = lg_u[(r % 2) * 4 + r // 2].astype(F32)
    for l in range(7):
        width = min(128, FF - 128 * l)
        o_up[:, 128 * l : 128 * l + width] = flat[50 * l : 50 * l + 50, 0:width]
    stage_wait(10, 8, sfin)
    for h, rows in ((0, 32), (1, 18)):
        tiny = sfin[4 * h].astype(F32)
        for j in range(1, 4):
            tiny = tiny + sfin[4 * h + j].astype(F32)
        o_stem[32 * h : 32 * h + rows, :] = tiny[0:rows, 0:V]
        o_kern[32 * h : 32 * h + rows, :] = pltpu.roll(tiny, LAT - V, 1)[0:rows, 0:49]
    for copy in first_weights + halo + [large_weights[a][i] for a in (0, 1) for i in (1, 2)]:
        copy.wait_send()

    @pl.when(alone)
    def _():
        large_weights[0][0].wait_send()
        large_weights[1][0].wait_send()

    @pl.when(helper)
    def _():
        help_copies[0].wait_send()
        help_copies[1].wait_send()

    for copy in [copy_d, copy_u, copy_l, copy_r] + pending:
        copy.wait_send()


def hand_over(*refs):
    copies = [pltpu.make_async_copy(refs[n], refs[7 + n], refs[14].at[n]) for n in range(7)]
    for n in (6, 2, 3, 0, 1, 4, 5):
        copies[n].start()
    for copy in copies:
        copy.wait()


SCRATCH = [
    ((V, COLS, LAT), BF16),
    ((V, COLS, LAT), BF16),
    ((COLS, LAT), jnp.int32),
    ((1, V), jnp.int32),
    ((50, V), BF16),
    ((50, SIDE * SIDE), BF16),
    ((50, FF), BF16),
    ((C, C), BF16),
    ((50, V), BF16),
    ((VP * COLS, LAT), F32),
    ((VP * COLS, LAT), F32),
    ((SLOTS, VP, LAT), BF16),
    ((VP, SLOTS * LAT), BF16),
    ((64, 256 + FP + 128), F32),
    ((208, CP), F32),
    ((4, 64, 128), BF16),
    ((4, 64, FP + 128), BF16),
    ((4, 208, CP), BF16),
    ((CP, 128), BF16),
    ((128, CP), BF16),
    ((CP, FP), BF16),
    ((FP, CP), BF16),
    ((CP, 128), F32),
    ((CP, 128), BF16),
    ((128, CP), BF16),
    ((FF, CP), BF16),
    ((CP, FF), BF16),
    ((FF, CP), F32),
    ((SIDE * SIDE, C, LAT), F32),
    ((SIDE * COLS, C, LAT), F32),
    ((SIDE * SIDE, C, LAT), F32),
    ((SLOTS, C, LAT), F32),
    ((COLS, C, LAT), F32),
    ((CP, CELLS), BF16),
    ((FF, CELLS), BF16),
    ((FF, CELLS), F32),
    ((FP, CELLS), BF16),
    ((CP, CELLS), BF16),
    ((VP, CELLS), BF16),
    ((1, LAT), F32),
    ((128, LAT), F32),
    ((32, 1, LAT), F32),
    ((8, 1, LAT), F32),
    ((C, CELLS), F32),
    ((CP, CELLS), BF16),
    ((4 * CP, 128), F32),
    ((7, CR, 128), F32),
    ((4 * 384, 128), F32),
    ((SLOTS, C, LAT), F32),
    ((CP, SLOTS * LAT), BF16),
    ((CP, 128), F32),
    ((CP, 128), BF16),
    ((32, 32, 128), BF16),
    ((32, 48, 128), BF16),
    ((16, 32, 128), BF16),
    ((16, 48, 128), BF16),
    ((16, 32, 128), BF16),
    ((16, 48, 128), BF16),
    ((16, 32, 128), BF16),
    ((16, 48, 128), BF16),
    ((8, 48, 128), BF16),
    ((8, 48, 128), BF16),
    ((8, 32, 128), BF16),
    ((8, 32, 128), BF16),
    ((8, 32, 128), BF16),
    ((8, 32, 128), BF16),
    ((8, 32, 128), BF16),
    ((8, 32, 128), BF16),
    ((12, VP, LAT), BF16),
    ((6, VP, LAT), BF16),
    ((6, VP, LAT), BF16),
    ((COLS, VP, LAT), F32),
]


def shards(
    fields, targets, land_sea, clip_level, stem_weight, dw_kernel, up_weight, down_weight, head_weight
):
    anywhere = pl.BlockSpec(memory_space=pl.ANY)
    vmem = pl.BlockSpec(memory_space=pltpu.VMEM)
    dma = pltpu.SemaphoreType.DMA
    shapes = [(50, V), (50, 49), (50, FF), (C, C), (50, V), (1, 1), (V * COLS, LAT)]
    results = [jax.ShapeDtypeStruct(s, F32) for s in shapes]
    made = pl.pallas_call(
        body,
        out_shape=[pltpu.VMEM(s, F32) for s in shapes],
        in_specs=[anywhere] * 9,
        out_specs=[vmem] * 7,
        scratch_shapes=[pltpu.VMEM(s, t) for s, t in SCRATCH]
        + [dma((n,)) for n in (11, 9, 4, 4, 13, 13, 9)],
        compiler_params=pltpu.CompilerParams(
            collective_id=0, has_side_effects=True, vmem_limit_bytes=58 * 1024 * 1024
        ),
    )(
        fields.reshape(V, COLS, LAT),
        targets.reshape(V, COLS, LAT),
        land_sea,
        clip_level.reshape(1, V),
        stem_weight,
        dw_kernel,
        up_weight,
        down_weight,
        head_weight,
    )
    outs = pl.pallas_call(
        hand_over,
        out_shape=results,
        in_specs=[vmem] * 7,
        out_specs=[anywhere] * 7,
        scratch_shapes=[dma((7,))],
    )(*[pltpu.with_memory_space_constraint(m, pltpu.VMEM) for m in made])
    return (
        outs[0], outs[1], outs[2], outs[3], outs[4],
        outs[5].reshape(()),
        outs[6].reshape(1, V, COLS, LAT),
    )


def solution(mesh):
    placed = (
        P("dp", None, "lon", None),
        P("dp", None, "lon", None),
        P("lon", None),
        P(),
        P("dp", None),
        P("dp", None),
        P("dp", None),
        P("dp", None),
        P("dp", None),
    )
    return jax.shard_map(
        shards,
        mesh=mesh,
        in_specs=placed,
        out_specs=(
            P("dp", None),
            P("dp", None),
            P("dp", None),
            P("dp", None),
            P("dp", None),
            P(),
            P("dp", None, "lon", None),
        ),
        check_vma=False,
    )
```

```python
import itertools

import jax
import jax.numpy as jnp
from jax import lax
from jax.experimental import pallas as pl
from jax.experimental.pallas import tpu as pltpu
from jax.sharding import PartitionSpec as P

MESH = pl.DeviceIdType.MESH
F32 = jnp.float32
BF16 = jnp.bfloat16

V = 77
VP = 80
C = 200
CP = 256
CR = 208
FF = 800
FP = 896
FB = 400
COLS = 8
LAT = 128
SIDE = 7
HALO = 6
SLOTS = COLS + 2 * HALO
CELLS = COLS * LAT
GELU_K = 0.7978845608


def dot(a, b):
    return jnp.dot(a, b, preferred_element_type=F32)


def dot_nt(a, b):
    return lax.dot_general(a, b, (((1,), (1,)), ((), ())), preferred_element_type=F32)


def remote(src, dst, send, recv, device):
    return pltpu.make_async_remote_copy(
        src_ref=src,
        dst_ref=dst,
        send_sem=send,
        recv_sem=recv,
        device_id=device,
        device_id_type=MESH,
    )


def hops(offset):
    a, b, c, d, e = offset
    x = {(0, 0): 0, (0, 1): 1, (1, 0): 2, (1, 1): 1}[a, d]
    return x + min(b, 4 - b) + min(c, 8 - c) + 0.5 * e


def group(*sizes):
    offsets = itertools.product(*(range(n) for n in sizes))
    return sorted((o for o in offsets if any(o)), key=lambda o: -hops(o))


def padded_row(channel):
    step = (channel >= 50).astype(jnp.int32)
    step += (channel >= 100).astype(jnp.int32)
    step += (channel >= 150).astype(jnp.int32)
    return channel + 14 * step


def body(*refs):
    inputs, made, rest = refs[:9], refs[9:16], refs[16:]
    held = rest[:9]
    o_stem, o_kern, o_up, o_down, o_head, o_loss, o_sens = made
    fields, targets, land, clip, stem, dw, up, down, head = held
    (
    f32a, f32b, fbuf, fm, wp, wd, ga, gb, gd,
        stem_w, stem_t, up_w, up_t, head_w, head_s, head_t, down_w, down_t, down_f,
        taps, partial, corrs, xs, ms, nh, act, slope, pre, bo, mis, limits, sq, sa, sb,
        bg, bh, gdn, gup, flat, back, sh, small, dsum,
        ld, lu, rd0, ru0, ls_d, ls_u, rx_d, rx_u, part_u, lg_u, part_d, lg_d,
        stx, srx, s2x, sfin, sen, hl, hr, cells,
        send_g, recv_g, send_h, recv_h, send_s, recv_s, load_sem,
    ) = rest[9:]
    lon = lax.axis_index("lon")
    dp = lax.axis_index("dp")
    x_hi, y, z = lon // 32, (lon // 8) % 4, lon % 8
    x_lo, core = dp // 2, dp % 2
    right = ((lon + 1) % 64, dp)
    left = ((lon + 63) % 64, dp)
    sibling = (lon, x_lo * 2 + (1 - core))
    idx_p = (x_hi * 4 + y) * 4 + dp
    idx_m = (x_lo * 4 + y) * 2 + x_hi
    idx_h = x_hi * 4 + y
    idx_e = x_hi * 4 + dp

    ends = ((y == 3) & (z == 7)) | ((y == 0) & (z == 0))

    def peer(offset):
        a, b, c, d, e = offset
        return (x_hi + a) % 2, (y + b) % 4, (z + c) % 8, (x_lo + d) % 2, (core + e) % 2

    def device(at):
        return at[0] * 32 + at[1] * 8 + at[2], at[3] * 2 + at[4]

    PLANE = group(2, 4, 1, 2, 2), lambda at: (at[0] * 4 + at[1]) * 4 + at[3] * 2 + at[4]
    RING = group(1, 1, 8, 1, 1), lambda at: at[2]
    CORES = group(2, 4, 1, 2, 1), lambda at: (at[3] * 4 + at[1]) * 2 + at[0]
    SHARE = group(2, 4, 1, 1, 1), lambda at: at[0] * 4 + at[1]
    ROW = group(2, 1, 1, 2, 2), lambda at: at[0] * 4 + at[3] * 2 + at[4]

    loads = [
        pltpu.make_async_copy(src, dst, load_sem.at[n])
        for n, (src, dst) in enumerate(zip(inputs, held))
    ]
    for copy in loads:
        copy.start()
    barrier = pltpu.get_barrier_semaphore()
    for offset in RING[0]:
        pl.semaphore_signal(
            barrier, inc=1, device_id=device(peer(offset)), device_id_type=MESH
        )
    for target in (right, left):
        pl.semaphore_signal(barrier, inc=1, device_id=target, device_id_type=MESH)
    for offset in PLANE[0]:
        pl.semaphore_signal(
            barrier, inc=1, device_id=device(peer(offset)), device_id_type=MESH
        )

    for copy in loads:
        copy.wait()
    f32a[0 : V * COLS, :] = fields[...].astype(F32).reshape(V * COLS, LAT)
    f32a[V * COLS : VP * COLS, :] = jnp.zeros(((VP - V) * COLS, LAT), F32)
    f32b[0 : V * COLS, :] = targets[...].astype(F32).reshape(V * COLS, LAT)
    f32b[V * COLS : VP * COLS, :] = jnp.zeros(((VP - V) * COLS, LAT), F32)
    for i in range(COLS):
        fbuf[HALO + i] = f32a[pl.ds(i, VP, stride=COLS), :].astype(BF16)
    wp[...] = jnp.zeros(wp.shape, F32)
    wp[0:50, 0:V] = stem[...].astype(F32)
    wp[0:50, 128:177] = dw[...].astype(F32)
    wp[0:50, 256 : 256 + FF] = up[...].astype(F32)
    wp[0:50, 256 + FP : 256 + FP + V] = head[...].astype(F32)
    wd[...] = jnp.zeros(wd.shape, F32)
    wd[0:C, 0:C] = down[...].astype(F32)
    ga[dp] = (wp[:, 0:128] + pltpu.roll(wp[:, 128:256], V, 1)).astype(BF16)
    gb[dp] = wp[:, 256 : 256 + FP + 128].astype(BF16)
    gd[dp] = wd[...].astype(BF16)

    pl.semaphore_wait(barrier, 40)

    halo = [
        remote(fbuf.at[pl.ds(8, 6)], fbuf.at[pl.ds(0, 6)], send_h.at[0], recv_h.at[0], right),
        remote(fbuf.at[pl.ds(6, 6)], fbuf.at[pl.ds(14, 6)], send_h.at[1], recv_h.at[1], left),
    ]
    first_weights = [
        remote(ga.at[dp], ga.at[dp], send_g.at[k - 1], recv_g.at[k - 1], (lon, (dp + k) % 4))
        for k in range(1, 4)
    ]
    for copy in first_weights:
        copy.start()
    across = (lon, (1 - x_lo) * 2 + core)
    far = (1 - x_lo) * 2 + core
    large_weights = []
    for a, buf in enumerate((gb, gd)):
        at = 3 + 3 * a
        large_weights.append(
            (
                remote(buf.at[dp], buf.at[dp], send_g.at[at], recv_g.at[at], across),
                remote(buf.at[dp], buf.at[dp], send_g.at[at + 1], recv_g.at[at + 1], sibling),
                remote(buf.at[far], buf.at[far], send_g.at[at + 2], recv_g.at[at + 2], sibling),
            )
        )

    for copy in halo:
        copy.start()
    large_weights[0][0].start()

    def pass_on(a):
        large_weights[a][0].wait_recv()
        large_weights[a][2].start()

    pending = []

    def stage(index, count, peers, src, dst):
        for offset in peers[0][: count - 1]:
            at = peer(offset)
            remote(
                src(peers[1](at)), dst, send_s.at[index], recv_s.at[index], device(at)
            ).start()

    def stage_wait(index, count, buf):
        whole = buf.at[pl.ds(0, count - 1)]
        both = remote(whole, whole, send_s.at[index], recv_s.at[index], right)
        both.wait_recv()
        pending.append(both)

    row = lax.broadcasted_iota(jnp.int32, (CP, CP), 0)
    col = lax.broadcasted_iota(jnp.int32, (CP, CP), 1)
    from_padded = jnp.where((row < C) & (col == padded_row(row)), 1.0, 0.0).astype(BF16)
    to_padded = jnp.where((col < C) & (row == padded_row(col)), 1.0, 0.0).astype(BF16)
    lane = lax.broadcasted_iota(jnp.int32, (8, LAT), 1)
    keep = {b: (lane + b >= 0) & (lane + b < LAT) for b in range(-HALO, HALO + 1, 2)}

    for i in range(COLS):
        fm[:, (HALO + i) * LAT : (HALO + i + 1) * LAT] = fbuf[HALO + i]

    for copy in first_weights:
        copy.wait_recv()
    large_weights[0][1].start()
    stem_w[...] = dot(from_padded, ga[...].reshape(CP, 128)).astype(BF16)
    def stem_pair(s):
        out = dot(stem_w[0:CR, 0:VP], fm[:, s * LAT : (s + 2) * LAT])[0:C].astype(BF16).astype(F32)
        xs[s] = out[:, 0:LAT]
        xs[s + 1] = out[:, LAT : 2 * LAT]

    for s in range(HALO, HALO + COLS, 2):
        stem_pair(s)
    kern_w = stem_w[0:CR, :]
    tap_row = lax.broadcasted_iota(jnp.int32, (LAT, 2 * LAT), 0)
    second_half = (lax.broadcasted_iota(jnp.int32, (LAT, 2 * LAT), 1) >= LAT).astype(jnp.int32)
    for t in range(0, SIDE * SIDE, 2):
        spread = dot(kern_w, jnp.where(tap_row == V + t + second_half, 1.0, 0.0).astype(BF16))[0:C]
        taps[t] = spread[:, 0:LAT]
        if t + 1 < SIDE * SIDE:
            taps[t + 1] = spread[:, LAT : 2 * LAT]
    def several(step):
        def steps(group, carry):
            for n in range(5):
                step(group * 5 + n, carry)
            return carry

        return steps

    def own_taps(i):
        return [p for p in range(SIDE) if HALO <= i + 2 * p < HALO + COLS]

    def conv_own(block, carry):
        here = pl.ds(pl.multiple_of(block * 8, 8), 8)
        x = {s: xs[s, here, :] for s in range(HALO, HALO + COLS)}
        for q in range(SIDE):
            w = [taps[p * SIDE + q, here, :] for p in range(SIDE)]
            for i in range(COLS):
                total = None
                for p in own_taps(i):
                    term = w[p] * x[i + 2 * p]
                    total = term if total is None else total + term
                partial[q * COLS + i, here, :] = total
        return carry

    large_weights[1][0].start()
    large_weights[1][1].start()
    lax.fori_loop(0, 5, several(conv_own), 0)
    for copy in halo:
        copy.wait_recv()
    for s in list(range(0, HALO)) + list(range(HALO + COLS, SLOTS)):
        fm[:, s * LAT : (s + 1) * LAT] = fbuf[s]
    for s in list(range(0, HALO, 2)) + list(range(HALO + COLS, SLOTS, 2)):
        stem_pair(s)

    def conv_forward(block, carry):
        here = pl.ds(pl.multiple_of(block * 8, 8), 8)
        x = {s: xs[s, here, :] for s in range(SLOTS) if not HALO <= s < HALO + COLS}
        out = [None] * COLS
        for q in range(SIDE):
            b = (q - 3) * 2
            w = [taps[p * SIDE + q, here, :] for p in range(SIDE)]
            for i in range(COLS):
                total = partial[q * COLS + i, here, :]
                for p in range(SIDE):
                    if p not in own_taps(i):
                        total = total + w[p] * x[i + 2 * p]
                if b != 0:
                    total = jnp.where(keep[b], pltpu.roll(total, (-b) % LAT, 1), 0.0)
                out[i] = total if out[i] is None else out[i] + total
        for i in range(COLS):
            ms[i, here, :] = out[i]
        return carry

    pl.when(ends)(lambda: pass_on(0))
    lax.fori_loop(0, 3, several(conv_forward), 0)
    pl.when(jnp.logical_not(ends))(lambda: pass_on(0))
    lax.fori_loop(3, 5, several(conv_forward), 0)

    nh[...] = jnp.zeros(nh.shape, BF16)
    rstds = []
    for i in range(COLS):
        tile = ms[i]
        centred = tile - jnp.mean(tile, axis=0, keepdims=True)
        rstd = lax.rsqrt(jnp.mean(centred * centred, axis=0, keepdims=True) + 1e-06)
        normed = centred * rstd
        ms[i] = normed
        rstds.append(rstd)
        nh[0:C, i * LAT : (i + 1) * LAT] = normed.astype(BF16)

    large_weights[0][1].wait_recv()
    large_weights[0][2].wait_recv()
    second = dot(from_padded, gb[...].reshape(CP, FP + 128))
    up_w[...] = second[:, 0:FP].astype(BF16)
    up_t[...] = second[:, 0:FP].T.astype(BF16)
    head_w[...] = second[:, FP : FP + 128]
    head_t[...] = second[:, FP : FP + 128].T.astype(BF16)
    pass_on(1)
    limits[...] = jnp.ones((1, LAT), F32)
    limits[:, 0:V] = clip[...].astype(F32) / 16.0
    sq[...] = jnp.zeros(sq.shape, F32)
    bo[...] = jnp.zeros(bo.shape, BF16)
    for j in range(COLS // 2):
        part = pl.ds(j * 2 * LAT, 2 * LAT)
        for f in range(0, FF, FB):
            u = dot(up_t[f : f + FB, :], nh[:, part])
            u2 = u * u
            half = 0.5 + 0.5 * jnp.tanh(u * (GELU_K + (GELU_K * 0.044715) * u2))
            value = u * half
            act[f : f + FB, part] = value.astype(BF16)
            slope[f : f + FB, part] = half + value * (1.0 - half) * (
                2.0 * GELU_K + (6.0 * GELU_K * 0.044715) * u2
            )
    large_weights[1][1].wait_recv()
    large_weights[1][2].wait_recv()
    for d in range(4):
        down_f[C * d : C * (d + 1), :] = gd[d].astype(F32)[0:C]
    down_w[...] = down_f[...].astype(BF16)
    down_t[...] = down_f[...].T.astype(BF16)

    for j in range(COLS // 2):
        part = pl.ds(j * 2 * LAT, 2 * LAT)
        branch = dot(down_t[0:CR, :], act[:, part])[0:C]
        centre = jnp.concatenate([xs[HALO + 2 * j], xs[HALO + 2 * j + 1]], axis=1)
        bo[0:C, part] = (centre + branch).astype(BF16)
    for j in range(COLS // 2):
        part = pl.ds(j * 2 * LAT, 2 * LAT)
        predicted = dot(head_t[0:VP, :], bo[:, part])
        for h in range(2):
            i = 2 * j + h
            ocean = land[i : i + 1, :].astype(F32)
            wanted = f32b[pl.ds(i, VP, stride=COLS), :]
            miss = (predicted[:, h * LAT : (h + 1) * LAT] - wanted) * ocean
            mis[:, i * LAT : (i + 1) * LAT] = miss.astype(BF16)
            sq[0:VP, :] = sq[0:VP, :] + miss * miss

    lanes = lax.broadcasted_iota(jnp.int32, (1, LAT), 1)
    ocean_local = jnp.sum(land[...].astype(F32))
    mine = jnp.sum(sq[...].T, axis=0, keepdims=True)
    sa[idx_p] = jnp.where(lanes == V, ocean_local, mine)
    stage(0, 32, PLANE, lambda j: sa.at[idx_p], sa.at[idx_p])

    gdn[...] = jnp.zeros(gdn.shape, F32)
    own_down = dot_nt(act[...], mis[...])
    for d in range(4):
        gdn[CP * d : CP * d + C, 0:VP] = own_down[C * d : C * d + C]
    own_head = dot_nt(bo[...], mis[...]).astype(BF16)
    own_head = dot(to_padded, own_head)
    for d in range(4):
        gdn[CP * d + C : CP * d + C + 56, 0:VP] = own_head[64 * d : 64 * d + 56]
    for d in range(4):
        for r in range(8):
            piece = (d % 2) * 16 + (d // 2) * 8 + r
            ld[piece] = gdn[CP * d + 32 * r : CP * d + 32 * r + 32, :].astype(BF16)
    away = pl.ds((1 - core) * 16, 16)
    copy_d = remote(ld.at[away], rd0, send_s.at[2], recv_s.at[2], sibling)
    copy_d.start()
    flat[...] = jnp.zeros(flat.shape, F32)
    bh[CR:CP, :] = jnp.zeros((CP - CR, CELLS), BF16)
    stem_t[...] = stem_w[...].astype(F32).T.astype(BF16)

    stage_wait(0, 32, sa)
    total = sa[0]
    for j in range(1, 32):
        total = total + sa[j]
    sb[z] = total
    stage(1, 8, RING, lambda j: sb.at[z], sb.at[z])
    copy_d.wait_recv()
    for j in range(16):
        ls_d[j] = (ld[core * 16 + j].astype(F32) + rd0[j].astype(F32)).astype(BF16)
    stage(4, 16, CORES, lambda j: ls_d.at[j], rx_d.at[idx_m])
    stage_wait(1, 8, sb)
    total = sb[0]
    for j in range(1, 8):
        total = total + sb[j]
    ocean_count = jnp.sum(jnp.where(lanes == V, total, 0.0), axis=1, keepdims=True)
    valid = lanes < V
    threshold = limits[...]
    mean_error = jnp.where(valid, total, 0.0) / ocean_count
    ratio = 1.0 + mean_error / threshold
    o_loss[...] = jnp.sum(jnp.where(valid, threshold * jnp.log(ratio), 0.0), axis=1, keepdims=True)
    factor = jnp.where(valid, 2.0 / (ocean_count * ratio), 0.0)

    head_s[...] = (head_w[...] * factor).astype(BF16)
    scaled = head_s[...]
    for j in range(COLS // 2):
        part = pl.ds(j * 2 * LAT, 2 * LAT)
        grad = dot(scaled[0:CR, 0:VP], mis[:, part])
        bg[:, part] = grad[0:C]
        bh[0:CR, part] = grad.astype(BF16)
    pre[FF:FP, :] = jnp.zeros((FP - FF, CELLS), BF16)
    for j in range(COLS // 2):
        part = pl.ds(j * 2 * LAT, 2 * LAT)
        for f in range(0, FF, 160):
            pre[f : f + 160, part] = (
                dot(down_w[f : f + 160, :], bh[:, part]) * slope[f : f + 160, part]
            ).astype(BF16)
    up_grad = dot_nt(nh[0:CR, :], pre[...])
    for l in range(7):
        gup[l] = up_grad[:, 128 * l : 128 * l + 128]
    for d in range(4):
        for l in range(7):
            at = 384 * d + 50 * l
            flat[at : at + 50, :] = gup[l, 50 * d : 50 * d + 50, :]
    for d in range(4):
        for r in range(8):
            piece = (d % 2) * 16 + (d // 2) * 8 + r
            lu[piece] = flat[384 * d + 48 * r : 384 * d + 48 * r + 48, :].astype(BF16)
    copy_u = remote(lu.at[away], ru0, send_s.at[3], recv_s.at[3], sibling)
    copy_u.start()

    for j in range(COLS // 2):
        part = pl.ds(j * 2 * LAT, 2 * LAT)
        grad = dot(up_w[0:CR, :], pre[:, part])[0:C]
        for h in range(2):
            i = 2 * j + h
            g = grad[:, h * LAT : (h + 1) * LAT]
            normed = ms[i]
            mean_g = jnp.mean(g, axis=0, keepdims=True)
            mean_gn = jnp.mean(g * normed, axis=0, keepdims=True)
            ms[i] = (rstds[i] * (g - mean_g - normed * mean_gn)).astype(BF16).astype(F32)

    stage_wait(4, 16, rx_d)
    rx_d[idx_m] = ls_d[idx_m]
    large = rx_d[0].astype(F32)
    for j in range(1, 16):
        large = large + rx_d[j].astype(F32)
    part_d[z] = large.astype(BF16)
    stage(7, 8, RING, lambda j: part_d.at[z], part_d.at[z])

    def conv_backward(block, carry):
        here = pl.ds(pl.multiple_of(block * 8, 8), 8)
        x = [xs[s, here, :] for s in range(SLOTS)]
        m = [ms[i, here, :] for i in range(COLS)]
        out = [None] * SLOTS
        for q in range(SIDE):
            b = (q - 3) * 2
            if b != 0:
                shifted = [jnp.where(keep[-b], pltpu.roll(t, b % LAT, 1), 0.0) for t in m]
            else:
                shifted = m
            for p in range(SIDE):
                t = p * SIDE + q
                w = taps[t, here, :]
                corr = None
                for i in range(COLS):
                    s = i + 2 * p
                    term = w * shifted[i]
                    out[s] = term if out[s] is None else out[s] + term
                    prod = shifted[i] * x[s]
                    corr = prod if corr is None else corr + prod
                corrs[t, here, :] = corr
        for s in range(SLOTS):
            back[s, here, :] = out[s]
        return carry

    lax.fori_loop(0, 1, several(conv_backward), 0)
    copy_u.wait_recv()
    for j in range(16):
        ls_u[j] = (lu[core * 16 + j].astype(F32) + ru0[j].astype(F32)).astype(BF16)
    stage(11, 16, CORES, lambda j: ls_u.at[j], rx_u.at[idx_m])
    lax.fori_loop(1, 5, several(conv_backward), 0)

    stage_wait(7, 8, part_d)
    large = part_d[0].astype(F32)
    for j in range(1, 8):
        large = large + part_d[j].astype(F32)
    lg_d[idx_h] = large.astype(BF16)
    stage(12, 8, SHARE, lambda j: lg_d.at[idx_h], lg_d.at[idx_h])
    stage_wait(11, 16, rx_u)
    rx_u[idx_m] = ls_u[idx_m]
    large = rx_u[0].astype(F32)
    for j in range(1, 16):
        large = large + rx_u[j].astype(F32)
    part_u[z] = large.astype(BF16)
    stage(5, 8, RING, lambda j: part_u.at[z], part_u.at[z])

    tap_col = lax.broadcasted_iota(jnp.int32, (2 * LAT, LAT), 1)
    lower_half = (lax.broadcasted_iota(jnp.int32, (2 * LAT, LAT), 0) >= LAT).astype(jnp.int32)
    kern = None
    for t in range(0, SIDE * SIDE, 2):
        place = jnp.where(tap_col == V + t + lower_half, 1.0, 0.0).astype(BF16)
        terms = corrs[t].astype(BF16)
        if t + 1 < SIDE * SIDE:
            terms = jnp.concatenate([terms, corrs[t + 1].astype(BF16)], axis=1)
        else:
            place = place[0:LAT]
        part_sum = dot(terms, place)
        kern = part_sum if kern is None else kern + part_sum

    sh[C:CP, :] = jnp.zeros((CP - C, SLOTS * LAT), BF16)
    for s in range(SLOTS):
        value = back[s]
        if HALO <= s < HALO + COLS:
            value = value + bg[:, (s - HALO) * LAT : (s - HALO + 1) * LAT]
        sh[0:C, s * LAT : (s + 1) * LAT] = value.astype(BF16)
    small[...] = jnp.zeros(small.shape, F32)
    small[0:CR, 0:VP] = dot_nt(sh[0:CR, :], fm[...])
    small[0:C, :] = small[0:C, :] + kern
    for j in range(8):
        at = 50 * (j % 4) + 32 * (j // 4)
        stx[j] = small[at : at + 32, :].astype(BF16)
    stage(6, 8, ROW, lambda j: stx.at[j], srx.at[idx_e])

    for s in list(range(0, HALO, 2)) + list(range(HALO + COLS, SLOTS, 2)):
        value = dot(stem_t[0:VP, :], sh[:, s * LAT : (s + 2) * LAT]).astype(BF16)
        sen[s if s < HALO else s - COLS] = value[:, 0:LAT]
        sen[s + 1 if s < HALO else s + 1 - COLS] = value[:, LAT : 2 * LAT]
    copy_l = remote(sen.at[pl.ds(0, 6)], hr, send_h.at[2], recv_h.at[2], left)
    copy_r = remote(sen.at[pl.ds(6, 6)], hl, send_h.at[3], recv_h.at[3], right)
    copy_l.start()
    copy_r.start()

    for j in range(COLS // 2):
        s = HALO + 2 * j
        value = dot(stem_t[0:VP, :], sh[:, s * LAT : (s + 2) * LAT])
        cells[2 * j] = value[:, 0:LAT]
        cells[2 * j + 1] = value[:, LAT : 2 * LAT]

    stage_wait(6, 8, srx)
    srx[idx_e] = stx[idx_e]
    tiny = srx[0].astype(F32)
    for j in range(1, 8):
        tiny = tiny + srx[j].astype(F32)
    s2x[z] = tiny.astype(BF16)
    stage(8, 8, RING, lambda j: s2x.at[z], s2x.at[z])

    stage_wait(5, 8, part_u)
    large = part_u[0].astype(F32)
    for j in range(1, 8):
        large = large + part_u[j].astype(F32)
    lg_u[idx_h] = large.astype(BF16)
    stage(9, 8, SHARE, lambda j: lg_u.at[idx_h], lg_u.at[idx_h])

    stage_wait(12, 8, lg_d)
    for r in range(8):
        dsum[32 * r : 32 * r + 32, :] = lg_d[(r % 2) * 4 + r // 2]
    o_down[...] = dot_nt(dsum[...], head_s[...])[0:C, 0:C]
    o_head[...] = (dsum[...].astype(F32)[C : C + 50] * factor)[:, 0:V]

    stage_wait(8, 8, s2x)
    tiny = s2x[0].astype(F32)
    for j in range(1, 8):
        tiny = tiny + s2x[j].astype(F32)
    sfin[idx_h] = tiny.astype(BF16)
    stage(10, 8, SHARE, lambda j: sfin.at[idx_h], sfin.at[idx_h])

    copy_l.wait_recv()
    copy_r.wait_recv()
    for i in range(COLS):
        value = cells[i]
        if i >= 2:
            value = value + hr[i - 2].astype(F32)
        if i < 6:
            value = value + hl[i].astype(F32)
        o_sens[pl.ds(i, V, stride=COLS), :] = (value * ocean_count)[0:V]

    stage_wait(9, 8, lg_u)
    for r in range(8):
        flat[48 * r : 48 * r + 48, :] = lg_u[(r % 2) * 4 + r // 2].astype(F32)
    for l in range(7):
        width = min(128, FF - 128 * l)
        o_up[:, 128 * l : 128 * l + width] = flat[50 * l : 50 * l + 50, 0:width]
    stage_wait(10, 8, sfin)
    for h, rows in ((0, 32), (1, 18)):
        tiny = sfin[4 * h].astype(F32)
        for j in range(1, 4):
            tiny = tiny + sfin[4 * h + j].astype(F32)
        o_stem[32 * h : 32 * h + rows, :] = tiny[0:rows, 0:V]
        o_kern[32 * h : 32 * h + rows, :] = pltpu.roll(tiny, LAT - V, 1)[0:rows, 0:49]
    for copy in first_weights + halo + list(large_weights[0] + large_weights[1]):
        copy.wait_send()
    for copy in [copy_d, copy_u, copy_l, copy_r] + pending:
        copy.wait_send()


def hand_over(*refs):
    copies = [pltpu.make_async_copy(refs[n], refs[7 + n], refs[14].at[n]) for n in range(7)]
    for n in (6, 2, 3, 0, 1, 4, 5):
        copies[n].start()
    for copy in copies:
        copy.wait()


SCRATCH = [
    ((V, COLS, LAT), BF16),
    ((V, COLS, LAT), BF16),
    ((COLS, LAT), jnp.int32),
    ((1, V), jnp.int32),
    ((50, V), BF16),
    ((50, SIDE * SIDE), BF16),
    ((50, FF), BF16),
    ((C, C), BF16),
    ((50, V), BF16),
    ((VP * COLS, LAT), F32),
    ((VP * COLS, LAT), F32),
    ((SLOTS, VP, LAT), BF16),
    ((VP, SLOTS * LAT), BF16),
    ((64, 256 + FP + 128), F32),
    ((208, CP), F32),
    ((4, 64, 128), BF16),
    ((4, 64, FP + 128), BF16),
    ((4, 208, CP), BF16),
    ((CP, 128), BF16),
    ((128, CP), BF16),
    ((CP, FP), BF16),
    ((FP, CP), BF16),
    ((CP, 128), F32),
    ((CP, 128), BF16),
    ((128, CP), BF16),
    ((FF, CP), BF16),
    ((CP, FF), BF16),
    ((FF, CP), F32),
    ((SIDE * SIDE, C, LAT), F32),
    ((SIDE * COLS, C, LAT), F32),
    ((SIDE * SIDE, C, LAT), F32),
    ((SLOTS, C, LAT), F32),
    ((COLS, C, LAT), F32),
    ((CP, CELLS), BF16),
    ((FF, CELLS), BF16),
    ((FF, CELLS), F32),
    ((FP, CELLS), BF16),
    ((CP, CELLS), BF16),
    ((VP, CELLS), BF16),
    ((1, LAT), F32),
    ((128, LAT), F32),
    ((32, 1, LAT), F32),
    ((8, 1, LAT), F32),
    ((C, CELLS), F32),
    ((CP, CELLS), BF16),
    ((4 * CP, 128), F32),
    ((7, CR, 128), F32),
    ((4 * 384, 128), F32),
    ((SLOTS, C, LAT), F32),
    ((CP, SLOTS * LAT), BF16),
    ((CP, 128), F32),
    ((CP, 128), BF16),
    ((32, 32, 128), BF16),
    ((32, 48, 128), BF16),
    ((16, 32, 128), BF16),
    ((16, 48, 128), BF16),
    ((16, 32, 128), BF16),
    ((16, 48, 128), BF16),
    ((16, 32, 128), BF16),
    ((16, 48, 128), BF16),
    ((8, 48, 128), BF16),
    ((8, 48, 128), BF16),
    ((8, 32, 128), BF16),
    ((8, 32, 128), BF16),
    ((8, 32, 128), BF16),
    ((8, 32, 128), BF16),
    ((8, 32, 128), BF16),
    ((8, 32, 128), BF16),
    ((12, VP, LAT), BF16),
    ((6, VP, LAT), BF16),
    ((6, VP, LAT), BF16),
    ((COLS, VP, LAT), F32),
]


def shards(
    fields, targets, land_sea, clip_level, stem_weight, dw_kernel, up_weight, down_weight, head_weight
):
    anywhere = pl.BlockSpec(memory_space=pl.ANY)
    vmem = pl.BlockSpec(memory_space=pltpu.VMEM)
    dma = pltpu.SemaphoreType.DMA
    shapes = [(50, V), (50, 49), (50, FF), (C, C), (50, V), (1, 1), (V * COLS, LAT)]
    results = [jax.ShapeDtypeStruct(s, F32) for s in shapes]
    made = pl.pallas_call(
        body,
        out_shape=[pltpu.VMEM(s, F32) for s in shapes],
        in_specs=[anywhere] * 9,
        out_specs=[vmem] * 7,
        scratch_shapes=[pltpu.VMEM(s, t) for s, t in SCRATCH]
        + [dma((n,)) for n in (9, 9, 4, 4, 13, 13, 9)],
        compiler_params=pltpu.CompilerParams(
            collective_id=0, has_side_effects=True, vmem_limit_bytes=58 * 1024 * 1024
        ),
    )(
        fields.reshape(V, COLS, LAT),
        targets.reshape(V, COLS, LAT),
        land_sea,
        clip_level.reshape(1, V),
        stem_weight,
        dw_kernel,
        up_weight,
        down_weight,
        head_weight,
    )
    outs = pl.pallas_call(
        hand_over,
        out_shape=results,
        in_specs=[vmem] * 7,
        out_specs=[anywhere] * 7,
        scratch_shapes=[dma((7,))],
    )(*[pltpu.with_memory_space_constraint(m, pltpu.VMEM) for m in made])
    return (
        outs[0], outs[1], outs[2], outs[3], outs[4],
        outs[5].reshape(()),
        outs[6].reshape(1, V, COLS, LAT),
    )


def solution(mesh):
    placed = (
        P("dp", None, "lon", None),
        P("dp", None, "lon", None),
        P("lon", None),
        P(),
        P("dp", None),
        P("dp", None),
        P("dp", None),
        P("dp", None),
        P("dp", None),
    )
    return jax.shard_map(
        shards,
        mesh=mesh,
        in_specs=placed,
        out_specs=(
            P("dp", None),
            P("dp", None),
            P("dp", None),
            P("dp", None),
            P("dp", None),
            P(),
            P("dp", None, "lon", None),
        ),
        check_vma=False,
    )
```
